32 devices in a mesh: grp: 8 (over z, x), shard: 4 (over y, core).
Axes of the slice: x: 2, y: 2, z: 4, core: 2. Of those that a mesh axis runs over, the one named last changes fastest.
Arguments:
- tokens: float32 [8192, 1152], P(('grp', 'shard')), may hold values from -6 to 6
- routes: int32 [8192, 1], P(('grp', 'shard')), may hold values from 0 to 1; in each aligned block of 256 rows (0 to 255, 256 to 511, ...) at most 192 rows name the same one
- lengths: int32 [8], P('grp'), may hold values from 512 to 1024, as said below
- cotangent: float32 [8192, 1152], P(('grp', 'shard')), may hold values from -6 to 6
- in_weight: bfloat16 [1152, 4608], P('shard'), may hold values from -0.1875 to 0.1875
- select_weight: bfloat16 [2304, 104], P('shard'), may hold values from -0.125 to 0.125
- step_weight: bfloat16 [72, 2304], P(None, 'shard'), may hold values from -0.75 to 0.75
- out_weight: bfloat16 [2304, 1152], P('shard'), may hold values from -0.125 to 0.125
- router_weight: bfloat16 [1152, 2], P('shard'), may hold values from -0.1875 to 0.1875
- up_weight: bfloat16 [2, 1152, 3072], P(None, 'shard'), may hold values from -0.1875 to 0.1875
- down_weight: bfloat16 [2, 3072, 1152], P(None, 'shard'), may hold values from -0.109375 to 0.109375
- conv_weight: bfloat16 [4, 2304], P(None, 'shard'), may hold values from -3 to 3
- conv_bias: bfloat16 [2304], P('shard'), may hold values from -1.5 to 1.5
- step_bias: bfloat16 [2304], P('shard'), may hold values from -9 to -2
- decay_log: bfloat16 [16, 2304], P(None, 'shard'), may hold values from 0 to 2.765625
- skip_gain: bfloat16 [2304], P('shard'), may hold values from 0.5 to 1.5
- mixer_gain: bfloat16 [1152], P('shard'), may hold values from 0.5 to 1.5
- expert_gain: bfloat16 [1152], P('shard'), may hold values from 0.5 to 1.5
Outputs:
- result: float32 [8192, 1152], P(('grp', 'shard'))
- tokens_grad: float32 [8192, 1152], P(('grp', 'shard'))
- in_grad: float32 [1152, 4608], P('shard', 'grp')
- out_grad: float32 [2304, 1152], P('shard', 'grp')
- up_grad: float32 [2, 1152, 3072], P(None, 'shard', 'grp')
- down_grad: float32 [2, 3072, 1152], P(None, 'shard', 'grp')
- select_grad: float32 [2304, 104], P('shard')
- step_grad: float32 [72, 2304], P(None, 'shard')
- router_grad: float32 [1152, 2], P('shard')
- conv_grad: float32 [4, 2304], P(None, 'shard')
- conv_bias_grad: float32 [2304], P('shard')
- step_bias_grad: float32 [2304], P('shard')
- decay_grad: float32 [16, 2304], P(None, 'shard')
- skip_grad: float32 [2304], P('shard')
- mixer_gain_grad: float32 [1152], P('shard')
- expert_gain_grad: float32 [1152], P('shard')
The draws below stay inside these ranges and needn't reach their ends.
Inputs may be any that keep to these rules, and one draw needn't show every extreme that they name: `lengths`: every sequence holds at least 512 tokens, and one sequence of each draw fills all 1024 slots. `routes`: among the token slots of one device, no expert is named by more than 192 slots.
All inputs are finite; a program needn't handle non-finite values.
Results may differ from the reference program's by a relative error of at most 0.011.
Values may be sent and summed in bfloat16 or wider, within the bound.
No kernel may reach another device: no remote copies, remote signals or barrier semaphores. Data moves between devices by JAX's collectives and lax.ppermute only.
A program may use at most 320 MiB of HBM per device.

```python
import math
import jax
import jax.numpy as jnp
import numpy as np
from jax import lax

D = 1152
DI = 2304
NS = 16
R = 72
FF = 3072
KW = 4
E = 2
BLOCK = 32
TOK_DEV = 256
CAP = 192
SEQ_LEN = 1024
GROUPS = 8
TOKENS = 8192


def draw_lengths(key, part):
    values = jax.random.randint(key, (GROUPS,), SEQ_LEN // 2, SEQ_LEN + 1)
    chosen = jax.random.randint(jax.random.fold_in(key, 7), (), 0, GROUPS)
    return jnp.where(jnp.arange(GROUPS) == chosen, SEQ_LEN, values).astype(jnp.int32)


def raised(values, stream_key, source, target, parts, factor):
    owner, partner = [(jnp.arange(values.shape[position]) // (values.shape[position] // parts)).reshape([-1 if axis == position else 1 for axis in range(values.ndim)]) for position in (source, target)]
    chosen = jax.random.permutation(stream_key, parts)[partner]
    strong = (owner == chosen) | (owner == (partner + parts // 2) % parts)
    return jnp.where(strong, factor * values, values)


def steps_of(own_key, dims, cuts, low, top_value):
    level, own = 1.0, jax.random.fold_in(own_key, 6)
    for axis_at, parts in cuts:
        steps = jnp.exp(jax.random.uniform(jax.random.fold_in(own, axis_at), (parts,), jnp.float32, low / len(cuts), top_value / len(cuts)))
        level = level * jnp.repeat(steps, dims[axis_at] // parts).reshape([-1 if axis == axis_at else 1 for axis in range(len(dims))])
    return level


def deal_out(rng, own, number, rows, count, top, bound, lean):
    ranking = jax.random.permutation(rng, count)
    crowded, ordinary = portions_of(count, rows * top, bound, lean, True), portions_of(count, rows * top, bound, lean, False)
    places = jnp.arange(count)

    def named(sizes, offset_by):
        used = int((sizes > 0).sum())
        fixed = max(1, used // 4)
        moved = fixed + (places - fixed + offset_by * (used - fixed)) % max(1, count - fixed)
        return jnp.zeros((count,), jnp.int32).at[ranking[jnp.where(places < fixed, places, moved)]].set(jnp.asarray(sizes, jnp.int32))

    sizes = jnp.where(number % 4 == 0, named(crowded, number // 4), named(ordinary, number - number // 4 - 1))
    mixed = jax.random.permutation(jax.random.fold_in(own, 3), count)
    source_of, taker = mixed[0:count // 2 * 2:2], mixed[1:count // 2 * 2:2]
    slack = jnp.minimum(sizes[source_of] - 1, bound - sizes[taker]) // 2
    slack = jnp.where((source_of == ranking[0]) | (taker == ranking[0]) | (sizes[taker] == 0), 0, jnp.maximum(slack, 0))
    moved = jax.random.randint(jax.random.fold_in(own, 4), (count // 2,), 0, 1 << 20) % (slack + 1)
    sizes = sizes.at[source_of].add(-moved).at[taker].add(moved)
    members = jnp.searchsorted(jnp.cumsum(sizes), jnp.arange(rows * top), side="right").astype(jnp.int32)
    listing = members.reshape(top, rows).T
    listing = listing[jax.random.permutation(jax.random.fold_in(own, 1), rows)]
    offset_by = jax.random.randint(jax.random.fold_in(own, 2), (rows, 1), 0, top)
    return jnp.take_along_axis(listing, (jnp.arange(top)[None, :] + offset_by) % top, axis=1)


def portions_of(number_of, total, bound, skew, full):
    weights = [(1 << 20) // math.isqrt(rank ** skew) + 1 for rank in range(1, number_of + 1)]
    largest = bound if full else min(bound, max(-(-total // number_of), total * weights[0] // sum(weights)))
    least = 1 if total - largest >= number_of - 1 else 0
    holding, spare = [largest] + [least] * (number_of - 1), total - largest - least * (number_of - 1)
    while spare > 0:
        free = [i for i in range(1, number_of) if holding[i] < largest] or [i for i in range(1, number_of) if holding[i] < bound]
        pool, left = sum([weights[i] for i in free]), spare
        for i in free:
            extra = min(bound - holding[i], max(1, left * weights[i] // pool), spare)
            holding[i] = holding[i] + extra
            spare = spare - extra
    return np.array(holding)


def centred(rng, dims, spread, bound, split=(), kind=jnp.bfloat16):
    result = jax.random.normal(rng, dims, jnp.float32) * spread
    if len(split) > 0:
        result = steps_of(rng, dims, split, -0.22, 0.18) * result
    return jnp.clip(result, min=-bound, max=bound).astype(kind)


def heavy_noise(own_key, shape, deviation, bound, cuts, heavy, held_as=jnp.bfloat16):
    array = deviation * jax.random.normal(own_key, shape, jnp.float32)
    if cuts:
        array = array * steps_of(own_key, shape, cuts, -0.22, 0.18)
    return jnp.clip(raised(array, jax.random.fold_in(own_key, 3), *heavy), -bound, bound).astype(held_as)


def setup_inputs(seed: int = 0) -> dict:
    key_list = jax.random.split(jax.random.key(seed), 19)
    tokens = centred(key_list[0], (TOKENS, D), 1.0, 6.0, ((0, 32),), jnp.float32)
    routes_keys = jax.random.split(jax.random.fold_in(key_list[1], 1), TOKENS // TOK_DEV)
    routes_turns = jax.random.permutation(jax.random.fold_in(key_list[1], 3), TOKENS // TOK_DEV)
    routes = jax.vmap(lambda own, number: deal_out(jax.random.fold_in(key_list[1], 2), own, number, TOK_DEV, E, 1, CAP, 1))(routes_keys, routes_turns).reshape((TOKENS, 1))
    lengths = draw_lengths(jax.random.fold_in(key_list[18], 71), 0)
    cotangent = heavy_noise(key_list[3], (TOKENS, D), 1.0, 6.0, ((0, 32),), (0, 1, 32, 2.75), jnp.float32)
    in_weight = centred(key_list[4], (D, 2 * DI), D ** -0.5, 0.1875, ((0, 4),))
    select_weight = centred(key_list[5], (DI, R + 2 * NS), DI ** -0.5, 0.125, ((0, 4),))
    step_weight = centred(key_list[6], (R, DI), R ** -0.5, 0.75, ((1, 4),))
    out_weight = centred(key_list[7], (DI, D), DI ** -0.5, 0.125, ((0, 4),))
    router_weight = centred(key_list[8], (D, E), D ** -0.5, 0.1875, ((0, 4),))
    up_weight = centred(key_list[9], (E, D, FF), D ** -0.5, 0.1875, ((1, 4),))
    down_weight = centred(key_list[10], (E, FF, D), FF ** -0.5, 0.109375, ((1, 4),))
    conv_weight = centred(key_list[11], (KW, DI), KW ** -0.5, 3.0, ((1, 4),))
    conv_bias = centred(key_list[12], (DI,), 0.3, 1.5, ((0, 4),))
    step_bias = jnp.clip(-9.0 + 7.0 * jax.random.uniform(key_list[13], (DI,), jnp.float32) ** steps_of(key_list[13], (DI,), ((0, 4),), -0.2, 0.2), -9.0, -2.0).astype(jnp.bfloat16)
    decay_log = jnp.clip(2.765625 * jax.random.uniform(key_list[14], (NS, DI), jnp.float32) ** steps_of(key_list[14], (NS, DI), ((1, 4),), -0.2, 0.2), 0.0, 2.765625).astype(jnp.bfloat16)
    skip_gain = jnp.clip(1.0 + 0.1 * jax.random.normal(key_list[15], (DI,), jnp.float32), 0.5, 1.5).astype(jnp.bfloat16)
    mixer_gain = jnp.clip(1.0 + 0.1 * jax.random.normal(key_list[16], (D,), jnp.float32), 0.5, 1.5).astype(jnp.bfloat16)
    expert_gain = jnp.clip(1.0 + 0.1 * jax.random.normal(key_list[17], (D,), jnp.float32), 0.5, 1.5).astype(jnp.bfloat16)
    return {"tokens": tokens, "routes": routes, "lengths": lengths, "cotangent": cotangent, "in_weight": in_weight, "select_weight": select_weight, "step_weight": step_weight, "out_weight": out_weight, "router_weight": router_weight, "up_weight": up_weight, "down_weight": down_weight, "conv_weight": conv_weight, "conv_bias": conv_bias, "step_bias": step_bias, "decay_log": decay_log, "skip_gain": skip_gain, "mixer_gain": mixer_gain, "expert_gain": expert_gain}


@jax.custom_vjp
def low(v):
    return lax.optimization_barrier(v.astype(jnp.bfloat16)).astype(jnp.float32)

@jax.custom_vjp
def low_back(v):
    return v

def low_keep(v):
    return (low(v), None)

def low_pass(kept, grad):
    return (grad,)

def back_keep(v):
    return (v, None)

def back_low(kept, grad):
    return (low(grad),)
low.defvjp(low_keep, low_pass)
low_back.defvjp(back_keep, back_low)
EPSILON = 1e-05

def rms_norm(values, gain):
    return values * lax.rsqrt(lax.optimization_barrier(jnp.mean(values * values, axis=-1, keepdims=True)) + EPSILON) * gain

def matmul(left, right):
    return jnp.dot(left, right, precision=lax.Precision.HIGHEST, preferred_element_type=jnp.float32)

def conv_act(padded, weight, bias):
    count = padded.shape[0] - (KW - 1)
    summed = bias[None, :] + weight[0][None, :] * padded[0:count]
    for offset in range(1, KW):
        summed = summed + weight[offset][None, :] * padded[offset:offset + count]
    return jax.nn.silu(summed)

def state_scan(inputs, steps, entry_map, read_map, decay, start):
    blocks = inputs.shape[0] // BLOCK

    def one_block(state, pieces):
        block_in, block_step, block_entry, block_read = pieces
        outputs = []
        for index in range(BLOCK):
            state = jnp.exp(block_step[index][None, :] * decay) * state + block_entry[index][:, None] * (block_step[index] * block_in[index])[None, :]
            outputs.append(lax.optimization_barrier(jnp.sum(block_read[index][:, None] * state, axis=0)))
        return (state, jnp.stack(outputs))
    pieces = (inputs.reshape(blocks, BLOCK, -1), steps.reshape(blocks, BLOCK, -1), entry_map.reshape(blocks, BLOCK, -1), read_map.reshape(blocks, BLOCK, -1))
    final, outputs = lax.scan(jax.checkpoint(one_block), start, pieces)
    return (outputs.reshape(inputs.shape[0], -1), final)

def layer(tokens, weights, length, route):
    in_weight, select_weight, step_weight, out_weight, router_weight, up_weight, down_weight, conv_weight, conv_bias, step_bias, decay_log, skip_gain, mixer_gain, expert_gain = weights
    count = tokens.shape[0]
    keep = (jnp.arange(count, dtype=jnp.int32) < length).astype(jnp.float32)[:, None]
    normed = low(rms_norm(tokens, mixer_gain))
    projected = low_back(matmul(normed, in_weight))
    inner = projected[:, :DI] * keep
    zgate = projected[:, DI:]
    padded = jnp.concatenate([jnp.zeros((KW - 1, DI), jnp.float32), inner], axis=0)
    conv_out = conv_act(padded, conv_weight, conv_bias)
    selected = low_back(matmul(low(conv_out), select_weight))
    step_pre = low_back(matmul(low(selected[:, :R]), step_weight)) + step_bias
    step_size = jax.nn.softplus(step_pre) * keep
    decay = -jnp.exp(decay_log)
    scanned, final = state_scan(conv_out, step_size, selected[:, R:R + NS], selected[:, R + NS:], decay, jnp.zeros((NS, DI), jnp.float32))
    mixed_in = scanned + skip_gain * conv_out
    gated = low(mixed_in * jax.nn.silu(zgate))
    first_sum = tokens + low_back(matmul(gated, out_weight))
    normed_two = low(rms_norm(first_sum, expert_gain))
    logits = low_back(matmul(normed_two, router_weight))
    probs = jax.nn.softmax(logits, axis=-1)
    onehot = (route == jnp.arange(E, dtype=jnp.int32)[None, :]).astype(jnp.float32)
    gate = lax.optimization_barrier(jnp.sum(probs * onehot, axis=1, keepdims=True)) * keep
    expert_sum = jnp.zeros((count, D), jnp.float32)
    for expert in range(E):
        pre = low_back(matmul(normed_two, up_weight[expert]))
        hidden_act = low(jax.nn.gelu(pre, approximate=True))
        expert_out = low_back(matmul(hidden_act, down_weight[expert]))
        expert_sum = expert_sum + onehot[:, expert:expert + 1] * expert_out
    return keep * (first_sum + gate * expert_sum)

def reference(tokens, routes, lengths, cotangent, in_weight, select_weight, step_weight, out_weight, router_weight, up_weight, down_weight, conv_weight, conv_bias, step_bias, decay_log, skip_gain, mixer_gain, expert_gain):
    weights = tuple((w.astype(jnp.float32) for w in (in_weight, select_weight, step_weight, out_weight, router_weight, up_weight, down_weight, conv_weight, conv_bias, step_bias, decay_log, skip_gain, mixer_gain, expert_gain)))
    seq_tokens = tokens.reshape(GROUPS, SEQ_LEN, D)
    seq_routes = routes.reshape(GROUPS, SEQ_LEN, 1)
    seq_cot = cotangent.reshape(GROUPS, SEQ_LEN, D)

    def one_seq(totals, pieces):
        seq_in, seq_route, length, seq_grad = pieces
        output, pull = jax.vjp(lambda value, params: layer(value, params, length, seq_route), seq_in, weights)
        grad_in, grad_params = pull(seq_grad)
        return (jax.tree.map(lambda left, right: left + right, totals, grad_params), (output, grad_in))
    start = tuple((jnp.zeros(w.shape, jnp.float32) for w in weights))
    totals, (outputs, grads) = lax.scan(one_seq, start, (seq_tokens, seq_routes, lengths, seq_cot))
    return (outputs.reshape(TOKENS, D), grads.reshape(TOKENS, D), totals[0], totals[3], totals[5], totals[6], totals[1], totals[2], totals[4], totals[7], totals[8], totals[9], totals[10], totals[11], totals[12], totals[13])
```

```python
import functools
import jax
import jax.numpy as jnp
from jax import lax
from jax.experimental import pallas as pl
from jax.experimental.pallas import tpu as pltpu
from jax.sharding import PartitionSpec as P

R = 72
KW = 4
E = 2
CAP = 192
EPSILON = 1e-05
LOG2E = 1.4426950408889634

NS = 16
LANES = 128
STEP = 8
CHUNK = 64


def fold_rows(parts):
    row = lax.broadcasted_iota(jnp.int32, (8, LANES), 0)
    top, pair, even = (row < 4, (row & 2) == 0, (row & 1) == 0)
    fours = [
        jnp.where(top, parts[i], parts[i + 4])
        + pltpu.roll(jnp.where(top, parts[i + 4], parts[i]), 4, 0)
        for i in range(4)
    ]
    twos = [
        jnp.where(
            pair,
            fours[i] + pltpu.roll(fours[i], 6, 0),
            fours[i + 2] + pltpu.roll(fours[i + 2], 2, 0),
        )
        for i in range(2)
    ]
    return jnp.where(
        even, twos[0] + pltpu.roll(twos[0], 7, 0), twos[1] + pltpu.roll(twos[1], 1, 0)
    )


def cut(value):
    return value.reshape(value.shape[0] // STEP, STEP, value.shape[1])


def halves(pair_ref, at, left):
    low, high = (pair_ref[at, 0:8], pair_ref[at, 8:16])
    return (low, high, jnp.where(left, low, high))


def scan_forward_kernel(tiles, dt_ref, dx_ref, entry_ref, read_ref, rate_ref, out_ref, state_ref, end_ref, held):
    @pl.when(pl.program_id(0) == 0)
    def start():
        held[...] = jnp.zeros_like(held)

    left = lax.broadcasted_iota(jnp.int32, (8, LANES), 1) < LANES // 2

    def group(g, states):
        at, base = (g, g * STEP)
        states = list(states)
        entry = [halves(entry_ref, base + t, left) for t in range(STEP)]
        read = [halves(read_ref, base + t, left) for t in range(STEP)]
        for tile in range(tiles + 1):
            columns = slice(tile * LANES, (tile + 1) * LANES)
            rows = [2 * tile] if tile == tiles else [2 * tile, 2 * tile + 1]
            which = [2] if tile == tiles else [0, 1]
            sums = []
            for t in range(STEP):
                step = dt_ref[at, t : t + 1, columns]
                fed = dx_ref[at, t : t + 1, columns]
                total = None
                for r, w in zip(rows, which):
                    state_ref[base + t, r] = states[r]
                    states[r] = jnp.exp2(step * rate_ref[r]) * states[r] + entry[t][w] * fed
                    term = read[t][w] * states[r]
                    total = term if total is None else total + term
                sums.append(total)
            out_ref[at, :, columns] = fold_rows(sums)
        return tuple(states)

    count = 2 * tiles + 1
    states = lax.fori_loop(0, dt_ref.shape[0], group, tuple(held[r] for r in range(count)))
    for r in range(count):
        held[r] = states[r]
        end_ref[r] = states[r]


def scan_forward(dt, dx, entry, read, rate, tiles):
    total, width = dt.shape
    count = 2 * tiles + 1
    chunk = min(CHUNK, total)
    row = pl.BlockSpec((chunk // STEP, STEP, width), lambda i: (i, 0, 0))
    pair = pl.BlockSpec((chunk, NS, LANES), lambda i: (i, 0, 0))
    fixed = pl.BlockSpec((count, 8, LANES), lambda i: (0, 0, 0))
    out, states, end = pl.pallas_call(
        functools.partial(scan_forward_kernel, tiles),
        grid=(total // chunk,),
        in_specs=[row, row, pair, pair, fixed],
        out_specs=[row, pl.BlockSpec((chunk, count, 8, LANES), lambda i: (i, 0, 0, 0)), fixed],
        out_shape=[
            jax.ShapeDtypeStruct((total // STEP, STEP, width), jnp.float32),
            jax.ShapeDtypeStruct((total, count, 8, LANES), jnp.float32),
            jax.ShapeDtypeStruct((count, 8, LANES), jnp.float32),
        ],
        scratch_shapes=[pltpu.VMEM((count, 8, LANES), jnp.float32)],
        compiler_params=pltpu.CompilerParams(vmem_limit_bytes=32 * 2**20),
        cost_estimate=pl.CostEstimate(flops=total * count * 8192, bytes_accessed=total * count * 4096, transcendentals=total * count * 1024),
        name="scan_forward",
    )(cut(dt), cut(dx), entry, read, rate)
    return out.reshape(total, width), states, end


def scan_backward_kernel(
    tiles, dt_ref, dx_ref, grad_ref, entry_ref, read_ref, rate_ref, state_ref, end_ref,
    fed_out, step_out, entry_out, read_out, rate_out, flow, after,
):
    count = 2 * tiles + 1

    @pl.when(pl.program_id(0) == 0)
    def start():
        flow[...] = jnp.zeros_like(flow)
        after[...] = end_ref[...]
        rate_out[...] = jnp.zeros_like(rate_out)

    left = lax.broadcasted_iota(jnp.int32, (8, LANES), 1) < LANES // 2
    groups = dt_ref.shape[0]

    def group(g, carry):
        at = groups - 1 - g
        base = at * STEP
        flows, afters = (list(carry[0]), list(carry[1]))
        entry = [halves(entry_ref, base + t, left) for t in range(STEP)]
        read = [halves(read_ref, base + t, left) for t in range(STEP)]
        entry_sum = [[None, None] for _ in range(STEP)]
        read_sum = [[None, None] for _ in range(STEP)]
        for tile in range(tiles + 1):
            last = tile == tiles
            columns = slice(tile * LANES, (tile + 1) * LANES)
            rows = [2 * tile] if last else [2 * tile, 2 * tile + 1]
            which = [2] if last else [0, 1]
            fed_sums, step_sums = ([None] * STEP, [None] * STEP)
            rate_sum = [rate_out[r] for r in rows]
            for t in reversed(range(STEP)):
                step = dt_ref[at, t : t + 1, columns]
                fed = dx_ref[at, t : t + 1, columns]
                grad = grad_ref[at, t : t + 1, columns]
                for i, (r, w) in enumerate(zip(rows, which)):
                    before = state_ref[base + t, r]
                    arriving = flows[r] + read[t][w] * grad
                    entry_term = arriving * fed
                    read_term = afters[r] * grad
                    fed_term = entry[t][w] * arriving
                    leaving = jnp.exp2(step * rate_ref[r]) * arriving
                    product = leaving * before
                    step_term = product * rate_ref[r]
                    rate_sum[i] = rate_sum[i] + product * step
                    flows[r] = leaving
                    afters[r] = before
                    fed_sums[t] = fed_term if i == 0 else fed_sums[t] + fed_term
                    step_sums[t] = step_term if i == 0 else step_sums[t] + step_term
                    for total, term in ((entry_sum[t], entry_term), (read_sum[t], read_term)):
                        if last:
                            total[0] = total[0] + jnp.where(left, term, 0.0)
                            total[1] = total[1] + jnp.where(left, 0.0, term)
                        else:
                            total[i] = term if total[i] is None else total[i] + term
            fed_out[at, :, columns] = fold_rows(fed_sums)
            step_out[at, :, columns] = fold_rows(step_sums)
            for i, r in enumerate(rows):
                rate_out[r] = rate_sum[i]
        for t in range(STEP):
            for i in range(2):
                entry_out[base + t, 8 * i : 8 * i + 8] = entry_sum[t][i]
                read_out[base + t, 8 * i : 8 * i + 8] = read_sum[t][i]
        return (tuple(flows), tuple(afters))

    flows, afters = lax.fori_loop(
        0,
        groups,
        group,
        (tuple(flow[r] for r in range(count)), tuple(after[r] for r in range(count))),
    )
    for r in range(count):
        flow[r] = flows[r]
        after[r] = afters[r]


def scan_backward(dt, dx, grad, entry, read, rate, states, end, tiles):
    total, width = dt.shape
    count = 2 * tiles + 1
    chunk = min(CHUNK, total)
    steps = total // chunk
    row = pl.BlockSpec((chunk // STEP, STEP, width), lambda i: (steps - 1 - i, 0, 0))
    pair = pl.BlockSpec((chunk, NS, LANES), lambda i: (steps - 1 - i, 0, 0))
    fixed = pl.BlockSpec((count, 8, LANES), lambda i: (0, 0, 0))
    wide = jax.ShapeDtypeStruct((total // STEP, STEP, width), jnp.float32)
    paired = jax.ShapeDtypeStruct((total, NS, LANES), jnp.float32)
    fed, rise, entry_parts, read_parts, rates = pl.pallas_call(
        functools.partial(scan_backward_kernel, tiles),
        grid=(steps,),
        in_specs=[row, row, row, pair, pair, fixed, pl.BlockSpec((chunk, count, 8, LANES), lambda i: (steps - 1 - i, 0, 0, 0)), fixed],
        out_specs=[row, row, pair, pair, fixed],
        out_shape=[wide, wide, paired, paired, jax.ShapeDtypeStruct((count, 8, LANES), jnp.float32)],
        scratch_shapes=[pltpu.VMEM((count, 8, LANES), jnp.float32)] * 2,
        compiler_params=pltpu.CompilerParams(vmem_limit_bytes=48 * 2**20),
        cost_estimate=pl.CostEstimate(flops=total * count * 20480, bytes_accessed=total * count * 4096, transcendentals=total * count * 1024),
        name="scan_backward",
    )(cut(dt), cut(dx), cut(grad), entry, read, rate, states, end)
    return fed.reshape(total, width), rise.reshape(total, width), entry_parts, read_parts, rates


def swap(value, bit):
    size = lax.axis_size("shard")
    return lax.ppermute(value, "shard", [(i, i ^ bit) for i in range(size)])


def gather_rows(value):
    me = lax.axis_index("shard")
    near, far = (swap(value, 1), swap(value, 2))
    pieces = (value, near, far, swap(far, 1))
    rows = value.shape[0]
    whole = jnp.zeros((4 * rows,) + value.shape[1:], value.dtype)
    for k, piece in enumerate(pieces):
        whole = lax.dynamic_update_slice_in_dim(whole, piece, (me ^ k) * rows, 0)
    return whole


def scatter_rows(value):
    me = lax.axis_index("shard")
    side, core = (me // 2, me % 2)
    rows = value.shape[0] // 4
    cut = value.reshape(2, 2, rows, value.shape[1])
    held = lax.dynamic_index_in_dim(cut, core, 1, False)
    given = lax.dynamic_index_in_dim(cut, 1 - core, 1, False).astype(jnp.bfloat16)
    held = held + swap(given, 1).astype(jnp.float32)
    mine = lax.dynamic_index_in_dim(held, side, 0, False)
    given = lax.dynamic_index_in_dim(held, 1 - side, 0, False).astype(jnp.bfloat16)
    return mine + swap(given, 2).astype(jnp.float32)


def sum_small(value):
    value = value + swap(value, 1)
    return value + swap(value, 2)


def turn_blocks(blocks, axis):
    me = lax.axis_index("shard")
    one = blocks.shape[1:]
    rows = one[axis]
    whole = jnp.zeros(one[:axis] + (4 * rows,) + one[axis + 1 :], blocks.dtype)
    for k in range(4):
        piece = lax.dynamic_index_in_dim(blocks, me ^ k, 0, False)
        if k > 0:
            piece = swap(piece, k)
        whole = lax.dynamic_update_slice_in_dim(whole, piece, (me ^ k) * rows, axis)
    return whole


def rms_norm(values, gain):
    return values * lax.rsqrt(jnp.mean(values * values, axis=-1, keepdims=True) + EPSILON) * gain


def matmul(left, right):
    return jnp.dot(left, right, preferred_element_type=jnp.float32)


def matmul_t(left, right):
    return lax.dot_general(left, right, (((1,), (1,)), ((), ())), preferred_element_type=jnp.float32)


def t_matmul(left, right):
    return lax.dot_general(left, right, (((0,), (0,)), ((), ())), preferred_element_type=jnp.float32)


def widen(value, tiles):
    return jnp.concatenate([value, value[:, tiles * LANES :]], axis=1)


def narrow(value, tiles):
    edge = tiles * LANES
    middle = edge + LANES // 2
    return jnp.concatenate([value[:, :edge], value[:, edge:middle] + value[:, middle:]], axis=1)


def pack(value, tiles):
    edge = tiles * LANES
    full = value[:, :edge].reshape(2, 8, tiles, LANES).transpose(2, 0, 1, 3)
    rest = jnp.concatenate([value[:8, edge:], value[8:, edge:]], axis=1)
    return jnp.concatenate([full.reshape(2 * tiles, 8, LANES), rest[None]], axis=0)


def unpack(value, tiles):
    full = value[: 2 * tiles].reshape(tiles, 2, 8, LANES).transpose(1, 2, 0, 3)
    rest = value[2 * tiles]
    rest = jnp.concatenate([rest[:, : LANES // 2], rest[:, LANES // 2 :]], axis=0)
    return jnp.concatenate([full.reshape(NS, tiles * LANES), rest], axis=1)


def spread(value):
    return jnp.broadcast_to(value[:, :, None], value.shape + (LANES,))


def body(
    tokens,
    routes,
    lengths,
    cotangent,
    in_weight,
    select_weight,
    step_weight,
    out_weight,
    router_weight,
    up_weight,
    down_weight,
    conv_weight,
    conv_bias,
    step_bias,
    decay_log,
    skip_gain,
    mixer_gain,
    expert_gain,
):
    f32, bf16 = (jnp.float32, jnp.bfloat16)
    span, width = tokens.shape
    groups, parts = (lax.axis_size("grp"), lax.axis_size("shard"))
    me = lax.axis_index("shard")
    total = span * parts
    inside = conv_bias.shape[0]
    tiles = inside // LANES
    slab = in_weight.shape[0]
    hidden_cols = up_weight.shape[2] // parts

    first = (routes[:, 0] == 0).astype(jnp.int32)
    count_first = jnp.sum(first)
    small = jnp.stack(
        [
            mixer_gain.astype(f32),
            expert_gain.astype(f32),
            router_weight[:, 0].astype(f32),
            router_weight[:, 1].astype(f32),
            jnp.full((slab,), count_first, jnp.int32).astype(f32),
        ]
    )
    small = gather_rows(small[None])
    mixer_full = small[:, 0].reshape(width)
    expert_full = small[:, 1].reshape(width)
    router_full = small[:, 2:4].transpose(0, 2, 1).reshape(width, E).astype(bf16)
    counts = small[:, 4, 0].astype(jnp.int32)

    normed_one, norm_pull = jax.vjp(rms_norm, tokens, mixer_full)
    normed = gather_rows(normed_one.astype(bf16))
    in_blocks = in_weight.reshape(slab, 2, parts, inside).transpose(2, 1, 0, 3)
    in_full = turn_blocks(in_blocks, 1)
    up_blocks = up_weight.reshape(E, slab, parts, hidden_cols).transpose(2, 0, 1, 3)
    up_full = turn_blocks(up_blocks, 1)

    keep = (jnp.arange(total, dtype=jnp.int32) < lengths[0]).astype(f32)[:, None]
    place = me * span + jnp.arange(span, dtype=jnp.int32)
    keep_mine = (place < lengths[0]).astype(f32)[:, None]

    inner = matmul(normed, in_full[0]) * keep
    zgate = matmul(normed, in_full[1])
    taps = conv_weight.astype(f32)
    padded = jnp.concatenate([jnp.zeros((KW - 1, inside), f32), inner], axis=0)
    summed = conv_bias.astype(f32)[None, :]
    for k in range(KW):
        summed = summed + taps[k][None, :] * padded[k : k + total]
    conv_out = jax.nn.silu(summed)
    conv_low = conv_out.astype(bf16)
    selected = sum_small(matmul(conv_low, select_weight))
    rank_low = selected[:, :R].astype(bf16)
    step_pre = matmul(rank_low, step_weight) + step_bias.astype(f32)[None, :]
    step_size = jax.nn.softplus(step_pre) * keep
    entry = spread(selected[:, R : R + NS])
    read = spread(selected[:, R + NS :])
    decay = -jnp.exp(decay_log.astype(f32))
    rate = pack(decay * LOG2E, tiles)
    dt_wide = widen(step_size, tiles)
    dx_wide = widen(step_size * conv_out, tiles)
    scanned, states, end = scan_forward(dt_wide, dx_wide, entry, read, rate, tiles)
    skip = skip_gain.astype(f32)[None, :]
    mixed_in = narrow(scanned, tiles) + skip * conv_out
    gated = (mixed_in * jax.nn.silu(zgate)).astype(bf16)
    first_sum = tokens + scatter_rows(matmul(gated, out_weight))

    normed_second, norm_two_pull = jax.vjp(rms_norm, first_sum, expert_full)
    normed_two = normed_second.astype(bf16)
    logits = matmul(normed_two, router_full)
    probs = jax.nn.softmax(logits, axis=-1)
    picked = (routes == jnp.arange(E, dtype=jnp.int32)[None, :]).astype(f32) * keep_mine
    gate = jnp.sum(probs * picked, axis=1, keepdims=True)
    grad_out = keep_mine * cotangent
    second = 1 - first
    goal = jnp.where(first > 0, jnp.cumsum(first) - 1, count_first + jnp.cumsum(second) - 1)
    order = (jnp.arange(span, dtype=jnp.int32)[:, None] == goal[None, :]).astype(bf16)
    pair = jnp.concatenate([normed_two, (gate * grad_out).astype(bf16)], axis=1)
    pair = gather_rows(matmul(order, pair).astype(bf16)).reshape(parts, span, 2 * width)
    offset = span - CAP
    pair = jnp.stack([pair[:, :CAP], pair[:, offset:]]).reshape(E, parts * CAP, 2 * width)
    rows, grad_rows_out = (pair[:, :, :width], pair[:, :, width:])
    at = jnp.arange(CAP, dtype=jnp.int32)[None, :]
    mask = jnp.stack([at < counts[:, None], at + offset >= counts[:, None]])
    mask = mask.reshape(E, parts * CAP, 1)
    pre = jnp.einsum("ecd,edf->ecf", rows, up_full, preferred_element_type=f32)
    hidden_f, gelu_pull = jax.vjp(lambda value: jax.nn.gelu(value, approximate=True), pre)
    hidden = jnp.where(mask, hidden_f, 0.0).astype(bf16)
    expert_out = jnp.einsum("ecf,efd->ecd", hidden, down_weight, preferred_element_type=f32)
    grad_hidden = jnp.einsum("ecd,efd->ecf", grad_rows_out, down_weight, preferred_element_type=f32)
    grad_pre = jnp.where(mask, gelu_pull(grad_hidden)[0], 0.0).astype(bf16)
    grad_rows = jnp.einsum("ecf,edf->ecd", grad_pre, up_full, preferred_element_type=f32)
    up_grad = jnp.einsum("ecd,ecf->edf", rows, grad_pre, preferred_element_type=f32).astype(bf16)
    down_grad = jnp.einsum("ecd,ecf->edf", grad_rows_out, hidden, preferred_element_type=f32).astype(bf16)
    both = jnp.concatenate([expert_out, grad_rows], axis=2).reshape(E, parts, CAP, 2 * width)
    both = jnp.pad(both[0], ((0, 0), (0, offset), (0, 0))) + jnp.pad(both[1], ((0, 0), (offset, 0), (0, 0)))
    both = scatter_rows(both.reshape(total, 2 * width))
    both = lax.dot_general(
        order.astype(f32),
        both,
        (((0,), (0,)), ((), ())),
        precision=lax.Precision.HIGHEST,
        preferred_element_type=f32,
    )
    token_out, grad_normed = (both[:, :width], both[:, width:])
    result = keep_mine * (first_sum + gate * token_out)

    grad_gate = picked * jnp.sum(token_out * grad_out, axis=1, keepdims=True)
    grad_logits = probs * (grad_gate - jnp.sum(grad_gate * probs, axis=1, keepdims=True))
    grad_logits = grad_logits.astype(bf16)
    router_grad = t_matmul(normed_two, grad_logits)
    grad_normed = grad_normed + matmul_t(grad_logits, router_full)
    grad_first_norm, expert_gain_grad = norm_two_pull(grad_normed)
    grad_first = grad_out + grad_first_norm

    grad_first_low = gather_rows(grad_first.astype(bf16))
    out_grad = t_matmul(grad_first_low, gated).astype(bf16)
    grad_gated = matmul_t(grad_first_low, out_weight)
    sig = jax.nn.sigmoid(zgate)
    grad_mixed = grad_gated * (zgate * sig)
    grad_zgate = grad_gated * mixed_in * (sig * (1.0 + zgate * (1.0 - sig)))
    skip_grad = jnp.sum(grad_mixed * conv_out, axis=0)
    fed_wide, rise_wide, entry_parts, read_parts, rate_parts = scan_backward(
        dt_wide, dx_wide, widen(grad_mixed, tiles), entry, read, rate, states, end, tiles
    )
    grad_fed = narrow(fed_wide, tiles)
    grad_step = narrow(rise_wide, tiles) * (1.0 / LOG2E) + grad_fed * conv_out
    decay_grad = decay * unpack(rate_parts, tiles)
    grad_step_pre = keep * jax.nn.sigmoid(step_pre) * grad_step
    step_bias_grad = jnp.sum(grad_step_pre, axis=0)
    grad_step_low = grad_step_pre.astype(bf16)
    step_grad = t_matmul(rank_low, grad_step_low)
    grad_rank = matmul_t(grad_step_low, step_weight)
    grad_selected = jnp.concatenate(
        [grad_rank, jnp.sum(entry_parts, axis=2), jnp.sum(read_parts, axis=2)], axis=1
    )
    grad_selected = sum_small(grad_selected).astype(bf16)
    select_grad = t_matmul(conv_low, grad_selected)
    grad_conv = grad_fed * step_size + skip * grad_mixed + matmul_t(grad_selected, select_weight)
    curve = jax.nn.sigmoid(summed)
    grad_summed = grad_conv * (curve * (1.0 + summed * (1.0 - curve)))
    conv_bias_grad = jnp.sum(grad_summed, axis=0)
    conv_grad = jnp.stack(
        [jnp.sum(grad_summed * padded[k : k + total], axis=0) for k in range(KW)]
    )
    grad_padded = jnp.concatenate([grad_summed, jnp.zeros((KW - 1, inside), f32)], axis=0)
    grad_inner = jnp.zeros((total, inside), f32)
    for k in range(KW):
        grad_inner = grad_inner + taps[k][None, :] * grad_padded[KW - 1 - k : KW - 1 - k + total]
    grad_inner_low = (keep * grad_inner).astype(bf16)
    grad_zgate_low = grad_zgate.astype(bf16)
    grad_normed_one = scatter_rows(
        matmul_t(grad_inner_low, in_full[0]) + matmul_t(grad_zgate_low, in_full[1])
    )
    in_grad = jnp.stack(
        [t_matmul(normed, grad_inner_low).astype(bf16), t_matmul(normed, grad_zgate_low).astype(bf16)]
    )
    grad_tokens_norm, mixer_gain_grad = norm_pull(grad_normed_one)
    tokens_grad = grad_first + grad_tokens_norm

    fours, eights = (groups // 4, groups // 8)
    up_cols = hidden_cols // fours
    up_cut = up_grad.reshape(E, parts, slab, fours, up_cols).transpose(3, 1, 0, 2, 4)
    up_cut = up_cut.reshape(groups, E * slab, up_cols)
    up_sum = lax.psum_scatter(up_cut, "grp", scatter_dimension=0, tiled=True)
    in_cols = inside // eights
    in_cut = in_grad.reshape(2, parts, slab, eights, in_cols).transpose(0, 3, 1, 2, 4)
    in_cut = in_cut.reshape(groups, slab, in_cols)
    in_sum = lax.psum_scatter(in_cut, "grp", scatter_dimension=0, tiled=True)
    out_sum = lax.psum_scatter(out_grad, "grp", scatter_dimension=0, tiled=True)
    down_sum = lax.psum_scatter(down_grad, "grp", scatter_dimension=1, tiled=True)
    up_moves, in_moves = ([], [])
    for g in range(groups):
        for s in range(parts):
            up_moves.append((g * parts + s, (s * fours + g // 4) * parts + g % 4))
            half, k = (g // (groups // 2), (g // 4) % eights)
            in_moves.append((g * parts + s, (half * (groups // 2) + s * eights + k) * parts + g % 4))
    both_axes = ("grp", "shard")
    up_sum = lax.ppermute(up_sum, both_axes, up_moves)
    in_sum = lax.ppermute(in_sum, both_axes, in_moves)

    mine = lax.psum(
        (select_grad, step_grad, conv_grad, conv_bias_grad, step_bias_grad, decay_grad, skip_grad),
        "grp",
    )
    shared = jnp.concatenate([router_grad.T, mixer_gain_grad[None], expert_gain_grad[None]], axis=0)
    shared = lax.psum(shared, both_axes)
    shared = lax.dynamic_slice_in_dim(shared, me * slab, slab, 1)
    return (
        result,
        tokens_grad,
        in_sum[0].astype(f32),
        out_sum.astype(f32).T,
        up_sum[0].astype(f32).reshape(E, slab, up_cols),
        down_sum.astype(f32).transpose(0, 2, 1),
        mine[0],
        mine[1],
        shared[0:2].T,
        mine[2],
        mine[3],
        mine[4],
        mine[5],
        mine[6],
        shared[2],
        shared[3],
    )


def solution(mesh):
    return jax.shard_map(
        body,
        mesh=mesh,
        in_specs=(
            P(("grp", "shard"), None),
            P(("grp", "shard"), None),
            P("grp"),
            P(("grp", "shard"), None),
            P("shard", None),
            P("shard", None),
            P(None, "shard"),
            P("shard", None),
            P("shard", None),
            P(None, "shard", None),
            P(None, "shard", None),
            P(None, "shard"),
            P("shard"),
            P("shard"),
            P(None, "shard"),
            P("shard"),
            P("shard"),
            P("shard"),
        ),
        out_specs=(
            P(("grp", "shard"), None),
            P(("grp", "shard"), None),
            P("shard", "grp"),
            P("shard", "grp"),
            P(None, "shard", "grp"),
            P(None, "shard", "grp"),
            P("shard", None),
            P(None, "shard"),
            P("shard", None),
            P(None, "shard"),
            P("shard"),
            P("shard"),
            P(None, "shard"),
            P("shard"),
            P("shard"),
            P("shard"),
        ),
        check_vma=False,
    )
```

```python
import functools
import jax
import jax.numpy as jnp
from jax import lax
from jax.experimental import pallas as pl
from jax.experimental.pallas import tpu as pltpu
from jax.sharding import PartitionSpec as P

R = 72
KW = 4
E = 2
CAP = 192
EPSILON = 1e-05
FTILE = 256
LOG2E = 1.4426950408889634

NS = 16
LANES = 128
STEP = 8
CHUNK = 64


def swap(value, bit):
    size = lax.axis_size("shard")
    return lax.ppermute(value, "shard", [(i, i ^ bit) for i in range(size)])


def swap_groups(value, bit):
    size = lax.axis_size("grp")
    return lax.ppermute(value, "grp", [(g, g ^ bit) for g in range(size)])


def tie(value, *others):
    for other in others:
        corner = other[(0,) * other.ndim].astype(jnp.float32)
        value = value + (0.0 * corner).astype(value.dtype)
    return value


def gather_pieces(value):
    far = swap(value, 2)
    return (value, swap(value, 1), far, swap(far, 1))


def scatter_near(held, given, *others):
    side = lax.axis_index("shard") // 2
    held = tie(held + swap(given, 1).astype(jnp.float32), *others)
    mine = lax.dynamic_index_in_dim(held, side, 0, False)
    return mine, lax.dynamic_index_in_dim(held, 1 - side, 0, False).astype(jnp.bfloat16)


def halve(value, axis, bit):
    mine = (lax.axis_index("grp") // bit) % 2
    shape = value.shape
    value = value.reshape(shape[:axis] + (shape[axis] // 2, 2) + shape[axis + 1 :])
    held = lax.dynamic_index_in_dim(value, mine, axis + 1, False)
    given = lax.dynamic_index_in_dim(value, 1 - mine, axis + 1, False)
    return held, given.astype(jnp.bfloat16)


def join(held, got, *others):
    return tie(held.astype(jnp.float32) + got.astype(jnp.float32), *others)


def sum_rest(value, steps):
    for axis, bit in steps:
        held, given = halve(value, axis, bit)
        value = join(held, swap_groups(given, bit))
    return value


def share_pieces(pieces):
    groups, parts = (lax.axis_size("grp"), lax.axis_size("shard"))
    moves = [
        (g * parts + s, g * parts + (s ^ (2 + g % 2))) for g in range(groups) for s in range(parts)
    ]
    crossed = lax.ppermute(pieces[2], ("grp", "shard"), moves)
    shared = lax.ppermute(crossed, "grp", [(g, g ^ 1) for g in range(groups)])
    return [pieces[0], swap(pieces[1], 1), crossed, shared]


def total_groups(value):
    groups = lax.axis_size("grp")
    bit = 1
    while bit < groups:
        value = value.astype(jnp.bfloat16)
        value = value.astype(jnp.float32) + swap_groups(value, bit).astype(jnp.float32)
        bit = 2 * bit
    return value


def matmul(left, right):
    return jnp.dot(left, right, preferred_element_type=jnp.float32)


def pack(value, tiles):
    edge = tiles * LANES
    full = value[:, :edge].reshape(2, 8, tiles, LANES).transpose(2, 0, 1, 3)
    rest = jnp.concatenate([value[:8, edge:], value[8:, edge:]], axis=1)
    return jnp.concatenate([full.reshape(2 * tiles, 8, LANES), rest[None]], axis=0)


def unpack(value, tiles):
    full = value[: 2 * tiles].reshape(tiles, 2, 8, LANES).transpose(1, 2, 0, 3)
    rest = value[2 * tiles]
    rest = jnp.concatenate([rest[:, : LANES // 2], rest[:, LANES // 2 :]], axis=0)
    return jnp.concatenate([full.reshape(NS, tiles * LANES), rest], axis=1)


def fold_rows(parts):
    row = lax.broadcasted_iota(jnp.int32, (8, LANES), 0)
    top, pair, even = (row < 4, (row & 2) == 0, (row & 1) == 0)
    fours = [
        jnp.where(top, parts[i], parts[i + 4])
        + pltpu.roll(jnp.where(top, parts[i + 4], parts[i]), 4, 0)
        for i in range(4)
    ]
    twos = [
        jnp.where(
            pair,
            fours[i] + pltpu.roll(fours[i], 6, 0),
            fours[i + 2] + pltpu.roll(fours[i + 2], 2, 0),
        )
        for i in range(2)
    ]
    return jnp.where(
        even, twos[0] + pltpu.roll(twos[0], 7, 0), twos[1] + pltpu.roll(twos[1], 1, 0)
    )


def halves(pair_ref, at, left):
    low, high = (pair_ref[at, 0:8], pair_ref[at, 8:16])
    return (low, high, jnp.where(left, low, high))


def scan_forward_chunk(tiles, dt_ref, dx_ref, entry_ref, read_ref, rate_ref, out_ref, state_ref, end_ref, held):
    left = lax.broadcasted_iota(jnp.int32, (8, LANES), 1) < LANES // 2

    def group(g, states):
        at, base = (g, g * STEP)
        states = list(states)
        entry = [halves(entry_ref, base + t, left) for t in range(STEP)]
        read = [halves(read_ref, base + t, left) for t in range(STEP)]
        for tile in range(tiles + 1):
            columns = slice(tile * LANES, (tile + 1) * LANES)
            rows = [2 * tile] if tile == tiles else [2 * tile, 2 * tile + 1]
            which = [2] if tile == tiles else [0, 1]
            sums = []
            for t in range(STEP):
                step = dt_ref[at, t : t + 1, columns]
                fed = dx_ref[at, t : t + 1, columns]
                total = None
                for r, w in zip(rows, which):
                    state_ref[base + t, r] = states[r]
                    states[r] = jnp.exp2(step * rate_ref[r]) * states[r] + entry[t][w] * fed
                    term = read[t][w] * states[r]
                    total = term if total is None else total + term
                sums.append(total)
            out_ref[at, :, columns] = fold_rows(sums)
        return tuple(states)

    count = 2 * tiles + 1
    states = lax.fori_loop(0, dt_ref.shape[0], group, tuple(held[r] for r in range(count)))
    for r in range(count):
        held[r] = states[r]
        end_ref[r] = states[r]


def scan_backward_chunk(
    tiles, dt_ref, dx_ref, grad_ref, entry_ref, read_ref, rate_ref, state_ref,
    fed_out, step_out, entry_out, read_out, rate_out, flow, after,
):
    count = 2 * tiles + 1
    left = lax.broadcasted_iota(jnp.int32, (8, LANES), 1) < LANES // 2
    groups = dt_ref.shape[0]

    def group(g, carry):
        at = groups - 1 - g
        base = at * STEP
        flows, afters = (list(carry[0]), list(carry[1]))
        entry = [halves(entry_ref, base + t, left) for t in range(STEP)]
        read = [halves(read_ref, base + t, left) for t in range(STEP)]
        entry_sum = [[None, None] for _ in range(STEP)]
        read_sum = [[None, None] for _ in range(STEP)]
        for tile in range(tiles + 1):
            last = tile == tiles
            columns = slice(tile * LANES, (tile + 1) * LANES)
            rows = [2 * tile] if last else [2 * tile, 2 * tile + 1]
            which = [2] if last else [0, 1]
            fed_sums, step_sums = ([None] * STEP, [None] * STEP)
            rate_sum = [rate_out[r] for r in rows]
            for t in reversed(range(STEP)):
                step = dt_ref[at, t : t + 1, columns]
                fed = dx_ref[at, t : t + 1, columns]
                grad = grad_ref[at, t : t + 1, columns]
                for i, (r, w) in enumerate(zip(rows, which)):
                    before = state_ref[base + t, r]
                    arriving = flows[r] + read[t][w] * grad
                    entry_term = arriving * fed
                    read_term = afters[r] * grad
                    fed_term = entry[t][w] * arriving
                    leaving = jnp.exp2(step * rate_ref[r]) * arriving
                    product = leaving * before
                    step_term = product * rate_ref[r]
                    rate_sum[i] = rate_sum[i] + product * step
                    flows[r] = leaving
                    afters[r] = before
                    fed_sums[t] = fed_term if i == 0 else fed_sums[t] + fed_term
                    step_sums[t] = step_term if i == 0 else step_sums[t] + step_term
                    for total, term in ((entry_sum[t], entry_term), (read_sum[t], read_term)):
                        if last:
                            total[0] = total[0] + jnp.where(left, term, 0.0)
                            total[1] = total[1] + jnp.where(left, 0.0, term)
                        else:
                            total[i] = term if total[i] is None else total[i] + term
            fed_out[at, :, columns] = fold_rows(fed_sums)
            step_out[at, :, columns] = fold_rows(step_sums)
            for i, r in enumerate(rows):
                rate_out[r] = rate_sum[i]
        for t in range(STEP):
            for i in range(2):
                entry_out[base + t, 8 * i : 8 * i + 8] = entry_sum[t][i]
                read_out[base + t, 8 * i : 8 * i + 8] = read_sum[t][i]
        return (tuple(flows), tuple(afters))

    flows, afters = lax.fori_loop(
        0,
        groups,
        group,
        (tuple(flow[r] for r in range(count)), tuple(after[r] for r in range(count))),
    )
    for r in range(count):
        flow[r] = flows[r]
        after[r] = afters[r]


def split_low(value):
    high = value.astype(jnp.bfloat16)
    return high, (value - high.astype(jnp.float32)).astype(jnp.bfloat16)


def dot(left, right):
    return jnp.dot(left, right, preferred_element_type=jnp.float32)


def dot_t(left, right):
    return lax.dot_general(left, right, (((1,), (1,)), ((), ())), preferred_element_type=jnp.float32)


def t_dot(left, right):
    return lax.dot_general(left, right, (((0,), (0,)), ((), ())), preferred_element_type=jnp.float32)


def live_rows(me_ref, length_ref, rows):
    slot = me_ref[0] * rows + lax.broadcasted_iota(jnp.int32, (rows, 1), 0)
    return slot < length_ref[0]


def router_rows(gains_ref):
    row = lax.broadcasted_iota(jnp.int32, gains_ref.shape, 0)
    return jnp.where(row < E, gains_ref[...], 0.0).astype(jnp.bfloat16)


def cut_kernel(parts, inside, cols, goal_ref, in_ref, up_ref, *rest):
    number = len(rest) // 2
    in_outs, up_outs, sems = (rest[:number], rest[number : 2 * number], rest[-1])
    copies = []
    for k in range(number):
        columns = pl.ds(pl.multiple_of(goal_ref[k] * cols, LANES), cols)
        copies.append(pltpu.make_async_copy(up_ref.at[:, :, columns], up_outs[k], sems.at[k]))
        copies[-1].start()
    for d in range(parts):
        for k in range(number):

            @pl.when(goal_ref[k] == d)
            def write():
                in_outs[k][:, :inside] = in_ref[:, d * inside : (d + 1) * inside]
                at = (parts + d) * inside
                in_outs[k][:, inside:] = in_ref[:, at : at + inside]

    for copy in copies:
        copy.wait()


def cut_weights(goal, in_weight, up_weight, parts, inside):
    slab = in_weight.shape[0]
    cols = up_weight.shape[2] // parts
    number = 3
    in_shape = jax.ShapeDtypeStruct((slab, 2 * inside), in_weight.dtype)
    up_shape = jax.ShapeDtypeStruct((up_weight.shape[0], slab, cols), up_weight.dtype)
    vmem, anywhere = (pl.BlockSpec(memory_space=pltpu.VMEM), pl.BlockSpec(memory_space=pl.ANY))
    outs = pl.pallas_call(
        functools.partial(cut_kernel, parts, inside, cols),
        in_specs=[pl.BlockSpec(memory_space=pltpu.SMEM), vmem, anywhere],
        out_specs=[vmem] * number + [anywhere] * number,
        out_shape=[in_shape] * number + [up_shape] * number,
        scratch_shapes=[pltpu.SemaphoreType.DMA((number,))],
        compiler_params=pltpu.CompilerParams(vmem_limit_bytes=24 * 2**20),
        name="cut_weights",
    )(goal, in_weight, up_weight)
    return outs[:number], outs[number:]


def to_power(value):
    return value / (1.0 + jnp.exp(-value))


def project_kernel(parts, inside, me_ref, source_ref, length_ref, *rest):
    normed_refs, weight_refs, rest = (rest[:parts], rest[parts : 2 * parts], rest[2 * parts :])
    taps_ref, bias_ref, select_ref, inner_out, gate_out, summed_out, conv_out, low_out, selected_out = rest[:9]
    normed, weight, shifted, sems = rest[9:]
    block = pl.program_id(0)
    me = me_ref[0]
    rows, slab = (normed_refs[0].shape[0], weight_refs[0].shape[0])

    @pl.when(block == 0)
    def fetch():
        copies = []
        for k in range(parts):
            at = pl.ds(pl.multiple_of(source_ref[k] * slab, 16), slab)
            copies.append(pltpu.make_async_copy(weight_refs[k], weight.at[at], sems.at[k]))
            at = pl.ds(pl.multiple_of((me ^ k) * rows, 16), rows)
            copies.append(pltpu.make_async_copy(normed_refs[k], normed.at[at], sems.at[parts + k]))
        for copy in copies:
            copy.start()
        for copy in copies:
            copy.wait()
        shifted[0:8] = jnp.zeros((8, inside), jnp.float32)

    start = pl.multiple_of(block * rows, 16)
    projected = jnp.dot(normed[pl.ds(start, rows)], weight[...], preferred_element_type=jnp.float32)
    slot = block * rows + lax.broadcasted_iota(jnp.int32, (rows, 1), 0)
    inner = jnp.where(slot < length_ref[0], projected[:, :inside], 0.0)
    gate_out[...] = projected[:, inside:]
    inner_out[...] = inner
    shifted[8:] = inner
    summed = bias_ref[...]
    for k in range(KW):
        summed = summed + taps_ref[k : k + 1] * shifted[8 - (KW - 1) + k : 8 - (KW - 1) + k + rows]
    shifted[0:8] = shifted[rows : rows + 8]
    summed_out[...] = summed
    value = to_power(summed)
    conv_out[...] = value
    low = value.astype(jnp.bfloat16)
    low_out[...] = low
    selected_out[...] = jnp.dot(low, select_ref[...], preferred_element_type=jnp.float32)


def project(me, source, length, normed_pieces, weight_pieces, taps, bias, select_wide):
    parts = len(normed_pieces)
    rows, width = normed_pieces[0].shape
    slab, both = weight_pieces[0].shape
    inside, picked = select_wide.shape
    total = rows * parts
    smem, anywhere = (pl.BlockSpec(memory_space=pltpu.SMEM), pl.BlockSpec(memory_space=pl.ANY))
    vmem = pl.BlockSpec(memory_space=pltpu.VMEM)
    row = pl.BlockSpec((rows, inside), lambda i: (i, 0))
    wide = jax.ShapeDtypeStruct((total, inside), jnp.float32)
    return pl.pallas_call(
        functools.partial(project_kernel, parts, inside),
        grid=(parts,),
        in_specs=[smem] * 3 + [anywhere] * (2 * parts) + [vmem] * 3,
        out_specs=[row] * 5 + [pl.BlockSpec((rows, picked), lambda i: (i, 0))],
        out_shape=[wide] * 4
        + [
            jax.ShapeDtypeStruct((total, inside), jnp.bfloat16),
            jax.ShapeDtypeStruct((total, picked), jnp.float32),
        ],
        scratch_shapes=[
            pltpu.VMEM((total, width), jnp.bfloat16),
            pltpu.VMEM((slab * parts, both), jnp.bfloat16),
            pltpu.VMEM((rows + 8, inside), jnp.float32),
            pltpu.SemaphoreType.DMA((2 * parts,)),
        ],
        compiler_params=pltpu.CompilerParams(vmem_limit_bytes=40 * 2**20),
        cost_estimate=pl.CostEstimate(flops=2 * total * width * both, bytes_accessed=20 * 2**20, transcendentals=total * inside),
        name="project",
    )(me, source, length, *normed_pieces, *weight_pieces, taps, bias, select_wide)


def live_slots(start, length_ref, rows):
    return start + lax.broadcasted_iota(jnp.int32, (rows, 1), 0) < length_ref[0]


def store_wide(ref, value):
    groups, _, width = ref.shape
    inside = value.shape[1]
    ref[:, :, :inside] = value.reshape(groups, STEP, inside)
    ref[:, :, inside:] = value[:, 2 * inside - width :].reshape(groups, STEP, width - inside)


def load_narrow(ref, inside):
    groups, _, width = ref.shape
    edge = 2 * inside - width
    value = ref[...].reshape(groups * STEP, width)
    return jnp.concatenate([value[:, :edge], value[:, edge:inside] + value[:, inside:]], axis=1)


def store_spread(entry_ref, read_ref, selected):
    turned = selected.T
    for t in range(selected.shape[0]):
        entry_ref[t] = jnp.broadcast_to(turned[R : R + NS, t : t + 1], (NS, LANES))
        read_ref[t] = jnp.broadcast_to(turned[R + NS : R + 2 * NS, t : t + 1], (NS, LANES))


def step_sizes(selected, weight_ref, bias_ref, live):
    low = selected.astype(jnp.bfloat16)
    pre = dot(low, weight_ref[...]) + bias_ref[...]
    soft = jnp.maximum(pre, 0.0) + jnp.log1p(jnp.exp(-jnp.abs(pre)))
    return low, pre, jnp.where(live, soft, 0.0)


def mixer_kernel(
    tiles, share, me_ref, length_ref, selected_ref, conv_ref, gate_ref, weight_ref, bias_ref, skip_ref, rate_ref, project_ref,
    state_ref, end_ref, mixed_out, gated_out, held_out, given_out,
    dt_ref, dx_ref, entry_ref, read_ref, out_ref, held,
):
    chunk, inside = conv_ref.shape
    step = pl.program_id(0)

    @pl.when(step == 0)
    def start():
        held[...] = jnp.zeros_like(held)

    selected, conv = (selected_ref[...], conv_ref[...])
    live = live_slots(step * chunk, length_ref, chunk)
    _, _, size = step_sizes(selected, weight_ref, bias_ref, live)
    store_wide(dt_ref, size)
    store_wide(dx_ref, size * conv)
    store_spread(entry_ref, read_ref, selected)
    scan_forward_chunk(tiles, dt_ref, dx_ref, entry_ref, read_ref, rate_ref, out_ref, state_ref, end_ref, held)
    mixed = load_narrow(out_ref, inside) + skip_ref[...] * conv
    mixed_out[...] = mixed
    gated = (mixed * to_power(gate_ref[...])).astype(jnp.bfloat16)
    gated_out[...] = gated
    part = dot(gated, project_ref[...])
    block = step // share
    rows = pl.ds(pl.multiple_of((step % share) * chunk, chunk), chunk)

    @pl.when(block % 2 == me_ref[0] % 2)
    def keep():
        held_out[0, rows] = part

    @pl.when(block % 2 != me_ref[0] % 2)
    def give():
        given_out[0, rows] = part.astype(jnp.bfloat16)


def mixer(me, length, selected, conv_out, zgate, step_wide, bias, skip, rate, out_weight, span, tiles):
    total, inside = conv_out.shape
    width = out_weight.shape[1]
    count = 2 * tiles + 1
    chunk = CHUNK
    wide = (tiles + 1) * LANES
    share = span // chunk
    smem, vmem = (pl.BlockSpec(memory_space=pltpu.SMEM), pl.BlockSpec(memory_space=pltpu.VMEM))
    row = pl.BlockSpec((chunk, inside), lambda i: (i, 0))
    part = pl.BlockSpec((1, span, width), lambda i: (i // (2 * share), 0, 0))
    f32, bf16 = (jnp.float32, jnp.bfloat16)
    return pl.pallas_call(
        functools.partial(mixer_kernel, tiles, share),
        grid=(total // chunk,),
        in_specs=[smem, smem, pl.BlockSpec((chunk, LANES), lambda i: (i, 0)), row, row] + [vmem] * 5,
        out_specs=[pl.BlockSpec((chunk, count, 8, LANES), lambda i: (i, 0, 0, 0)), vmem, row, row, part, part],
        out_shape=[
            jax.ShapeDtypeStruct((total, count, 8, LANES), f32),
            jax.ShapeDtypeStruct((count, 8, LANES), f32),
            jax.ShapeDtypeStruct((total, inside), f32),
            jax.ShapeDtypeStruct((total, inside), bf16),
            jax.ShapeDtypeStruct((2, span, width), f32),
            jax.ShapeDtypeStruct((2, span, width), bf16),
        ],
        scratch_shapes=[pltpu.VMEM((chunk // STEP, STEP, wide), f32)] * 2
        + [pltpu.VMEM((chunk, NS, LANES), f32)] * 2
        + [pltpu.VMEM((chunk // STEP, STEP, wide), f32), pltpu.VMEM((count, 8, LANES), f32)],
        compiler_params=pltpu.CompilerParams(vmem_limit_bytes=40 * 2**20),
        name="mixer",
    )(me, length, selected, conv_out, zgate, step_wide, bias, skip, rate, out_weight)


def row_sums(value):
    high, low = split_low(value)
    ones = jnp.ones((8, LANES), jnp.bfloat16)
    return dot_t(ones, high) + dot_t(ones, low)


def mixer_back_kernel(
    tiles, share, me_ref, length_ref, *rest,
):
    grad_refs, rest = (rest[:4], rest[4:])
    (
        selected_ref, conv_ref, gate_ref, mixed_ref, gated_ref, state_ref, end_ref, weight_ref, bias_ref, skip_ref, rate_ref, project_ref,
        gate_out, conv_out, rank_out, entry_sum_out, read_sum_out, step_out, bias_out, skip_out, rate_out, project_out,
        grads, dt_ref, dx_ref, mix_ref, entry_ref, read_ref, fed_ref, rise_ref, entry_parts, read_parts, flow, after, total, sems,
    ) = rest
    chunk, inside = conv_ref.shape
    span = grad_refs[0].shape[0]
    index = pl.program_id(0)
    step = pl.num_programs(0) - 1 - index

    @pl.when(index == 0)
    def start():
        copies = []
        for k in range(4):
            at = pl.ds(pl.multiple_of((me_ref[0] ^ k) * span, 16), span)
            copies.append(pltpu.make_async_copy(grad_refs[k], grads.at[at], sems.at[k]))
            copies[-1].start()
        flow[...] = jnp.zeros_like(flow)
        after[...] = end_ref[...]
        rate_out[...] = jnp.zeros_like(rate_out)
        step_out[...] = jnp.zeros_like(step_out)
        bias_out[...] = jnp.zeros_like(bias_out)
        skip_out[...] = jnp.zeros_like(skip_out)
        total[...] = jnp.zeros_like(total)
        for copy in copies:
            copy.wait()

    rows = pl.ds(pl.multiple_of(step * chunk, chunk), chunk)
    grad_gated = dot_t(grads[rows], project_ref[...])
    gate, mixed, conv = (gate_ref[...], mixed_ref[...], conv_ref[...])
    curve = 1.0 / (1.0 + jnp.exp(-gate))
    grad_mixed = grad_gated * (gate * curve)
    gate_out[...] = (grad_gated * mixed * (curve * (1.0 + gate * (1.0 - curve)))).astype(jnp.bfloat16)
    skip_out[...] += jnp.sum(grad_mixed * conv, axis=0, keepdims=True)
    selected = selected_ref[...]
    live = live_slots(step * chunk, length_ref, chunk)
    low, pre, size = step_sizes(selected, weight_ref, bias_ref, live)
    store_wide(dt_ref, size)
    store_wide(dx_ref, size * conv)
    store_wide(mix_ref, grad_mixed)
    store_spread(entry_ref, read_ref, selected)
    scan_backward_chunk(
        tiles, dt_ref, dx_ref, mix_ref, entry_ref, read_ref, rate_ref, state_ref,
        fed_ref, rise_ref, entry_parts, read_parts, rate_out, flow, after,
    )
    fed = load_narrow(fed_ref, inside)
    grad_size = load_narrow(rise_ref, inside) * (1.0 / LOG2E) + fed * conv
    grad_pre = jnp.where(live, grad_size / (1.0 + jnp.exp(-pre)), 0.0)
    bias_out[...] += jnp.sum(grad_pre, axis=0, keepdims=True)
    grad_low = grad_pre.astype(jnp.bfloat16)
    rank_out[...] = dot_t(grad_low, weight_ref[...])
    step_out[...] += t_dot(low, grad_low)
    conv_out[...] = fed * size + skip_ref[...] * grad_mixed
    entry_sum_out[0] = row_sums(entry_parts[...].reshape(chunk * NS, LANES))
    read_sum_out[0] = row_sums(read_parts[...].reshape(chunk * NS, LANES))

    @pl.when(step % share == 0)
    def weigh():
        block = pl.ds(pl.multiple_of(step * chunk, span), span)
        total[...] += t_dot(grads[block], gated_ref[...])

    @pl.when(step == 0)
    def finish():
        project_out[...] = total[...].astype(jnp.bfloat16)


def mixer_back(me, length, grad_pieces, selected, conv_out, zgate, mixed, gated, states, end, step_wide, bias, skip, rate, out_weight, tiles):
    total, inside = conv_out.shape
    span, width = grad_pieces[0].shape
    count = 2 * tiles + 1
    chunk = CHUNK
    steps = total // chunk
    wide = (tiles + 1) * LANES
    share = span // chunk
    smem, vmem = (pl.BlockSpec(memory_space=pltpu.SMEM), pl.BlockSpec(memory_space=pltpu.VMEM))
    anywhere = pl.BlockSpec(memory_space=pl.ANY)
    row = pl.BlockSpec((chunk, inside), lambda i: (steps - 1 - i, 0))
    lane = pl.BlockSpec((chunk, LANES), lambda i: (steps - 1 - i, 0))
    sums = pl.BlockSpec((1, 8, chunk * NS), lambda i: (steps - 1 - i, 0, 0))
    f32, bf16 = (jnp.float32, jnp.bfloat16)
    one = jax.ShapeDtypeStruct((1, inside), f32)
    summed = jax.ShapeDtypeStruct((steps, 8, chunk * NS), f32)
    return pl.pallas_call(
        functools.partial(mixer_back_kernel, tiles, share),
        grid=(steps,),
        in_specs=[smem, smem]
        + [anywhere] * 4
        + [lane, row, row, row]
        + [pl.BlockSpec((span, inside), lambda i: ((steps - 1 - i) // share, 0))]
        + [pl.BlockSpec((chunk, count, 8, LANES), lambda i: (steps - 1 - i, 0, 0, 0))]
        + [vmem] * 6,
        out_specs=[row, row, lane, sums, sums] + [vmem] * 5,
        out_shape=[
            jax.ShapeDtypeStruct((total, inside), bf16),
            jax.ShapeDtypeStruct((total, inside), f32),
            jax.ShapeDtypeStruct((total, LANES), f32),
            summed,
            summed,
            jax.ShapeDtypeStruct((LANES, inside), f32),
            one,
            one,
            jax.ShapeDtypeStruct((count, 8, LANES), f32),
            jax.ShapeDtypeStruct((width, inside), bf16),
        ],
        scratch_shapes=[pltpu.VMEM((total, width), bf16)]
        + [pltpu.VMEM((chunk // STEP, STEP, wide), f32)] * 3
        + [pltpu.VMEM((chunk, NS, LANES), f32)] * 2
        + [pltpu.VMEM((chunk // STEP, STEP, wide), f32)] * 2
        + [pltpu.VMEM((chunk, NS, LANES), f32)] * 2
        + [pltpu.VMEM((count, 8, LANES), f32)] * 2
        + [pltpu.VMEM((width, inside), f32), pltpu.SemaphoreType.DMA((4,))],
        compiler_params=pltpu.CompilerParams(vmem_limit_bytes=48 * 2**20),
        name="mixer_back",
    )(me, length, *grad_pieces, selected, conv_out, zgate, mixed, gated, states, end, step_wide, bias, skip, rate, out_weight)


def project_back_kernel(parts, me_ref, source_ref, length_ref, *rest):
    normed_refs, weight_refs, rest = (rest[:parts], rest[parts : 2 * parts], rest[2 * parts :])
    (
        selected_ref, conv_ref, summed_ref, inner_ref, gate_ref, low_ref, taps_ref, select_ref,
        held_out, given_out, inner_held, inner_given, gate_held, gate_given, select_out, taps_out, bias_out, gain_out,
        normed, weight, shifted, projected, total, sems,
    ) = rest
    index = pl.program_id(0)
    block = parts - 1 - index
    rows, inside = inner_ref.shape
    slab = weight_refs[0].shape[0]
    me = me_ref[0]
    odd = source_ref[parts]

    @pl.when(index == 0)
    def fetch():
        copies = []
        for k in range(parts):
            at = pl.ds(pl.multiple_of(source_ref[k] * slab, 16), slab)
            copies.append(pltpu.make_async_copy(weight_refs[k], weight.at[at], sems.at[k]))
            at = pl.ds(pl.multiple_of((me ^ k) * rows, 16), rows)
            copies.append(pltpu.make_async_copy(normed_refs[k], normed.at[at], sems.at[parts + k]))
        for copy in copies:
            copy.start()
        shifted[rows:] = jnp.zeros((8, inside), jnp.float32)
        total[...] = jnp.zeros_like(total)
        select_out[...] = jnp.zeros_like(select_out)
        taps_out[...] = jnp.zeros_like(taps_out)
        bias_out[...] = jnp.zeros_like(bias_out)
        gain_out[...] = jnp.zeros_like(gain_out)
        for copy in copies:
            copy.wait()

    selected = selected_ref[...]
    summed = summed_ref[...]
    curve = 1.0 / (1.0 + jnp.exp(-summed))
    grad_summed = (conv_ref[...] + dot_t(selected, select_ref[...])) * (curve * (1.0 + summed * (1.0 - curve)))
    select_out[...] += t_dot(selected, low_ref[...])
    bias_out[...] += jnp.sum(grad_summed, axis=0, keepdims=True)
    shifted[:rows] = grad_summed
    inner = inner_ref[...]
    grad_inner = jnp.zeros((rows, inside), jnp.float32)
    for k in range(KW):
        moved = shifted[KW - 1 - k : KW - 1 - k + rows]
        grad_inner = grad_inner + taps_ref[k : k + 1] * moved
        taps_out[k : k + 1] += jnp.sum(inner * moved, axis=0, keepdims=True)
    shifted[rows:] = shifted[0:8]
    live = live_slots(block * rows, length_ref, rows)
    projected[:, :inside] = jnp.where(live, grad_inner, 0.0).astype(jnp.bfloat16)
    projected[:, inside:] = gate_ref[...]
    normed_rows = normed[pl.ds(pl.multiple_of(block * rows, rows), rows)]
    grad_normed = dot_t(projected[...], weight[...])
    gain_out[...] += jnp.sum(grad_normed * normed_rows.astype(jnp.float32), axis=0, keepdims=True)
    total[...] += t_dot(normed_rows, projected[...])

    @pl.when(block % 2 == me % 2)
    def keep():
        held_out[0] = grad_normed

    @pl.when(block % 2 != me % 2)
    def give():
        given_out[0] = grad_normed.astype(jnp.bfloat16)

    @pl.when(block == 0)
    def finish():
        for h in range(parts // 2):
            at = pl.ds(pl.multiple_of((2 * h + odd) * slab, 16), slab)
            inner_held[h] = total[at, :inside]
            gate_held[h] = total[at, inside:]
            at = pl.ds(pl.multiple_of((2 * h + 1 - odd) * slab, 16), slab)
            inner_given[h] = total[at, :inside].astype(jnp.bfloat16)
            gate_given[h] = total[at, inside:].astype(jnp.bfloat16)


def project_back(me, source, length, normed_pieces, weight_pieces, grad_selected, conv_grad, summed, inner, gate_grad, conv_low, taps, select_wide):
    parts = len(normed_pieces)
    rows, width = normed_pieces[0].shape
    slab, both = weight_pieces[0].shape
    total, inside = inner.shape
    smem, anywhere = (pl.BlockSpec(memory_space=pltpu.SMEM), pl.BlockSpec(memory_space=pl.ANY))
    vmem = pl.BlockSpec(memory_space=pltpu.VMEM)
    row = pl.BlockSpec((rows, inside), lambda i: (parts - 1 - i, 0))
    part = pl.BlockSpec((1, rows, width), lambda i: ((parts - 1 - i) // 2, 0, 0))
    f32, bf16 = (jnp.float32, jnp.bfloat16)
    return pl.pallas_call(
        functools.partial(project_back_kernel, parts),
        grid=(parts,),
        in_specs=[smem] * 3
        + [anywhere] * (2 * parts)
        + [pl.BlockSpec((rows, LANES), lambda i: (parts - 1 - i, 0))]
        + [row] * 5
        + [vmem] * 2,
        out_specs=[part, part] + [vmem] * 8,
        out_shape=[
            jax.ShapeDtypeStruct((2, rows, width), f32),
            jax.ShapeDtypeStruct((2, rows, width), bf16),
            jax.ShapeDtypeStruct((2, slab, inside), f32),
            jax.ShapeDtypeStruct((2, slab, inside), bf16),
            jax.ShapeDtypeStruct((2, slab, inside), f32),
            jax.ShapeDtypeStruct((2, slab, inside), bf16),
            jax.ShapeDtypeStruct((LANES, inside), f32),
            jax.ShapeDtypeStruct((8, inside), f32),
            jax.ShapeDtypeStruct((1, inside), f32),
            jax.ShapeDtypeStruct((1, width), f32),
        ],
        scratch_shapes=[
            pltpu.VMEM((total, width), bf16),
            pltpu.VMEM((slab * parts, both), bf16),
            pltpu.VMEM((rows + 8, inside), f32),
            pltpu.VMEM((rows, both), bf16),
            pltpu.VMEM((slab * parts, both), f32),
            pltpu.SemaphoreType.DMA((2 * parts,)),
        ],
        compiler_params=pltpu.CompilerParams(vmem_limit_bytes=56 * 2**20),
        name="project_back",
    )(me, source, length, *normed_pieces, *weight_pieces, grad_selected, conv_grad, summed, inner, gate_grad, conv_low, taps, select_wide)


def norm_kernel(parts, me_ref, tokens_ref, *rest):
    small_refs, normed_out, gains_out = (rest[:parts], rest[parts], rest[parts + 1])
    slab = small_refs[0].shape[1]
    for m in range(parts):

        @pl.when(me_ref[0] == m)
        def lay():
            for p in range(parts):
                gains_out[:, p * slab : (p + 1) * slab] = small_refs[p ^ m][...]

    tokens = tokens_ref[...]
    scale = lax.rsqrt(jnp.mean(tokens * tokens, axis=-1, keepdims=True) + EPSILON)
    normed_out[...] = (tokens * scale * gains_out[2:3]).astype(jnp.bfloat16)


def norm_rows(me, tokens, small_pieces):
    parts = len(small_pieces)
    smem, vmem = (pl.BlockSpec(memory_space=pltpu.SMEM), pl.BlockSpec(memory_space=pltpu.VMEM))
    return pl.pallas_call(
        functools.partial(norm_kernel, parts),
        in_specs=[smem] + [vmem] * (1 + parts),
        out_specs=[vmem] * 2,
        out_shape=[
            jax.ShapeDtypeStruct(tokens.shape, jnp.bfloat16),
            jax.ShapeDtypeStruct((small_pieces[0].shape[0], tokens.shape[1]), jnp.float32),
        ],
        compiler_params=pltpu.CompilerParams(vmem_limit_bytes=16 * 2**20),
        name="norm_rows",
    )(me, tokens, *small_pieces)


def route_kernel(
    me_ref, length_ref, tokens_ref, near_ref, got_ref, gains_ref, order_ref, routes_ref,
    first_out, normed_out, sent_out, probs_out,
):
    rows, width = tokens_ref.shape
    first = tokens_ref[...] + near_ref[...] + got_ref[...].astype(jnp.float32)
    first_out[...] = first
    scale = lax.rsqrt(jnp.mean(first * first, axis=-1, keepdims=True) + EPSILON)
    normed = (first * scale * gains_ref[3:4]).astype(jnp.bfloat16)
    normed_out[...] = normed
    logits = dot_t(normed, router_rows(gains_ref))
    gap = logits[:, 0:1] - logits[:, 1:2]
    prob_zero = 1.0 / (1.0 + jnp.exp(-gap))
    prob_one = 1.0 / (1.0 + jnp.exp(gap))
    lane = lax.broadcasted_iota(jnp.int32, (rows, LANES), 1)
    probs_out[...] = jnp.where(lane == 0, prob_zero, jnp.where(lane == 1, prob_one, 0.0))
    gate = jnp.where(routes_ref[...] == 0, prob_zero, prob_one)
    gate = jnp.where(live_rows(me_ref, length_ref, rows), gate, 0.0)
    high, low = split_low(gate)
    high, low = (high.astype(jnp.float32), low.astype(jnp.float32))
    gates = jnp.where(lane == 0, high, jnp.where(lane == 1, low, 0.0)).astype(jnp.bfloat16)
    sent_out[:, :width] = dot(order_ref[...], normed).astype(jnp.bfloat16)
    sent_out[:, width:] = dot(order_ref[...], gates).astype(jnp.bfloat16)


def route(me, length, tokens, near, got, gains, order, routes):
    rows, width = tokens.shape
    smem, vmem = (pl.BlockSpec(memory_space=pltpu.SMEM), pl.BlockSpec(memory_space=pltpu.VMEM))
    return pl.pallas_call(
        route_kernel,
        in_specs=[smem, smem] + [vmem] * 6,
        out_specs=[vmem] * 4,
        out_shape=[
            jax.ShapeDtypeStruct((rows, width), jnp.float32),
            jax.ShapeDtypeStruct((rows, width), jnp.bfloat16),
            jax.ShapeDtypeStruct((rows, width + LANES), jnp.bfloat16),
            jax.ShapeDtypeStruct((rows, LANES), jnp.float32),
        ],
        compiler_params=pltpu.CompilerParams(vmem_limit_bytes=32 * 2**20),
        name="route",
    )(me, length, tokens, near, got, gains, order, routes)


def expert_kernel(parts, cap, steps, pair, me_ref, source_ref, counts_ref, *rest):
    sent_refs, cot_refs, up_refs = (rest[:parts], rest[parts : 2 * parts], rest[2 * parts : 3 * parts])
    (
        down_ref, grad_held, grad_given, out_held, out_given, up_held, up_given, down_held, down_given,
    ) = rest[3 * parts : 3 * parts + 9]
    rows, cots, up, down, rows_t, cots_t, scale, dots, grad_sum, out_sum, product, sems = rest[3 * parts + 9 :]
    step = pl.program_id(0)
    expert, tile = (step // steps, step % steps)
    span, width = cots.shape[1:]
    slab = up_refs[0].shape[1]
    offset = span - cap
    count = parts * cap
    me = me_ref[0]

    @pl.when(step == 0)
    def fetch():
        copies = [pltpu.make_async_copy(down_ref, down, sems.at[0])]
        for k in range(parts):
            copies.append(pltpu.make_async_copy(sent_refs[k], rows.at[me ^ k], sems.at[1 + k]))
            copies.append(pltpu.make_async_copy(cot_refs[k], cots.at[me ^ k], sems.at[1 + parts + k]))
            at = pl.ds(pl.multiple_of(source_ref[k] * slab, 16), slab)
            copies.append(pltpu.make_async_copy(up_refs[k], up.at[:, at], sems.at[1 + 2 * parts + k]))
        for copy in copies:
            copy.start()
        grad_sum[...] = jnp.zeros_like(grad_sum)
        out_sum[...] = jnp.zeros_like(out_sum)
        dots[...] = jnp.zeros_like(dots)
        for copy in copies:
            copy.wait()

    at = pl.ds(pl.multiple_of(expert * offset, 16), cap)
    mine = rows[:, at, :width].reshape(count, width)
    cot = cots[:, at].reshape(count, width)

    @pl.when(tile == 0)
    def turn():
        rows_t[...] = mine.T
        cots_t[...] = cot.T
        slot = lax.broadcasted_iota(jnp.int32, (cap, LANES), 0)
        for b in range(parts):
            gates = rows[b, at, width:].astype(jnp.float32)
            gate = gates[:, 0:1] + gates[:, 1:2]
            first = slot < counts_ref[b]
            later = slot + offset >= counts_ref[b]
            live = jnp.where(expert == 0, first.astype(jnp.float32), later.astype(jnp.float32))
            scale[b * cap : (b + 1) * cap] = live * gate

    columns = pl.ds(pl.multiple_of(tile * FTILE, FTILE), FTILE)
    up_tile = up[expert, :, columns]
    down_tile = down[expert, columns, :]
    weight = scale[...][:, 0:1]
    pre = dot(mine, up_tile)
    grad_hidden = dot_t(cot, down_tile)
    square = pre * pre
    bend = jnp.tanh(0.7978845608028654 * pre * (1.0 + 0.044715 * square))
    rise = 0.5 * (1.0 + bend)
    slope = rise + 0.5 * pre * (1.0 - bend * bend) * (0.7978845608028654 * (1.0 + 0.134145 * square))
    hidden = (weight * (pre * rise)).astype(jnp.bfloat16)
    grad_pre = (weight * slope * grad_hidden).astype(jnp.bfloat16)
    part = jnp.sum(hidden.astype(jnp.float32) * grad_hidden, axis=1, keepdims=True)
    dots[:, at] += jnp.broadcast_to(part, (count, LANES)).reshape(parts, cap, LANES)
    out_sum[:, at] += dot(hidden, down_tile).reshape(parts, cap, width)
    grad_sum[:, at] += dot_t(grad_pre, up_tile).reshape(parts, cap, width)
    odd, second = (source_ref[parts], source_ref[parts + 1])
    product[...] = dot(rows_t[...], grad_pre)
    for h in range(parts // 2):
        at = pl.ds(pl.multiple_of((2 * h + odd) * slab, 16), slab)
        up_held[0, h] = product[at]
        at = pl.ds(pl.multiple_of((2 * h + 1 - odd) * slab, 16), slab)
        up_given[0, h] = product[at].astype(jnp.bfloat16)
    product[...] = dot(cots_t[...], hidden)
    for h in range(width // (2 * pair)):
        at = pl.ds(pl.multiple_of((2 * h + second) * pair, 8), pair)
        down_held[0, h] = product[at]
        at = pl.ds(pl.multiple_of((2 * h + 1 - second) * pair, 8), pair)
        down_given[0, h] = product[at].astype(jnp.bfloat16)

    @pl.when(step == pl.num_programs(0) - 1)
    def finish():
        for b in range(parts):

            @pl.when(me % 2 == b % 2)
            def hold():
                grad_held[b // 2, :, :width] = grad_sum[b]
                grad_held[b // 2, :, width:] = dots[b]
                out_held[b // 2] = out_sum[b]

            @pl.when(me % 2 != b % 2)
            def give():
                grad_given[b // 2, :, :width] = grad_sum[b].astype(jnp.bfloat16)
                grad_given[b // 2, :, width:] = dots[b].astype(jnp.bfloat16)
                out_given[b // 2] = out_sum[b].astype(jnp.bfloat16)


def experts(me, source, counts, sent_pieces, cot_pieces, up_pieces, down_weight, pair):
    parts = len(sent_pieces)
    span, width = cot_pieces[0].shape
    number, hid = down_weight.shape[:2]
    steps = hid // FTILE
    slab = up_pieces[0].shape[1]
    smem, anywhere = (pl.BlockSpec(memory_space=pltpu.SMEM), pl.BlockSpec(memory_space=pl.ANY))
    vmem = pl.BlockSpec(memory_space=pltpu.VMEM)
    f32, bf16 = (jnp.float32, jnp.bfloat16)
    pairs = width // (2 * pair)
    up_block = pl.BlockSpec((1, parts // 2, slab, FTILE), lambda i: (i // steps, 0, 0, i % steps))
    down_block = pl.BlockSpec((1, pairs, pair, FTILE), lambda i: (i // steps, 0, 0, i % steps))
    up_shape = (number, parts // 2, slab, hid)
    down_shape = (number, pairs, pair, hid)
    count = parts * CAP
    return pl.pallas_call(
        functools.partial(expert_kernel, parts, CAP, steps, pair),
        grid=(number * steps,),
        in_specs=[smem] * 3 + [anywhere] * (3 * parts + 1),
        out_specs=[vmem] * 4 + [up_block] * 2 + [down_block] * 2,
        out_shape=[
            jax.ShapeDtypeStruct((2, span, width + LANES), f32),
            jax.ShapeDtypeStruct((2, span, width + LANES), bf16),
            jax.ShapeDtypeStruct((2, span, width), f32),
            jax.ShapeDtypeStruct((2, span, width), bf16),
            jax.ShapeDtypeStruct(up_shape, f32),
            jax.ShapeDtypeStruct(up_shape, bf16),
            jax.ShapeDtypeStruct(down_shape, f32),
            jax.ShapeDtypeStruct(down_shape, bf16),
        ],
        scratch_shapes=[
            pltpu.VMEM((parts, span, width + LANES), bf16),
            pltpu.VMEM((parts, span, width), bf16),
            pltpu.VMEM((number, slab * parts, hid), bf16),
            pltpu.VMEM((number, hid, width), bf16),
            pltpu.VMEM((width, count), bf16),
            pltpu.VMEM((width, count), bf16),
            pltpu.VMEM((count, LANES), f32),
            pltpu.VMEM((parts, span, LANES), f32),
            pltpu.VMEM((parts, span, width), f32),
            pltpu.VMEM((parts, span, width), f32),
            pltpu.VMEM((width, FTILE), f32),
            pltpu.SemaphoreType.DMA((1 + 3 * parts,)),
        ],
        compiler_params=pltpu.CompilerParams(vmem_limit_bytes=60 * 2**20),
        cost_estimate=pl.CostEstimate(flops=12 * number * count * width * hid, bytes_accessed=24 * 2**20, transcendentals=number * count * hid),
        name="experts",
    )(me, source, counts, *sent_pieces, *cot_pieces, *up_pieces, down_weight)


def return_kernel(
    me_ref, length_ref, near_ref, got_ref, order_ref, normed_ref, probs_ref, routes_ref, first_ref, cot_ref, gains_ref,
    grad_out, low_out, gain_out, router_out,
):
    rows, width = first_ref.shape
    grad = near_ref[...] + got_ref[...].astype(jnp.float32)
    high, low = split_low(grad)
    grad = dot(order_ref[...], high) + dot(order_ref[...], low)
    lane = lax.broadcasted_iota(jnp.int32, (rows, LANES), 1)
    chosen = (lane == routes_ref[...]).astype(jnp.float32)
    grad_logits = (grad[:, width : width + 1] * (chosen - probs_ref[...])).astype(jnp.bfloat16)
    grad_normed = grad[:, :width] + dot(grad_logits[:, :NS], router_rows(gains_ref))
    router_out[...] = t_dot(grad_logits, normed_ref[...])[0:8]
    first = first_ref[...]
    scale = lax.rsqrt(jnp.mean(first * first, axis=-1, keepdims=True) + EPSILON)
    unit = first * scale
    gain_out[...] = jnp.sum(grad_normed * unit, axis=0, keepdims=True)
    pulled = grad_normed * gains_ref[3:4]
    pulled = scale * (pulled - unit * jnp.mean(pulled * unit, axis=-1, keepdims=True))
    total = jnp.where(live_rows(me_ref, length_ref, rows), cot_ref[...], 0.0) + pulled
    grad_out[...] = total
    low_out[...] = total.astype(jnp.bfloat16)


def return_rows(me, length, *operands):
    rows, width = operands[6].shape
    smem, vmem = (pl.BlockSpec(memory_space=pltpu.SMEM), pl.BlockSpec(memory_space=pltpu.VMEM))
    return pl.pallas_call(
        return_kernel,
        in_specs=[smem, smem] + [vmem] * 9,
        out_specs=[vmem] * 4,
        out_shape=[
            jax.ShapeDtypeStruct((rows, width), jnp.float32),
            jax.ShapeDtypeStruct((rows, width), jnp.bfloat16),
            jax.ShapeDtypeStruct((1, width), jnp.float32),
            jax.ShapeDtypeStruct((8, width), jnp.float32),
        ],
        compiler_params=pltpu.CompilerParams(vmem_limit_bytes=32 * 2**20),
        name="return_rows",
    )(me, length, *operands)


def finish_kernel(
    me_ref, length_ref, near_ref, got_ref, out_near_ref, out_got_ref, order_ref, first_ref, grad_ref, tokens_ref, gains_ref,
    result_out, grad_out,
):
    rows = tokens_ref.shape[0]
    grad = near_ref[...] + got_ref[...].astype(jnp.float32)
    tokens = tokens_ref[...]
    scale = lax.rsqrt(jnp.mean(tokens * tokens, axis=-1, keepdims=True) + EPSILON)
    unit = tokens * scale
    pulled = grad * gains_ref[2:3]
    grad_out[...] = grad_ref[...] + scale * (pulled - unit * jnp.mean(pulled * unit, axis=-1, keepdims=True))
    high, low = split_low(out_near_ref[...] + out_got_ref[...].astype(jnp.float32))
    added = dot(order_ref[...], high) + dot(order_ref[...], low)
    result_out[...] = jnp.where(live_rows(me_ref, length_ref, rows), first_ref[...] + added, 0.0)


def finish_rows(me, length, *operands):
    shape = operands[5].shape
    smem, vmem = (pl.BlockSpec(memory_space=pltpu.SMEM), pl.BlockSpec(memory_space=pltpu.VMEM))
    return pl.pallas_call(
        finish_kernel,
        in_specs=[smem, smem] + [vmem] * 9,
        out_specs=[vmem] * 2,
        out_shape=[jax.ShapeDtypeStruct(shape, jnp.float32)] * 2,
        compiler_params=pltpu.CompilerParams(vmem_limit_bytes=32 * 2**20),
        name="finish_rows",
    )(me, length, *operands)


def body(
    tokens,
    routes,
    lengths,
    cotangent,
    in_weight,
    select_weight,
    step_weight,
    out_weight,
    router_weight,
    up_weight,
    down_weight,
    conv_weight,
    conv_bias,
    step_bias,
    decay_log,
    skip_gain,
    mixer_gain,
    expert_gain,
):
    f32, bf16 = (jnp.float32, jnp.bfloat16)
    span, width = tokens.shape
    groups, parts = (lax.axis_size("grp"), lax.axis_size("shard"))
    me, group = (lax.axis_index("shard"), lax.axis_index("grp"))
    total = span * parts
    inside = conv_bias.shape[0]
    tiles = inside // LANES
    slab = in_weight.shape[0]
    hidden_cols = up_weight.shape[2] // parts
    share = width // groups
    bits = [2**i for i in range(groups.bit_length() - 1)]
    down_bit = 2 if share % 8 == 0 else bits[-1]
    pair = 2 * share if share % 8 == 0 else width // 2
    odd, second = (group % 2, (group // down_bit) % 2)
    me_one = jnp.full((1,), me, jnp.int32)
    source = [me, me ^ 1, me ^ (2 + odd), me ^ (3 - odd), odd, second]
    source = jnp.stack(source).astype(jnp.int32)

    first = (routes[:, 0] == 0).astype(jnp.int32)
    count_first = jnp.sum(first)
    small = jnp.concatenate(
        [
            router_weight.astype(f32).T,
            mixer_gain.astype(f32)[None],
            expert_gain.astype(f32)[None],
            jnp.full((1, slab), count_first, jnp.int32).astype(f32),
            jnp.zeros((11, slab), f32),
        ],
        axis=0,
    )
    small = [small] + [swap(small, k) for k in range(1, parts)]
    in_pieces, up_pieces = cut_weights(source[:3], in_weight, up_weight, parts, inside)
    in_pieces = share_pieces(in_pieces)
    normed, gains = norm_rows(me_one, tokens, small)
    normed_pieces = gather_pieces(normed)
    counts = gains[4].reshape(parts, slab)[:, 0].astype(jnp.int32)

    goal = jnp.where(first > 0, jnp.cumsum(first), count_first + jnp.cumsum(1 - first)) - 1
    slots = jnp.arange(span, dtype=jnp.int32)
    order = (slots[:, None] == goal[None, :]).astype(bf16)
    order_t = (goal[:, None] == slots[None, :]).astype(bf16)
    live = (me * span + slots < lengths[0])[:, None]
    cots = matmul(order, jnp.where(live, cotangent, 0.0).astype(bf16)).astype(bf16)
    cot_pieces = gather_pieces(cots)

    taps = conv_weight.astype(f32)
    spare = LANES - select_weight.shape[1]
    select_wide = jnp.pad(select_weight, ((0, 0), (0, spare)))
    inner, zgate, summed, conv_out, conv_low, selected = project(
        me_one,
        source,
        lengths,
        normed_pieces,
        in_pieces,
        taps,
        conv_bias.astype(f32)[None, :],
        select_wide,
    )
    selected = tie(selected + swap(selected, 1), cot_pieces[2])
    selected = selected + swap(selected, 2)
    step_wide = jnp.pad(step_weight, ((0, LANES - R), (0, 0)))
    step_row = step_bias.astype(f32)[None, :]
    decay = -jnp.exp(decay_log.astype(f32))
    rate = pack(decay * LOG2E, tiles)
    skip = skip_gain.astype(f32)[None, :]
    states, end, mixed, gated, held, given = mixer(
        me_one, lengths, selected, conv_out, zgate, step_wide, step_row, skip, rate, out_weight, span, tiles
    )
    up_pieces = share_pieces(up_pieces)
    near, given = scatter_near(held, given, up_pieces[2])
    first_sum, normed_two, sent, probs = route(
        me_one, lengths, tokens, near, swap(given, 2), gains, order, routes
    )
    grad_held, grad_given, out_held, out_given, up_held, up_given, down_held, down_given = experts(
        me_one, source, counts, gather_pieces(sent), cot_pieces, up_pieces, down_weight, pair
    )
    near, given = scatter_near(grad_held, grad_given)
    up_got, down_got = (swap_groups(up_given, 1), swap_groups(down_given, down_bit))
    grad_first, grad_first_low, expert_gain_grad, router_grad = return_rows(
        me_one,
        lengths,
        near,
        swap(given, 2),
        order_t,
        normed_two,
        probs,
        routes,
        first_sum,
        cotangent,
        gains,
    )
    grad_pieces = gather_pieces(grad_first_low)
    out_near, out_given = scatter_near(out_held, out_given)
    out_got = swap(out_given, 2)
    fours, eights = (groups // 4, groups // 8)
    up_sum = join(up_held, up_got, grad_pieces[2]).reshape(E, 2, slab, fours, hidden_cols // fours)
    down_sum = join(down_held, down_got, grad_pieces[2])
    down_sum = down_sum.reshape(E, groups // 4, 2, share, hidden_cols)
    up_held, up_given = halve(up_sum, 1, 2)
    down_held, down_given = halve(down_sum, 2, 1)
    up_got, down_got = (swap_groups(up_given, 2), swap_groups(down_given, 1))

    (
        grad_zgate,
        conv_part,
        rank_part,
        entry_part,
        read_part,
        step_grad,
        step_bias_grad,
        skip_grad,
        rate_grad,
        out_grad,
    ) = mixer_back(
        me_one,
        lengths,
        grad_pieces,
        selected,
        conv_out,
        zgate,
        mixed,
        gated,
        states,
        end,
        step_wide,
        step_row,
        skip,
        rate,
        out_weight,
        tiles,
    )
    grad_selected = jnp.concatenate(
        [
            rank_part[:, :R],
            entry_part[:, 0].reshape(total, NS),
            read_part[:, 0].reshape(total, NS),
            jnp.zeros((total, spare), f32),
        ],
        axis=1,
    )
    grad_selected = tie(grad_selected + swap(grad_selected, 1), out_got)
    grad_selected = (grad_selected + swap(grad_selected, 2)).astype(bf16)
    up_sum = join(up_held, up_got, rank_part)
    down_sum = join(down_held, down_got, rank_part)
    up_held, up_given = halve(up_sum, 3, 4)
    down_bits = [bit for bit in bits[1:] if bit != down_bit]
    down_held, down_given = halve(down_sum, 1, down_bits[0])
    up_got, down_got = (swap_groups(up_given, 4), swap_groups(down_given, down_bits[0]))
    (
        held,
        given,
        inner_held,
        inner_given,
        gate_held,
        gate_given,
        select_grad,
        conv_grad,
        conv_bias_grad,
        mixer_part,
    ) = project_back(
        me_one,
        source,
        lengths,
        normed_pieces,
        in_pieces,
        grad_selected,
        conv_part,
        summed,
        inner,
        grad_zgate,
        conv_low,
        taps,
        select_wide,
    )
    near, given = scatter_near(held, given)
    result, tokens_grad = finish_rows(
        me_one,
        lengths,
        near,
        swap(given, 2),
        out_near,
        out_got,
        order_t,
        first_sum,
        grad_first,
        tokens,
        gains,
    )

    in_cols = inside // eights
    in_sum = jnp.stack(
        [join(inner_held, swap_groups(inner_given, 1)), join(gate_held, swap_groups(gate_given, 1))], axis=2
    )
    in_sum = in_sum.reshape(2, slab, 2, eights, in_cols)
    in_sum = sum_rest(in_sum, [(0, 2)] + [(3, bit) for bit in bits[2:-1]] + [(2, bits[-1])])
    in_sum = in_sum.reshape(slab, in_cols)
    up_sum = sum_rest(join(up_held, up_got, mixer_part), [(3, bit) for bit in bits[3:]])
    down_sum = sum_rest(join(down_held, down_got, mixer_part), [(1, bit) for bit in down_bits[1:]])
    down_sum = down_sum.reshape(E, share, hidden_cols)
    out_sum = sum_rest(out_grad.reshape(groups, share, inside), [(0, bit) for bit in bits])[0]
    up_moves, in_moves = ([], [])
    for g in range(groups):
        for s in range(parts):
            up_moves.append((g * parts + s, (s * fours + g // 4) * parts + g % 4))
            half, k = (g // (groups // 2), (g // 4) % eights)
            in_moves.append((g * parts + s, (half * (groups // 2) + s * eights + k) * parts + g % 4))
    both_axes = ("grp", "shard")
    up_cols = hidden_cols // fours
    up_sum = lax.ppermute(up_sum.reshape(E, slab, up_cols).astype(bf16), both_axes, up_moves)
    in_sum = lax.ppermute(in_sum.astype(bf16), both_axes, in_moves)

    decay_grad = decay * unpack(rate_grad, tiles)
    early = jnp.concatenate([step_grad[:R], decay_grad, step_bias_grad, skip_grad], axis=0)
    early = total_groups(early)
    shared = jnp.concatenate([router_grad[0:E], expert_gain_grad, mixer_part / gains[2:3]], axis=0)
    shared = shared + swap(shared, 1)
    shared = shared + swap(shared, 2)
    shared = lax.dynamic_slice_in_dim(shared, me * slab, slab, 1)
    picked = select_weight.shape[1]
    late = jnp.concatenate(
        [select_grad[:picked], conv_grad[:KW], conv_bias_grad, shared.reshape(2, inside)], axis=0
    )
    late = total_groups(late)
    shared = late[picked + KW + 1 :].reshape(4, slab)
    return (
        result,
        tokens_grad,
        in_sum.astype(f32),
        out_sum.T,
        up_sum.astype(f32),
        down_sum.transpose(0, 2, 1),
        late[:picked].T,
        early[:R],
        shared[0:2].T,
        late[picked : picked + KW],
        late[picked + KW],
        early[R + NS],
        early[R : R + NS],
        early[R + NS + 1],
        shared[3],
        shared[2],
    )


def solution(mesh):
    return jax.shard_map(
        body,
        mesh=mesh,
        in_specs=(
            P(("grp", "shard"), None),
            P(("grp", "shard"), None),
            P("grp"),
            P(("grp", "shard"), None),
            P("shard", None),
            P("shard", None),
            P(None, "shard"),
            P("shard", None),
            P("shard", None),
            P(None, "shard", None),
            P(None, "shard", None),
            P(None, "shard"),
            P("shard"),
            P("shard"),
            P(None, "shard"),
            P("shard"),
            P("shard"),
            P("shard"),
        ),
        out_specs=(
            P(("grp", "shard"), None),
            P(("grp", "shard"), None),
            P("shard", "grp"),
            P("shard", "grp"),
            P(None, "shard", "grp"),
            P(None, "shard", "grp"),
            P("shard", None),
            P(None, "shard"),
            P("shard", None),
            P(None, "shard"),
            P("shard"),
            P("shard"),
            P(None, "shard"),
            P("shard"),
            P("shard"),
            P("shard"),
        ),
        check_vma=False,
    )
```

```python
import functools
import jax
import jax.numpy as jnp
from jax import lax
from jax.experimental import pallas as pl
from jax.experimental.pallas import tpu as pltpu
from jax.sharding import PartitionSpec as P

R = 72
KW = 4
E = 2
CAP = 192
EPSILON = 1e-05
FTILE = 256
LOG2E = 1.4426950408889634

NS = 16
LANES = 128
STEP = 8
CHUNK = 64


def swap(value, bit):
    size = lax.axis_size("shard")
    return lax.ppermute(value, "shard", [(i, i ^ bit) for i in range(size)])


def swap_groups(value, bit):
    size = lax.axis_size("grp")
    return lax.ppermute(value, "grp", [(g, g ^ bit) for g in range(size)])


def tie(value, *others):
    for other in others:
        corner = other[(0,) * other.ndim].astype(jnp.float32)
        value = value + (0.0 * corner).astype(value.dtype)
    return value


def gather_pieces(value):
    far = swap(value, 2)
    return (value, swap(value, 1), far, swap(far, 1))


def scatter_near(held, given, *others):
    side = lax.axis_index("shard") // 2
    held = tie(held + swap(given, 1).astype(jnp.float32), *others)
    mine = lax.dynamic_index_in_dim(held, side, 0, False)
    return mine, lax.dynamic_index_in_dim(held, 1 - side, 0, False).astype(jnp.bfloat16)


def halve(value, axis, bit, *others):
    mine = (lax.axis_index("grp") // bit) % 2
    terms = value if isinstance(value, tuple) else (value,)
    size = terms[0].shape[axis] // 2

    def side(index):
        picked = [lax.dynamic_slice_in_dim(term, index * size, size, axis) for term in terms]
        total = picked[0].astype(jnp.float32)
        for term in picked[1:]:
            total = total + term.astype(jnp.float32)
        return tie(total, *others)

    return side(mine), side(1 - mine).astype(jnp.bfloat16)


def join(held, got, *others):
    return tie(held.astype(jnp.float32) + got.astype(jnp.float32), *others)


def share_pieces(pieces):
    groups, parts = (lax.axis_size("grp"), lax.axis_size("shard"))
    moves = [
        (g * parts + s, g * parts + (s ^ (2 + g % 2))) for g in range(groups) for s in range(parts)
    ]
    crossed = lax.ppermute(pieces[2], ("grp", "shard"), moves)
    shared = lax.ppermute(crossed, "grp", [(g, g ^ 1) for g in range(groups)])
    return [pieces[0], swap(pieces[1], 1), crossed, shared]


def exchange(value, bits):
    return [value] + [swap_groups(value, sum(bits[i] for i in range(len(bits)) if k >> i & 1)) for k in range(1, 2 ** len(bits))]


def balanced(terms, *others):
    terms = [term.astype(jnp.float32) for term in terms]
    while len(terms) > 1:
        terms = [terms[i] + terms[i + 1] for i in range(0, len(terms), 2)]
    return tie(terms[0], *others)


def total_rest(value, bits, kind=jnp.bfloat16):
    for bit in bits:
        value = balanced(exchange(value.astype(kind), [bit]))
    return value


def matmul(left, right):
    return jnp.dot(left, right, preferred_element_type=jnp.float32)


def pack(value, tiles):
    edge = tiles * LANES
    full = value[:, :edge].reshape(2, 8, tiles, LANES).transpose(2, 0, 1, 3)
    rest = jnp.concatenate([value[:8, edge:], value[8:, edge:]], axis=1)
    return jnp.concatenate([full.reshape(2 * tiles, 8, LANES), rest[None]], axis=0)


def unpack(value, tiles):
    full = value[: 2 * tiles].reshape(tiles, 2, 8, LANES).transpose(1, 2, 0, 3)
    rest = value[2 * tiles]
    rest = jnp.concatenate([rest[:, : LANES // 2], rest[:, LANES // 2 :]], axis=0)
    return jnp.concatenate([full.reshape(NS, tiles * LANES), rest], axis=1)


def fold_rows(parts):
    row = lax.broadcasted_iota(jnp.int32, (8, LANES), 0)
    top, pair, even = (row < 4, (row & 2) == 0, (row & 1) == 0)
    fours = [
        jnp.where(top, parts[i], parts[i + 4])
        + pltpu.roll(jnp.where(top, parts[i + 4], parts[i]), 4, 0)
        for i in range(4)
    ]
    twos = [
        jnp.where(
            pair,
            fours[i] + pltpu.roll(fours[i], 6, 0),
            fours[i + 2] + pltpu.roll(fours[i + 2], 2, 0),
        )
        for i in range(2)
    ]
    return jnp.where(
        even, twos[0] + pltpu.roll(twos[0], 7, 0), twos[1] + pltpu.roll(twos[1], 1, 0)
    )


def halves(pair_ref, at, left):
    low, high = (pair_ref[at, 0:8], pair_ref[at, 8:16])
    return (low, high, jnp.where(left, low, high))


def scan_forward_chunk(tiles, dt_ref, dx_ref, entry_ref, read_ref, rate_ref, out_ref, state_ref, end_ref, held):
    left = lax.broadcasted_iota(jnp.int32, (8, LANES), 1) < LANES // 2

    def group(g, states):
        at, base = (g, g * STEP)
        states = list(states)
        entry = [halves(entry_ref, base + t, left) for t in range(STEP)]
        read = [halves(read_ref, base + t, left) for t in range(STEP)]
        for tile in range(tiles + 1):
            columns = slice(tile * LANES, (tile + 1) * LANES)
            rows = [2 * tile] if tile == tiles else [2 * tile, 2 * tile + 1]
            which = [2] if tile == tiles else [0, 1]
            sums = []
            for t in range(STEP):
                step = dt_ref[at, t : t + 1, columns]
                fed = dx_ref[at, t : t + 1, columns]
                total = None
                for r, w in zip(rows, which):
                    state_ref[base + t, r] = states[r]
                    states[r] = jnp.exp2(step * rate_ref[r]) * states[r] + entry[t][w] * fed
                    term = read[t][w] * states[r]
                    total = term if total is None else total + term
                sums.append(total)
            out_ref[at, :, columns] = fold_rows(sums)
        return tuple(states)

    count = 2 * tiles + 1
    states = lax.fori_loop(0, dt_ref.shape[0], group, tuple(held[r] for r in range(count)))
    for r in range(count):
        held[r] = states[r]
        end_ref[r] = states[r]


def scan_backward_chunk(
    tiles, dt_ref, dx_ref, grad_ref, entry_ref, read_ref, rate_ref, state_ref,
    fed_out, step_out, entry_out, read_out, rate_out, flow, after,
):
    count = 2 * tiles + 1
    left = lax.broadcasted_iota(jnp.int32, (8, LANES), 1) < LANES // 2
    groups = dt_ref.shape[0]

    def group(g, carry):
        at = groups - 1 - g
        base = at * STEP
        flows, afters = (list(carry[0]), list(carry[1]))
        entry = [halves(entry_ref, base + t, left) for t in range(STEP)]
        read = [halves(read_ref, base + t, left) for t in range(STEP)]
        entry_sum = [[None, None] for _ in range(STEP)]
        read_sum = [[None, None] for _ in range(STEP)]
        for tile in range(tiles + 1):
            last = tile == tiles
            columns = slice(tile * LANES, (tile + 1) * LANES)
            rows = [2 * tile] if last else [2 * tile, 2 * tile + 1]
            which = [2] if last else [0, 1]
            fed_sums, step_sums = ([None] * STEP, [None] * STEP)
            rate_sum = [rate_out[r] for r in rows]
            for t in reversed(range(STEP)):
                step = dt_ref[at, t : t + 1, columns]
                fed = dx_ref[at, t : t + 1, columns]
                grad = grad_ref[at, t : t + 1, columns]
                for i, (r, w) in enumerate(zip(rows, which)):
                    before = state_ref[base + t, r]
                    arriving = flows[r] + read[t][w] * grad
                    entry_term = arriving * fed
                    read_term = afters[r] * grad
                    fed_term = entry[t][w] * arriving
                    leaving = jnp.exp2(step * rate_ref[r]) * arriving
                    product = leaving * before
                    step_term = product * rate_ref[r]
                    rate_sum[i] = rate_sum[i] + product * step
                    flows[r] = leaving
                    afters[r] = before
                    fed_sums[t] = fed_term if i == 0 else fed_sums[t] + fed_term
                    step_sums[t] = step_term if i == 0 else step_sums[t] + step_term
                    for total, term in ((entry_sum[t], entry_term), (read_sum[t], read_term)):
                        if last:
                            total[0] = total[0] + jnp.where(left, term, 0.0)
                            total[1] = total[1] + jnp.where(left, 0.0, term)
                        else:
                            total[i] = term if total[i] is None else total[i] + term
            fed_out[at, :, columns] = fold_rows(fed_sums)
            step_out[at, :, columns] = fold_rows(step_sums)
            for i, r in enumerate(rows):
                rate_out[r] = rate_sum[i]
        for t in range(STEP):
            for i in range(2):
                entry_out[base + STEP - 1 - t, 8 * i : 8 * i + 8] = entry_sum[t][i]
                read_out[base + STEP - 1 - t, 8 * i : 8 * i + 8] = read_sum[t][i]
        return (tuple(flows), tuple(afters))

    flows, afters = lax.fori_loop(
        0,
        groups,
        group,
        (tuple(flow[r] for r in range(count)), tuple(after[r] for r in range(count))),
    )
    for r in range(count):
        flow[r] = flows[r]
        after[r] = afters[r]


def split_low(value):
    high = value.astype(jnp.bfloat16)
    return high, (value - high.astype(jnp.float32)).astype(jnp.bfloat16)


def dot(left, right):
    return jnp.dot(left, right, preferred_element_type=jnp.float32)


def dot_t(left, right):
    return lax.dot_general(left, right, (((1,), (1,)), ((), ())), preferred_element_type=jnp.float32)


def t_dot(left, right):
    return lax.dot_general(left, right, (((0,), (0,)), ((), ())), preferred_element_type=jnp.float32)


def live_rows(me_ref, length_ref, rows):
    slot = me_ref[0] * rows + lax.broadcasted_iota(jnp.int32, (rows, 1), 0)
    return slot < length_ref[0]


def router_rows(gains_ref):
    row = lax.broadcasted_iota(jnp.int32, gains_ref.shape, 0)
    return jnp.where(row < E, gains_ref[...], 0.0).astype(jnp.bfloat16)


def cut_kernel(parts, inside, cols, goal_ref, in_ref, up_ref, *rest):
    number = len(rest) // 2
    in_outs, up_outs, sems = (rest[:number], rest[number : 2 * number], rest[-1])
    copies = []
    for k in range(number):
        columns = pl.ds(pl.multiple_of(goal_ref[k] * cols, LANES), cols)
        copies.append(pltpu.make_async_copy(up_ref.at[:, :, columns], up_outs[k], sems.at[k]))
        copies[-1].start()
    for d in range(parts):
        for k in range(number):

            @pl.when(goal_ref[k] == d)
            def write():
                in_outs[k][:, :inside] = in_ref[:, d * inside : (d + 1) * inside]
                at = (parts + d) * inside
                in_outs[k][:, inside:] = in_ref[:, at : at + inside]

    for copy in copies:
        copy.wait()


def cut_weights(goal, in_weight, up_weight, parts, inside):
    slab = in_weight.shape[0]
    cols = up_weight.shape[2] // parts
    number = 3
    in_shape = jax.ShapeDtypeStruct((slab, 2 * inside), in_weight.dtype)
    up_shape = jax.ShapeDtypeStruct((up_weight.shape[0], slab, cols), up_weight.dtype)
    vmem, anywhere = (pl.BlockSpec(memory_space=pltpu.VMEM), pl.BlockSpec(memory_space=pl.ANY))
    outs = pl.pallas_call(
        functools.partial(cut_kernel, parts, inside, cols),
        in_specs=[pl.BlockSpec(memory_space=pltpu.SMEM), vmem, anywhere],
        out_specs=[vmem] * number + [anywhere] * number,
        out_shape=[in_shape] * number + [up_shape] * number,
        scratch_shapes=[pltpu.SemaphoreType.DMA((number,))],
        compiler_params=pltpu.CompilerParams(vmem_limit_bytes=24 * 2**20),
        name="cut_weights",
    )(goal, in_weight, up_weight)
    return outs[:number], outs[number:]


def to_power(value):
    return value / (1.0 + jnp.exp(-value))


def project_kernel(parts, inside, me_ref, source_ref, length_ref, *rest):
    normed_refs, weight_refs, rest = (rest[:parts], rest[parts : 2 * parts], rest[2 * parts :])
    taps_ref, bias_ref, select_ref, inner_out, gate_out, summed_out, conv_out, low_out, selected_out = rest[:9]
    normed, weight, shifted, sems = rest[9:]
    block = pl.program_id(0)
    me = me_ref[0]
    rows, slab = (normed_refs[0].shape[0], weight_refs[0].shape[0])

    @pl.when(block == 0)
    def fetch():
        copies = []
        for k in range(parts):
            at = pl.ds(pl.multiple_of(source_ref[k] * slab, 16), slab)
            copies.append(pltpu.make_async_copy(weight_refs[k], weight.at[at], sems.at[k]))
            at = pl.ds(pl.multiple_of((me ^ k) * rows, 16), rows)
            copies.append(pltpu.make_async_copy(normed_refs[k], normed.at[at], sems.at[parts + k]))
        for copy in copies:
            copy.start()
        for copy in copies:
            copy.wait()
        shifted[0:8] = jnp.zeros((8, inside), jnp.float32)

    start = pl.multiple_of(block * rows, 16)
    projected = jnp.dot(normed[pl.ds(start, rows)], weight[...], preferred_element_type=jnp.float32)
    slot = block * rows + lax.broadcasted_iota(jnp.int32, (rows, 1), 0)
    inner = jnp.where(slot < length_ref[0], projected[:, :inside], 0.0)
    gate_out[...] = projected[:, inside:]
    inner_out[...] = inner
    shifted[8:] = inner
    summed = bias_ref[...]
    for k in range(KW):
        summed = summed + taps_ref[k : k + 1] * shifted[8 - (KW - 1) + k : 8 - (KW - 1) + k + rows]
    shifted[0:8] = shifted[rows : rows + 8]
    summed_out[...] = summed
    value = to_power(summed)
    conv_out[...] = value
    low = value.astype(jnp.bfloat16)
    low_out[...] = low
    selected_out[...] = jnp.dot(low, select_ref[...], preferred_element_type=jnp.float32)


def project(me, source, length, normed_pieces, weight_pieces, taps, bias, select_wide):
    parts = len(normed_pieces)
    rows, width = normed_pieces[0].shape
    slab, both = weight_pieces[0].shape
    inside, picked = select_wide.shape
    total = rows * parts
    smem, anywhere = (pl.BlockSpec(memory_space=pltpu.SMEM), pl.BlockSpec(memory_space=pl.ANY))
    vmem = pl.BlockSpec(memory_space=pltpu.VMEM)
    row = pl.BlockSpec((rows, inside), lambda i: (i, 0))
    wide = jax.ShapeDtypeStruct((total, inside), jnp.float32)
    return pl.pallas_call(
        functools.partial(project_kernel, parts, inside),
        grid=(parts,),
        in_specs=[smem] * 3 + [anywhere] * (2 * parts) + [vmem] * 3,
        out_specs=[row] * 5 + [pl.BlockSpec((rows, picked), lambda i: (i, 0))],
        out_shape=[wide] * 4
        + [
            jax.ShapeDtypeStruct((total, inside), jnp.bfloat16),
            jax.ShapeDtypeStruct((total, picked), jnp.float32),
        ],
        scratch_shapes=[
            pltpu.VMEM((total, width), jnp.bfloat16),
            pltpu.VMEM((slab * parts, both), jnp.bfloat16),
            pltpu.VMEM((rows + 8, inside), jnp.float32),
            pltpu.SemaphoreType.DMA((2 * parts,)),
        ],
        compiler_params=pltpu.CompilerParams(vmem_limit_bytes=40 * 2**20),
        cost_estimate=pl.CostEstimate(flops=4 * 10**9, bytes_accessed=2**20, transcendentals=0),
        name="project",
    )(me, source, length, *normed_pieces, *weight_pieces, taps, bias, select_wide)


def live_slots(start, length_ref, rows):
    return start + lax.broadcasted_iota(jnp.int32, (rows, 1), 0) < length_ref[0]


def store_wide(ref, value):
    groups, _, width = ref.shape
    inside = value.shape[1]
    ref[:, :, :inside] = value.reshape(groups, STEP, inside)
    ref[:, :, inside:] = value[:, 2 * inside - width :].reshape(groups, STEP, width - inside)


def load_narrow(ref, inside):
    groups, _, width = ref.shape
    edge = 2 * inside - width
    value = ref[...].reshape(groups * STEP, width)
    return jnp.concatenate([value[:, :edge], value[:, edge:inside] + value[:, inside:]], axis=1)


def store_spread(entry_ref, read_ref, selected):
    turned = selected.T
    for t in range(selected.shape[0]):
        entry_ref[t] = jnp.broadcast_to(turned[R : R + NS, t : t + 1], (NS, LANES))
        read_ref[t] = jnp.broadcast_to(turned[R + NS : R + 2 * NS, t : t + 1], (NS, LANES))


def step_sizes(selected, weight_ref, bias_ref, live):
    low = selected.astype(jnp.bfloat16)
    pre = dot(low, weight_ref[...]) + bias_ref[...]
    soft = jnp.maximum(pre, 0.0) + jnp.log1p(jnp.exp(-jnp.abs(pre)))
    return low, pre, jnp.where(live, soft, 0.0)


def mixer_kernel(
    tiles, share, me_ref, length_ref, selected_ref, conv_ref, gate_ref, weight_ref, bias_ref, skip_ref, rate_ref, project_ref,
    state_ref, end_ref, mixed_out, gated_out, held_out, given_out,
    dt_ref, dx_ref, entry_ref, read_ref, out_ref, held,
):
    chunk, inside = conv_ref.shape
    step = pl.program_id(0)

    @pl.when(step == 0)
    def start():
        held[...] = jnp.zeros_like(held)

    selected, conv = (selected_ref[...], conv_ref[...])
    live = live_slots(step * chunk, length_ref, chunk)
    _, _, size = step_sizes(selected, weight_ref, bias_ref, live)
    store_wide(dt_ref, size)
    store_wide(dx_ref, size * conv)
    store_spread(entry_ref, read_ref, selected)
    scan_forward_chunk(tiles, dt_ref, dx_ref, entry_ref, read_ref, rate_ref, out_ref, state_ref, end_ref, held)
    mixed = load_narrow(out_ref, inside) + skip_ref[...] * conv
    mixed_out[...] = mixed
    gated = (mixed * to_power(gate_ref[...])).astype(jnp.bfloat16)
    gated_out[...] = gated
    part = dot(gated, project_ref[...])
    block = step // share
    rows = pl.ds(pl.multiple_of((step % share) * chunk, chunk), chunk)

    @pl.when(block % 2 == me_ref[0] % 2)
    def keep():
        held_out[0, rows] = part

    @pl.when(block % 2 != me_ref[0] % 2)
    def give():
        given_out[0, rows] = part.astype(jnp.bfloat16)


def mixer(me, length, selected, conv_out, zgate, step_wide, bias, skip, rate, out_weight, span, tiles):
    total, inside = conv_out.shape
    width = out_weight.shape[1]
    count = 2 * tiles + 1
    chunk = CHUNK
    wide = (tiles + 1) * LANES
    share = span // chunk
    smem, vmem = (pl.BlockSpec(memory_space=pltpu.SMEM), pl.BlockSpec(memory_space=pltpu.VMEM))
    row = pl.BlockSpec((chunk, inside), lambda i: (i, 0))
    part = pl.BlockSpec((1, span, width), lambda i: (i // (2 * share), 0, 0))
    f32, bf16 = (jnp.float32, jnp.bfloat16)
    return pl.pallas_call(
        functools.partial(mixer_kernel, tiles, share),
        grid=(total // chunk,),
        in_specs=[smem, smem, pl.BlockSpec((chunk, LANES), lambda i: (i, 0)), row, row] + [vmem] * 5,
        out_specs=[pl.BlockSpec((chunk, count, 8, LANES), lambda i: (i, 0, 0, 0)), vmem, row, row, part, part],
        out_shape=[
            jax.ShapeDtypeStruct((total, count, 8, LANES), f32),
            jax.ShapeDtypeStruct((count, 8, LANES), f32),
            jax.ShapeDtypeStruct((total, inside), f32),
            jax.ShapeDtypeStruct((total, inside), bf16),
            jax.ShapeDtypeStruct((2, span, width), f32),
            jax.ShapeDtypeStruct((2, span, width), bf16),
        ],
        scratch_shapes=[pltpu.VMEM((chunk // STEP, STEP, wide), f32)] * 2
        + [pltpu.VMEM((chunk, NS, LANES), f32)] * 2
        + [pltpu.VMEM((chunk // STEP, STEP, wide), f32), pltpu.VMEM((count, 8, LANES), f32)],
        compiler_params=pltpu.CompilerParams(vmem_limit_bytes=40 * 2**20),
        cost_estimate=pl.CostEstimate(flops=4 * 10**9, bytes_accessed=2**20, transcendentals=0),
        name="mixer",
    )(me, length, selected, conv_out, zgate, step_wide, bias, skip, rate, out_weight)


def row_sums(value):
    high, low = split_low(value)
    ones = jnp.ones((8, LANES), jnp.bfloat16)
    return dot_t(ones, high) + dot_t(ones, low)


def mixer_back_kernel(tiles, length_ref, *rest):
    (
        selected_ref, conv_ref, grad_ref, state_ref, end_ref, weight_ref, bias_ref, skip_ref, rate_ref,
        conv_out, rank_out, step_out, bias_out, skip_out, rate_out,
        dt_ref, dx_ref, mix_ref, entry_ref, read_ref, fed_ref, rise_ref, entry_parts, read_parts, flow, after,
    ) = rest
    chunk, inside = conv_ref.shape
    index = pl.program_id(0)
    step = pl.num_programs(0) - 1 - index

    @pl.when(index == 0)
    def start():
        flow[...] = jnp.zeros_like(flow)
        after[...] = end_ref[...]
        rate_out[...] = jnp.zeros_like(rate_out)
        step_out[...] = jnp.zeros_like(step_out)
        bias_out[...] = jnp.zeros_like(bias_out)
        skip_out[...] = jnp.zeros_like(skip_out)

    conv, grad_mixed = (conv_ref[...], grad_ref[...])
    skip_out[...] += jnp.sum(grad_mixed * conv, axis=0, keepdims=True)
    selected = selected_ref[...]
    live = live_slots(step * chunk, length_ref, chunk)
    low, pre, size = step_sizes(selected, weight_ref, bias_ref, live)
    store_wide(dt_ref, size)
    store_wide(dx_ref, size * conv)
    store_wide(mix_ref, grad_mixed)
    store_spread(entry_ref, read_ref, selected)
    scan_backward_chunk(
        tiles, dt_ref, dx_ref, mix_ref, entry_ref, read_ref, rate_ref, state_ref,
        fed_ref, rise_ref, entry_parts, read_parts, rate_out, flow, after,
    )
    fed = load_narrow(fed_ref, inside)
    grad_size = load_narrow(rise_ref, inside) * (1.0 / LOG2E) + fed * conv
    grad_pre = jnp.where(live, grad_size / (1.0 + jnp.exp(-pre)), 0.0)
    bias_out[...] += jnp.sum(grad_pre, axis=0, keepdims=True)
    grad_low = grad_pre.astype(jnp.bfloat16)
    rank = dot_t(grad_low, weight_ref[...])
    sums = [row_sums(part[...].reshape(chunk * NS, LANES)) for part in (entry_parts, read_parts)]
    lane = lax.broadcasted_iota(jnp.int32, (STEP, LANES), 1)
    for g in range(chunk // STEP):
        total = rank[g * STEP : (g + 1) * STEP]
        for i, part in enumerate(sums):
            start = R + i * NS
            moved = pltpu.roll(part[:, g * LANES : (g + 1) * LANES], start + NS, 1)
            moved = pltpu.roll(moved, 0, 1, stride=NS, stride_axis=0)
            total = jnp.where((lane >= start) & (lane < start + NS), moved, total)
        rank_out[g * STEP : (g + 1) * STEP] = total
    step_out[...] += t_dot(low, grad_low)
    conv_out[...] = fed * size + skip_ref[...] * grad_mixed


def mixer_back(length, selected, conv_out, grad_mixed, states, end, step_wide, bias, skip, rate, tiles):
    total, inside = conv_out.shape
    count = 2 * tiles + 1
    chunk = CHUNK
    steps = total // chunk
    wide = (tiles + 1) * LANES
    smem, vmem = (pl.BlockSpec(memory_space=pltpu.SMEM), pl.BlockSpec(memory_space=pltpu.VMEM))
    row = pl.BlockSpec((chunk, inside), lambda i: (steps - 1 - i, 0))
    lane = pl.BlockSpec((chunk, LANES), lambda i: (steps - 1 - i, 0))
    f32 = jnp.float32
    one = jax.ShapeDtypeStruct((1, inside), f32)
    return pl.pallas_call(
        functools.partial(mixer_back_kernel, tiles),
        grid=(steps,),
        in_specs=[smem, lane, row, row]
        + [pl.BlockSpec((chunk, count, 8, LANES), lambda i: (steps - 1 - i, 0, 0, 0))]
        + [vmem] * 5,
        out_specs=[row, lane] + [vmem] * 4,
        out_shape=[
            jax.ShapeDtypeStruct((total, inside), f32),
            jax.ShapeDtypeStruct((total, LANES), f32),
            jax.ShapeDtypeStruct((LANES, inside), f32),
            one,
            one,
            jax.ShapeDtypeStruct((count, 8, LANES), f32),
        ],
        scratch_shapes=[pltpu.VMEM((chunk // STEP, STEP, wide), f32)] * 3
        + [pltpu.VMEM((chunk, NS, LANES), f32)] * 2
        + [pltpu.VMEM((chunk // STEP, STEP, wide), f32)] * 2
        + [pltpu.VMEM((chunk, NS, LANES), f32)] * 2
        + [pltpu.VMEM((count, 8, LANES), f32)] * 2,
        compiler_params=pltpu.CompilerParams(vmem_limit_bytes=48 * 2**20),
        cost_estimate=pl.CostEstimate(flops=4 * 10**9, bytes_accessed=2**20, transcendentals=0),
        name="mixer_back",
    )(length, selected, conv_out, grad_mixed, states, end, step_wide, bias, skip, rate)


def gate_back_kernel(parts, pair, me_ref, source_ref, *rest):
    normed_refs, grad_refs, rest = (rest[:parts], rest[parts : 2 * parts], rest[2 * parts :])
    (
        gate_ref, mixed_ref, gated_ref, project_ref,
        mix_out, gate_out, gate_held, gate_given, out_held, out_given,
        normed, grads, gate_sum, out_sum, sems,
    ) = rest
    block = pl.program_id(0)
    rows, width = normed_refs[0].shape
    slab = width // parts
    me, odd, second = (me_ref[0], source_ref[parts], source_ref[parts + 1])

    @pl.when(block == 0)
    def fetch():
        copies = []
        for k in range(parts):
            at = pl.ds(pl.multiple_of((me ^ k) * rows, 16), rows)
            copies.append(pltpu.make_async_copy(normed_refs[k], normed.at[at], sems.at[k]))
            copies.append(pltpu.make_async_copy(grad_refs[k], grads.at[at], sems.at[parts + k]))
        for copy in copies:
            copy.start()
        gate_sum[...] = jnp.zeros_like(gate_sum)
        out_sum[...] = jnp.zeros_like(out_sum)
        for copy in copies:
            copy.wait()

    at = pl.ds(pl.multiple_of(block * rows, rows), rows)
    grad = grads[at]
    grad_gated = dot_t(grad, project_ref[...])
    gate = gate_ref[...]
    curve = 1.0 / (1.0 + jnp.exp(-gate))
    mix_out[...] = grad_gated * (gate * curve)
    low = (grad_gated * mixed_ref[...] * (curve * (1.0 + gate * (1.0 - curve)))).astype(jnp.bfloat16)
    gate_out[...] = low
    gate_sum[...] += t_dot(normed[at], low)
    out_sum[...] += t_dot(grad, gated_ref[...])

    @pl.when(block == parts - 1)
    def finish():
        for h in range(parts // 2):
            at = pl.ds(pl.multiple_of((2 * h + odd) * slab, 8), slab)
            gate_held[h] = gate_sum[at]
            at = pl.ds(pl.multiple_of((2 * h + 1 - odd) * slab, 8), slab)
            gate_given[h] = gate_sum[at].astype(jnp.bfloat16)
        for h in range(width // (2 * pair)):
            at = pl.ds(pl.multiple_of((2 * h + second) * pair, 8), pair)
            out_held[h] = out_sum[at]
            at = pl.ds(pl.multiple_of((2 * h + 1 - second) * pair, 8), pair)
            out_given[h] = out_sum[at].astype(jnp.bfloat16)


def gate_back(me, source, normed_pieces, grad_pieces, zgate, mixed, gated, out_weight, pair):
    parts = len(normed_pieces)
    rows, width = normed_pieces[0].shape
    total, inside = gated.shape
    slab = width // parts
    smem, anywhere = (pl.BlockSpec(memory_space=pltpu.SMEM), pl.BlockSpec(memory_space=pl.ANY))
    vmem = pl.BlockSpec(memory_space=pltpu.VMEM)
    row = pl.BlockSpec((rows, inside), lambda i: (i, 0))
    f32, bf16 = (jnp.float32, jnp.bfloat16)
    gate_shape = (parts // 2, slab, inside)
    out_shape = (width // (2 * pair), pair, inside)
    return pl.pallas_call(
        functools.partial(gate_back_kernel, parts, pair),
        grid=(parts,),
        in_specs=[smem] * 2 + [anywhere] * (2 * parts) + [row] * 3 + [vmem],
        out_specs=[row] * 2 + [vmem] * 4,
        out_shape=[
            jax.ShapeDtypeStruct((total, inside), f32),
            jax.ShapeDtypeStruct((total, inside), bf16),
            jax.ShapeDtypeStruct(gate_shape, f32),
            jax.ShapeDtypeStruct(gate_shape, bf16),
            jax.ShapeDtypeStruct(out_shape, f32),
            jax.ShapeDtypeStruct(out_shape, bf16),
        ],
        scratch_shapes=[
            pltpu.VMEM((total, width), bf16),
            pltpu.VMEM((total, width), bf16),
            pltpu.VMEM((width, inside), f32),
            pltpu.VMEM((width, inside), f32),
            pltpu.SemaphoreType.DMA((2 * parts,)),
        ],
        compiler_params=pltpu.CompilerParams(vmem_limit_bytes=48 * 2**20),
        cost_estimate=pl.CostEstimate(flops=4 * 10**9, bytes_accessed=2**20, transcendentals=0),
        name="gate_back",
    )(me, source, *normed_pieces, *grad_pieces, zgate, mixed, gated, out_weight)


def conv_back_kernel(parts, me_ref, source_ref, length_ref, *rest):
    normed_refs, rest = (rest[:parts], rest[parts:])
    (
        selected_ref, conv_ref, summed_ref, inner_ref, low_ref, taps_ref, select_ref,
        inner_out, inner_held, inner_given, select_out, taps_out, bias_out,
        normed, shifted, total, sems,
    ) = rest
    index = pl.program_id(0)
    block = parts - 1 - index
    rows, inside = inner_ref.shape
    slab = normed.shape[1] // parts
    me = me_ref[0]
    odd = source_ref[parts]

    def fetched(k):
        at = pl.ds(pl.multiple_of((me ^ k) * rows, 16), rows)
        return pltpu.make_async_copy(normed_refs[k], normed.at[at], sems.at[k])

    @pl.when(index == 0)
    def fetch():
        for k in range(parts):
            fetched(k).start()
        shifted[rows:] = jnp.zeros((8, inside), jnp.float32)
        total[...] = jnp.zeros_like(total)
        select_out[...] = jnp.zeros_like(select_out)
        taps_out[...] = jnp.zeros_like(taps_out)
        bias_out[...] = jnp.zeros_like(bias_out)

    selected = selected_ref[...]
    summed = summed_ref[...]
    curve = 1.0 / (1.0 + jnp.exp(-summed))
    grad_summed = (conv_ref[...] + dot_t(selected, select_ref[...])) * (curve * (1.0 + summed * (1.0 - curve)))
    select_out[...] += t_dot(selected, low_ref[...])
    bias_out[...] += jnp.sum(grad_summed, axis=0, keepdims=True)
    shifted[:rows] = grad_summed
    inner = inner_ref[...]
    grad_inner = jnp.zeros((rows, inside), jnp.float32)
    for k in range(KW):
        moved = shifted[KW - 1 - k : KW - 1 - k + rows]
        grad_inner = grad_inner + taps_ref[k : k + 1] * moved
        taps_out[k : k + 1] += jnp.sum(inner * moved, axis=0, keepdims=True)
    shifted[rows:] = shifted[0:8]
    live = live_slots(block * rows, length_ref, rows)
    low = jnp.where(live, grad_inner, 0.0).astype(jnp.bfloat16)
    inner_out[...] = low

    @pl.when(index == 0)
    def arrive():
        for k in range(parts):
            fetched(k).wait()

    total[...] += t_dot(normed[pl.ds(pl.multiple_of(block * rows, rows), rows)], low)

    @pl.when(block == 0)
    def finish():
        for h in range(parts // 2):
            at = pl.ds(pl.multiple_of((2 * h + odd) * slab, 8), slab)
            inner_held[h] = total[at]
            at = pl.ds(pl.multiple_of((2 * h + 1 - odd) * slab, 8), slab)
            inner_given[h] = total[at].astype(jnp.bfloat16)


def conv_back(me, source, length, normed_pieces, grad_selected, conv_grad, summed, inner, conv_low, taps, select_wide):
    parts = len(normed_pieces)
    rows, width = normed_pieces[0].shape
    slab = width // parts
    total, inside = inner.shape
    smem, anywhere = (pl.BlockSpec(memory_space=pltpu.SMEM), pl.BlockSpec(memory_space=pl.ANY))
    vmem = pl.BlockSpec(memory_space=pltpu.VMEM)
    row = pl.BlockSpec((rows, inside), lambda i: (parts - 1 - i, 0))
    f32, bf16 = (jnp.float32, jnp.bfloat16)
    return pl.pallas_call(
        functools.partial(conv_back_kernel, parts),
        grid=(parts,),
        in_specs=[smem] * 3
        + [anywhere] * parts
        + [pl.BlockSpec((rows, LANES), lambda i: (parts - 1 - i, 0))]
        + [row] * 4
        + [vmem] * 2,
        out_specs=[row] + [vmem] * 5,
        out_shape=[
            jax.ShapeDtypeStruct((total, inside), bf16),
            jax.ShapeDtypeStruct((2, slab, inside), f32),
            jax.ShapeDtypeStruct((2, slab, inside), bf16),
            jax.ShapeDtypeStruct((LANES, inside), f32),
            jax.ShapeDtypeStruct((8, inside), f32),
            jax.ShapeDtypeStruct((1, inside), f32),
        ],
        scratch_shapes=[
            pltpu.VMEM((total, width), bf16),
            pltpu.VMEM((rows + 8, inside), f32),
            pltpu.VMEM((width, inside), f32),
            pltpu.SemaphoreType.DMA((parts,)),
        ],
        compiler_params=pltpu.CompilerParams(vmem_limit_bytes=48 * 2**20),
        cost_estimate=pl.CostEstimate(flops=4 * 10**9, bytes_accessed=2**20, transcendentals=0),
        name="conv_back",
    )(me, source, length, *normed_pieces, grad_selected, conv_grad, summed, inner, conv_low, taps, select_wide)


def project_back_kernel(parts, me_ref, source_ref, *rest):
    normed_refs, weight_refs, rest = (rest[:parts], rest[parts : 2 * parts], rest[2 * parts :])
    inner_ref, gate_ref, held_out, given_out, gain_out, normed, weight, projected, sems = rest
    block = pl.program_id(0)
    rows, inside = inner_ref.shape
    slab = weight_refs[0].shape[0]
    me = me_ref[0]

    @pl.when(block == 0)
    def fetch():
        copies = []
        for k in range(parts):
            at = pl.ds(pl.multiple_of(source_ref[k] * slab, 16), slab)
            copies.append(pltpu.make_async_copy(weight_refs[k], weight.at[at], sems.at[k]))
            at = pl.ds(pl.multiple_of((me ^ k) * rows, 16), rows)
            copies.append(pltpu.make_async_copy(normed_refs[k], normed.at[at], sems.at[parts + k]))
        for copy in copies:
            copy.start()
        gain_out[...] = jnp.zeros_like(gain_out)
        for copy in copies:
            copy.wait()

    projected[:, :inside] = inner_ref[...]
    projected[:, inside:] = gate_ref[...]
    normed_rows = normed[pl.ds(pl.multiple_of(block * rows, rows), rows)]
    grad_normed = dot_t(projected[...], weight[...])
    gain_out[...] += jnp.sum(grad_normed * normed_rows.astype(jnp.float32), axis=0, keepdims=True)

    @pl.when(block % 2 == me % 2)
    def keep():
        held_out[0] = grad_normed

    @pl.when(block % 2 != me % 2)
    def give():
        given_out[0] = grad_normed.astype(jnp.bfloat16)


def project_back(me, source, normed_pieces, weight_pieces, inner_grad, gate_grad):
    parts = len(normed_pieces)
    rows, width = normed_pieces[0].shape
    slab, both = weight_pieces[0].shape
    total, inside = inner_grad.shape
    smem, anywhere = (pl.BlockSpec(memory_space=pltpu.SMEM), pl.BlockSpec(memory_space=pl.ANY))
    vmem = pl.BlockSpec(memory_space=pltpu.VMEM)
    row = pl.BlockSpec((rows, inside), lambda i: (i, 0))
    part = pl.BlockSpec((1, rows, width), lambda i: (i // 2, 0, 0))
    f32, bf16 = (jnp.float32, jnp.bfloat16)
    return pl.pallas_call(
        functools.partial(project_back_kernel, parts),
        grid=(parts,),
        in_specs=[smem] * 2 + [anywhere] * (2 * parts) + [row] * 2,
        out_specs=[part, part, vmem],
        out_shape=[
            jax.ShapeDtypeStruct((2, rows, width), f32),
            jax.ShapeDtypeStruct((2, rows, width), bf16),
            jax.ShapeDtypeStruct((1, width), f32),
        ],
        scratch_shapes=[
            pltpu.VMEM((total, width), bf16),
            pltpu.VMEM((slab * parts, both), bf16),
            pltpu.VMEM((rows, both), bf16),
            pltpu.SemaphoreType.DMA((2 * parts,)),
        ],
        compiler_params=pltpu.CompilerParams(vmem_limit_bytes=40 * 2**20),
        cost_estimate=pl.CostEstimate(flops=4 * 10**9, bytes_accessed=2**20, transcendentals=0),
        name="project_back",
    )(me, source, *normed_pieces, *weight_pieces, inner_grad, gate_grad)


def norm_kernel(parts, me_ref, tokens_ref, *rest):
    small_refs, normed_out, gains_out = (rest[:parts], rest[parts], rest[parts + 1])
    slab = small_refs[0].shape[1]
    for m in range(parts):

        @pl.when(me_ref[0] == m)
        def lay():
            for p in range(parts):
                gains_out[:, p * slab : (p + 1) * slab] = small_refs[p ^ m][...]

    tokens = tokens_ref[...]
    scale = lax.rsqrt(jnp.mean(tokens * tokens, axis=-1, keepdims=True) + EPSILON)
    normed_out[...] = (tokens * scale * gains_out[2:3]).astype(jnp.bfloat16)


def norm_rows(me, tokens, small_pieces):
    parts = len(small_pieces)
    smem, vmem = (pl.BlockSpec(memory_space=pltpu.SMEM), pl.BlockSpec(memory_space=pltpu.VMEM))
    return pl.pallas_call(
        functools.partial(norm_kernel, parts),
        in_specs=[smem] + [vmem] * (1 + parts),
        out_specs=[vmem] * 2,
        out_shape=[
            jax.ShapeDtypeStruct(tokens.shape, jnp.bfloat16),
            jax.ShapeDtypeStruct((small_pieces[0].shape[0], tokens.shape[1]), jnp.float32),
        ],
        compiler_params=pltpu.CompilerParams(vmem_limit_bytes=16 * 2**20),
        name="norm_rows",
    )(me, tokens, *small_pieces)


def route_kernel(
    me_ref, length_ref, tokens_ref, near_ref, got_ref, gains_ref, order_ref, routes_ref,
    first_out, normed_out, sent_out, probs_out,
):
    rows, width = tokens_ref.shape
    first = tokens_ref[...] + near_ref[...] + got_ref[...].astype(jnp.float32)
    first_out[...] = first
    scale = lax.rsqrt(jnp.mean(first * first, axis=-1, keepdims=True) + EPSILON)
    normed = (first * scale * gains_ref[3:4]).astype(jnp.bfloat16)
    normed_out[...] = normed
    logits = dot_t(normed, router_rows(gains_ref))
    gap = logits[:, 0:1] - logits[:, 1:2]
    prob_zero = 1.0 / (1.0 + jnp.exp(-gap))
    prob_one = 1.0 / (1.0 + jnp.exp(gap))
    lane = lax.broadcasted_iota(jnp.int32, (rows, LANES), 1)
    probs_out[...] = jnp.where(lane == 0, prob_zero, jnp.where(lane == 1, prob_one, 0.0))
    gate = jnp.where(routes_ref[...] == 0, prob_zero, prob_one)
    gate = jnp.where(live_rows(me_ref, length_ref, rows), gate, 0.0)
    high, low = split_low(gate)
    high, low = (high.astype(jnp.float32), low.astype(jnp.float32))
    gates = jnp.where(lane == 0, high, jnp.where(lane == 1, low, 0.0)).astype(jnp.bfloat16)
    sent_out[:, :width] = dot(order_ref[...], normed).astype(jnp.bfloat16)
    sent_out[:, width:] = dot(order_ref[...], gates).astype(jnp.bfloat16)


def route(me, length, tokens, near, got, gains, order, routes):
    rows, width = tokens.shape
    smem, vmem = (pl.BlockSpec(memory_space=pltpu.SMEM), pl.BlockSpec(memory_space=pltpu.VMEM))
    return pl.pallas_call(
        route_kernel,
        in_specs=[smem, smem] + [vmem] * 6,
        out_specs=[vmem] * 4,
        out_shape=[
            jax.ShapeDtypeStruct((rows, width), jnp.float32),
            jax.ShapeDtypeStruct((rows, width), jnp.bfloat16),
            jax.ShapeDtypeStruct((rows, width + LANES), jnp.bfloat16),
            jax.ShapeDtypeStruct((rows, LANES), jnp.float32),
        ],
        compiler_params=pltpu.CompilerParams(vmem_limit_bytes=32 * 2**20),
        name="route",
    )(me, length, tokens, near, got, gains, order, routes)


def expert_kernel(parts, cap, steps, me_ref, source_ref, counts_ref, *rest):
    sent_refs, cot_refs, up_refs = (rest[:parts], rest[parts : 2 * parts], rest[2 * parts : 3 * parts])
    (
        down_ref, grad_held, grad_given, out_held, out_given, packed,
    ) = rest[3 * parts : 3 * parts + 6]
    rows, cots, up, down, rows_t, cots_t, scale, dots, grad_sum, out_sum, product, sems = rest[3 * parts + 6 :]
    step = pl.program_id(0)
    expert, tile = (step // steps, step % steps)
    span, width = cots.shape[1:]
    slab = up_refs[0].shape[1]
    offset = span - cap
    count = parts * cap
    me = me_ref[0]

    @pl.when(step == 0)
    def fetch():
        copies = [pltpu.make_async_copy(down_ref, down, sems.at[0])]
        for k in range(parts):
            copies.append(pltpu.make_async_copy(sent_refs[k], rows.at[me ^ k], sems.at[1 + k]))
            copies.append(pltpu.make_async_copy(cot_refs[k], cots.at[me ^ k], sems.at[1 + parts + k]))
            at = pl.ds(pl.multiple_of(source_ref[k] * slab, 16), slab)
            copies.append(pltpu.make_async_copy(up_refs[k], up.at[:, at], sems.at[1 + 2 * parts + k]))
        for copy in copies:
            copy.start()
        grad_sum[...] = jnp.zeros_like(grad_sum)
        out_sum[...] = jnp.zeros_like(out_sum)
        dots[...] = jnp.zeros_like(dots)
        for copy in copies:
            copy.wait()

    at = pl.ds(pl.multiple_of(expert * offset, 16), cap)
    mine = rows[:, at, :width].reshape(count, width)
    cot = cots[:, at].reshape(count, width)

    @pl.when(tile == 0)
    def turn():
        rows_t[...] = mine.T
        cots_t[...] = cot.T
        slot = lax.broadcasted_iota(jnp.int32, (cap, LANES), 0)
        for b in range(parts):
            gates = rows[b, at, width:].astype(jnp.float32)
            gate = gates[:, 0:1] + gates[:, 1:2]
            first = slot < counts_ref[b]
            later = slot + offset >= counts_ref[b]
            live = jnp.where(expert == 0, first.astype(jnp.float32), later.astype(jnp.float32))
            scale[b * cap : (b + 1) * cap] = live * gate

    columns = pl.ds(pl.multiple_of(tile * FTILE, FTILE), FTILE)
    up_tile = up[expert, :, columns]
    down_tile = down[expert, columns, :]
    weight = scale[...][:, 0:1]
    pre = dot(mine, up_tile)
    grad_hidden = dot_t(cot, down_tile)
    square = pre * pre
    bend = jnp.tanh(0.7978845608028654 * pre * (1.0 + 0.044715 * square))
    rise = 0.5 * (1.0 + bend)
    slope = rise + 0.5 * pre * (1.0 - bend * bend) * (0.7978845608028654 * (1.0 + 0.134145 * square))
    hidden = (weight * (pre * rise)).astype(jnp.bfloat16)
    grad_pre = (weight * slope * grad_hidden).astype(jnp.bfloat16)
    part = jnp.sum(hidden.astype(jnp.float32) * grad_hidden, axis=1, keepdims=True)
    dots[:, at] += jnp.broadcast_to(part, (count, LANES)).reshape(parts, cap, LANES)
    out_sum[:, at] += dot(hidden, down_tile).reshape(parts, cap, width)
    grad_sum[:, at] += dot_t(grad_pre, up_tile).reshape(parts, cap, width)
    product[...] = dot(rows_t[...], grad_pre)
    fours = packed.shape[0]
    inside = packed.shape[-1] // LANES
    share = width // (fours * parts)
    pieces = []
    for q in range(FTILE // LANES):
        piece = tile * (FTILE // LANES) + q
        pieces.append((piece // inside, pl.ds(pl.multiple_of(piece % inside * LANES, LANES), LANES)))
    up_rows = pl.ds(pl.multiple_of(expert * slab, 16), slab)
    for q, (block, lanes) in enumerate(pieces):
        for r in range(parts):
            taken = product[r * slab : (r + 1) * slab, q * LANES : (q + 1) * LANES]
            packed[block, r, up_rows, lanes] = taken.astype(jnp.bfloat16)
    product[...] = dot(cots_t[...], hidden)
    base = 2 * slab
    for q, (block, lanes) in enumerate(pieces):
        down_rows = pl.ds(pl.multiple_of(base + (expert * fours + block) * share, 16), share)
        for g in range(fours * parts):
            taken = product[g * share : (g + 1) * share, q * LANES : (q + 1) * LANES]
            packed[g // parts, g % parts, down_rows, lanes] = taken.astype(jnp.bfloat16)

    @pl.when(step == pl.num_programs(0) - 1)
    def finish():
        for b in range(parts):

            @pl.when(me % 2 == b % 2)
            def hold():
                grad_held[b // 2, :, :width] = grad_sum[b]
                grad_held[b // 2, :, width:] = dots[b]
                out_held[b // 2] = out_sum[b]

            @pl.when(me % 2 != b % 2)
            def give():
                grad_given[b // 2, :, :width] = grad_sum[b].astype(jnp.bfloat16)
                grad_given[b // 2, :, width:] = dots[b].astype(jnp.bfloat16)
                out_given[b // 2] = out_sum[b].astype(jnp.bfloat16)


def experts(me, source, counts, sent_pieces, cot_pieces, up_pieces, down_weight, fours):
    parts = len(sent_pieces)
    span, width = cot_pieces[0].shape
    number, hid = down_weight.shape[:2]
    steps = hid // FTILE
    slab = up_pieces[0].shape[1]
    smem, anywhere = (pl.BlockSpec(memory_space=pltpu.SMEM), pl.BlockSpec(memory_space=pl.ANY))
    vmem = pl.BlockSpec(memory_space=pltpu.VMEM)
    f32, bf16 = (jnp.float32, jnp.bfloat16)
    packed = (fours, parts, 2 * number * slab, hid // fours)
    count = parts * CAP
    return pl.pallas_call(
        functools.partial(expert_kernel, parts, CAP, steps),
        grid=(number * steps,),
        in_specs=[smem] * 3 + [anywhere] * (3 * parts + 1),
        out_specs=[vmem] * 5,
        out_shape=[
            jax.ShapeDtypeStruct((2, span, width + LANES), f32),
            jax.ShapeDtypeStruct((2, span, width + LANES), bf16),
            jax.ShapeDtypeStruct((2, span, width), f32),
            jax.ShapeDtypeStruct((2, span, width), bf16),
            jax.ShapeDtypeStruct(packed, bf16),
        ],
        scratch_shapes=[
            pltpu.VMEM((parts, span, width + LANES), bf16),
            pltpu.VMEM((parts, span, width), bf16),
            pltpu.VMEM((number, slab * parts, hid), bf16),
            pltpu.VMEM((number, hid, width), bf16),
            pltpu.VMEM((width, count), bf16),
            pltpu.VMEM((width, count), bf16),
            pltpu.VMEM((count, LANES), f32),
            pltpu.VMEM((parts, span, LANES), f32),
            pltpu.VMEM((parts, span, width), f32),
            pltpu.VMEM((parts, span, width), f32),
            pltpu.VMEM((width, FTILE), f32),
            pltpu.SemaphoreType.DMA((1 + 3 * parts,)),
        ],
        compiler_params=pltpu.CompilerParams(vmem_limit_bytes=60 * 2**20),
        cost_estimate=pl.CostEstimate(flops=4 * 10**9, bytes_accessed=2**20, transcendentals=0),
        name="experts",
    )(me, source, counts, *sent_pieces, *cot_pieces, *up_pieces, down_weight)


def return_kernel(
    me_ref, length_ref, near_ref, got_ref, order_ref, normed_ref, probs_ref, routes_ref, first_ref, cot_ref, gains_ref,
    grad_out, low_out, gain_out, router_out,
):
    rows, width = first_ref.shape
    grad = near_ref[...] + got_ref[...].astype(jnp.float32)
    high, low = split_low(grad)
    grad = dot(order_ref[...], high) + dot(order_ref[...], low)
    lane = lax.broadcasted_iota(jnp.int32, (rows, LANES), 1)
    chosen = (lane == routes_ref[...]).astype(jnp.float32)
    grad_logits = (grad[:, width : width + 1] * (chosen - probs_ref[...])).astype(jnp.bfloat16)
    grad_normed = grad[:, :width] + dot(grad_logits[:, :NS], router_rows(gains_ref))
    router_out[...] = t_dot(grad_logits, normed_ref[...])[0:8]
    first = first_ref[...]
    scale = lax.rsqrt(jnp.mean(first * first, axis=-1, keepdims=True) + EPSILON)
    unit = first * scale
    gain_out[...] = jnp.sum(grad_normed * unit, axis=0, keepdims=True)
    pulled = grad_normed * gains_ref[3:4]
    pulled = scale * (pulled - unit * jnp.mean(pulled * unit, axis=-1, keepdims=True))
    total = jnp.where(live_rows(me_ref, length_ref, rows), cot_ref[...], 0.0) + pulled
    grad_out[...] = total
    low_out[...] = total.astype(jnp.bfloat16)


def return_rows(me, length, *operands):
    rows, width = operands[6].shape
    smem, vmem = (pl.BlockSpec(memory_space=pltpu.SMEM), pl.BlockSpec(memory_space=pltpu.VMEM))
    return pl.pallas_call(
        return_kernel,
        in_specs=[smem, smem] + [vmem] * 9,
        out_specs=[vmem] * 4,
        out_shape=[
            jax.ShapeDtypeStruct((rows, width), jnp.float32),
            jax.ShapeDtypeStruct((rows, width), jnp.bfloat16),
            jax.ShapeDtypeStruct((1, width), jnp.float32),
            jax.ShapeDtypeStruct((8, width), jnp.float32),
        ],
        compiler_params=pltpu.CompilerParams(vmem_limit_bytes=32 * 2**20),
        name="return_rows",
    )(me, length, *operands)


def finish_kernel(
    me_ref, length_ref, near_ref, got_ref, out_near_ref, out_got_ref, order_ref, first_ref, grad_ref, tokens_ref, gains_ref,
    result_out, grad_out,
):
    rows = tokens_ref.shape[0]
    grad = near_ref[...] + got_ref[...].astype(jnp.float32)
    tokens = tokens_ref[...]
    scale = lax.rsqrt(jnp.mean(tokens * tokens, axis=-1, keepdims=True) + EPSILON)
    unit = tokens * scale
    pulled = grad * gains_ref[2:3]
    grad_out[...] = grad_ref[...] + scale * (pulled - unit * jnp.mean(pulled * unit, axis=-1, keepdims=True))
    high, low = split_low(out_near_ref[...] + out_got_ref[...].astype(jnp.float32))
    added = dot(order_ref[...], high) + dot(order_ref[...], low)
    result_out[...] = jnp.where(live_rows(me_ref, length_ref, rows), first_ref[...] + added, 0.0)


def finish_rows(me, length, *operands):
    shape = operands[5].shape
    smem, vmem = (pl.BlockSpec(memory_space=pltpu.SMEM), pl.BlockSpec(memory_space=pltpu.VMEM))
    return pl.pallas_call(
        finish_kernel,
        in_specs=[smem, smem] + [vmem] * 9,
        out_specs=[vmem] * 2,
        out_shape=[jax.ShapeDtypeStruct(shape, jnp.float32)] * 2,
        compiler_params=pltpu.CompilerParams(vmem_limit_bytes=32 * 2**20),
        name="finish_rows",
    )(me, length, *operands)


def body(
    tokens,
    routes,
    lengths,
    cotangent,
    in_weight,
    select_weight,
    step_weight,
    out_weight,
    router_weight,
    up_weight,
    down_weight,
    conv_weight,
    conv_bias,
    step_bias,
    decay_log,
    skip_gain,
    mixer_gain,
    expert_gain,
):
    f32, bf16 = (jnp.float32, jnp.bfloat16)
    span, width = tokens.shape
    groups, parts = (lax.axis_size("grp"), lax.axis_size("shard"))
    me, group = (lax.axis_index("shard"), lax.axis_index("grp"))
    total = span * parts
    inside = conv_bias.shape[0]
    tiles = inside // LANES
    slab = in_weight.shape[0]
    hidden_cols = up_weight.shape[2] // parts
    share = width // groups
    bits = [2**i for i in range(groups.bit_length() - 1)]
    down_bit = 2 if share % 8 == 0 else bits[-1]
    pair = 2 * share if share % 8 == 0 else width // 2
    odd, second = (group % 2, (group // down_bit) % 2)
    me_one = jnp.full((1,), me, jnp.int32)
    source = [me, me ^ 1, me ^ (2 + odd), me ^ (3 - odd), odd, second]
    source = jnp.stack(source).astype(jnp.int32)

    first = (routes[:, 0] == 0).astype(jnp.int32)
    count_first = jnp.sum(first)
    small = jnp.concatenate(
        [
            router_weight.astype(f32).T,
            mixer_gain.astype(f32)[None],
            expert_gain.astype(f32)[None],
            jnp.full((1, slab), count_first, jnp.int32).astype(f32),
            jnp.zeros((11, slab), f32),
        ],
        axis=0,
    )
    small = [small] + [swap(small, k) for k in range(1, parts)]
    in_pieces, up_pieces = cut_weights(source[:3], in_weight, up_weight, parts, inside)
    in_pieces = share_pieces(in_pieces)
    normed, gains = norm_rows(me_one, tokens, small)
    normed_pieces = gather_pieces(normed)
    counts = gains[4].reshape(parts, slab)[:, 0].astype(jnp.int32)

    goal = jnp.where(first > 0, jnp.cumsum(first), count_first + jnp.cumsum(1 - first)) - 1
    slots = jnp.arange(span, dtype=jnp.int32)
    order = (slots[:, None] == goal[None, :]).astype(bf16)
    order_t = (goal[:, None] == slots[None, :]).astype(bf16)
    live = (me * span + slots < lengths[0])[:, None]
    cots = matmul(order, jnp.where(live, cotangent, 0.0).astype(bf16)).astype(bf16)
    cot_pieces = gather_pieces(cots)

    taps = conv_weight.astype(f32)
    spare = LANES - select_weight.shape[1]
    select_wide = jnp.pad(select_weight, ((0, 0), (0, spare)))
    inner, zgate, summed, conv_out, conv_low, selected = project(
        me_one,
        source,
        lengths,
        normed_pieces,
        in_pieces,
        taps,
        conv_bias.astype(f32)[None, :],
        select_wide,
    )
    selected = tie(selected + swap(selected, 1), cot_pieces[2])
    selected = selected + swap(selected, 2)
    up_pieces = share_pieces([up_pieces[0], up_pieces[1], tie(up_pieces[2], selected)])
    step_wide = jnp.pad(step_weight, ((0, LANES - R), (0, 0)))
    step_row = step_bias.astype(f32)[None, :]
    decay = -jnp.exp(decay_log.astype(f32))
    rate = pack(decay * LOG2E, tiles)
    skip = skip_gain.astype(f32)[None, :]
    states, end, mixed, gated, held, given = mixer(
        me_one, lengths, selected, conv_out, zgate, step_wide, step_row, skip, rate, out_weight, span, tiles
    )
    near, given = scatter_near(held, tie(given, up_pieces[2]))
    first_sum, normed_two, sent, probs = route(
        me_one, lengths, tokens, near, swap(given, 2), gains, order, routes
    )
    fours, eights = (groups // 4, groups // 8)
    fine = hidden_cols // fours % LANES == 0 and share % 16 == 0
    grad_held, grad_given, out_held, out_given, packed = experts(
        me_one, source, counts, gather_pieces(sent), cot_pieces, up_pieces, down_weight, fours if fine else 1
    )
    up_cols = hidden_cols // fours
    if not fine:
        up_rows = packed[0, :, : E * slab].reshape(parts, E * slab, fours, up_cols).transpose(2, 0, 1, 3)
        down_rows = packed[0, :, E * slab :].reshape(parts, E, fours, share, fours, up_cols)
        down_rows = down_rows.transpose(2, 0, 1, 4, 3, 5).reshape(fours, parts, E * fours * share, up_cols)
        down_rows = down_rows.swapaxes(0, 1).reshape(fours, parts, E * fours * share, up_cols)
        packed = jnp.concatenate([up_rows, down_rows], axis=2)
    packed = packed.reshape(groups, 2 * E * slab, up_cols)
    packed = lax.psum_scatter(packed, "grp", scatter_dimension=0, tiled=True)
    up_sum, down_sum = (packed[:, : E * slab], packed[:, E * slab :])
    near, given = scatter_near(grad_held, grad_given)
    grad_first, grad_first_low, expert_gain_grad, router_grad = return_rows(
        me_one,
        lengths,
        near,
        swap(given, 2),
        order_t,
        normed_two,
        probs,
        routes,
        first_sum,
        cotangent,
        gains,
    )
    grad_pieces = gather_pieces(grad_first_low)
    top = bits[-1]
    out_bits = [bit for bit in bits[:0:-1] if bit != down_bit]
    blocks = (groups // 4, 2, share, inside)
    grad_mixed, grad_zgate, gate_held, gate_given, out_grad_held, out_grad_given = gate_back(
        me_one, source, normed_pieces, grad_pieces, zgate, mixed, gated, out_weight, pair
    )
    gate_got, out_grad_got = (swap_groups(gate_given, 1), swap_groups(out_grad_given, down_bit))
    conv_part, grad_selected, step_grad, step_bias_grad, skip_grad, rate_grad = mixer_back(
        lengths, selected, conv_out, grad_mixed, states, end, step_wide, step_row, skip, rate, tiles
    )
    chip_selected = grad_selected + swap(grad_selected, 1)
    gate_held, gate_given = halve((gate_held, gate_got), 0, 2, chip_selected)
    gate_got = swap_groups(gate_given, 2)
    out_parts = (out_grad_held.reshape(blocks), out_grad_got.reshape(blocks))
    out_grad_held, out_grad_given = halve(out_parts, 1, 1, chip_selected)
    out_grad_got = swap_groups(out_grad_given, 1)

    def up_home(g, s):
        return (s * fours + g // 4) * parts + g % 4

    def in_home(g, s):
        half, k = (g // (groups // 2), (g // 4) % eights)
        return (half * (groups // 2) + s * eights + k) * parts + g % 4

    both_axes = ("grp", "shard")
    places = [(g, s) for g in range(groups) for s in range(parts)]
    up_sum = lax.ppermute(tie(up_sum, chip_selected), both_axes, [(g * parts + s, up_home(g, s)) for g, s in places])
    grad_selected = (chip_selected + swap(chip_selected, 2)).astype(bf16)
    inner_grad, inner_held, inner_given, select_grad, conv_grad, conv_bias_grad = conv_back(
        me_one,
        source,
        lengths,
        normed_pieces,
        grad_selected,
        conv_part,
        summed,
        inner,
        conv_low,
        taps,
        select_wide,
    )
    inner_got = swap_groups(inner_given, 1)
    held, given, mixer_part = project_back(
        me_one, source, normed_pieces, in_pieces, inner_grad, grad_zgate
    )
    inner_held, inner_given = halve((inner_held, inner_got), 0, 2, given)
    inner_got = swap_groups(inner_given, 2)
    gate_sum = join(gate_held, gate_got, inner_held)
    for bit in out_bits:
        out_grad_held, out_grad_given = halve((out_grad_held, out_grad_got), 0, bit, inner_held)
        out_grad_got = swap_groups(out_grad_given, bit)
    shared = jnp.concatenate([router_grad[0:E], expert_gain_grad, mixer_part / gains[2:3]], axis=0)
    shared = shared + swap(shared, 1)
    shared = tie(shared + swap(shared, 2), inner_held)
    shared = lax.dynamic_slice_in_dim(shared, me * slab, slab, 1)
    decay_grad = decay * unpack(rate_grad, tiles)
    picked = select_weight.shape[1]
    few = [
        select_grad[:picked],
        conv_grad[:KW],
        conv_bias_grad,
        step_grad[:R],
        decay_grad,
        step_bias_grad,
        skip_grad,
        shared.reshape(2, inside),
    ]
    starts = [0]
    for part in few:
        starts.append(starts[-1] + part.shape[0])
    few = jnp.concatenate(few, axis=0).astype(bf16)
    few_got = swap_groups(few, 1)
    near, given = scatter_near(held, given, inner_held)
    got = swap(given, 2)
    out_near, out_given = scatter_near(out_held, out_given, inner_held)
    out_got = swap(out_given, 2)
    few = join(few, few_got, given, out_given).astype(bf16)
    few_got = swap_groups(few, 2)

    inner_sum = join(inner_held, inner_got, few)
    for bit in bits[-2:1:-1]:
        inner_held, inner_given = halve(inner_sum, 2, bit)
        inner_sum = join(inner_held, swap_groups(inner_given, bit))
        gate_held, gate_given = halve(gate_sum, 2, bit)
        gate_sum = join(gate_held, swap_groups(gate_given, bit))
    upper = group >= top
    own = jnp.where(upper, gate_sum, inner_sum).reshape(slab, inside // eights).astype(bf16)
    other = jnp.where(upper, inner_sum, gate_sum).reshape(slab, inside // eights).astype(bf16)
    own = lax.ppermute(own, both_axes, [(g * parts + s, in_home(g, s)) for g, s in places])
    other = lax.ppermute(other, both_axes, [(g * parts + s, in_home(g ^ top, s)) for g, s in places])
    few = join(few, few_got, inner_sum).astype(bf16)
    few_got = swap_groups(few, bits[2])
    out_sum = join(out_grad_held, out_grad_got, inner_sum).reshape(share, inside)
    result, tokens_grad = finish_rows(
        tie(me_one, few),
        lengths,
        near,
        got,
        out_near,
        out_got,
        order_t,
        first_sum,
        grad_first,
        tokens,
        gains,
    )
    in_sum = join(own, other, result)
    few = total_rest(join(few, few_got, result), bits[3:])
    few = [few[a:b] for a, b in zip(starts[:-1], starts[1:])]
    select_grad, conv_grad, conv_bias_grad, step_grad, decay_grad, step_bias_grad, skip_grad, shared = few
    shared = shared.reshape(4, slab)
    up_sum = up_sum.astype(f32).reshape(E, slab, up_cols)
    down_sum = down_sum.astype(f32).reshape(E, fours, share, up_cols).transpose(0, 2, 1, 3)
    down_sum = down_sum.reshape(E, share, hidden_cols)
    return (
        result,
        tokens_grad,
        in_sum,
        out_sum.T,
        up_sum,
        down_sum.transpose(0, 2, 1),
        select_grad.T,
        step_grad,
        shared[0:E].T,
        conv_grad,
        conv_bias_grad[0],
        step_bias_grad[0],
        decay_grad,
        skip_grad[0],
        shared[3],
        shared[2],
    )


def solution(mesh):
    return jax.shard_map(
        body,
        mesh=mesh,
        in_specs=(
            P(("grp", "shard"), None),
            P(("grp", "shard"), None),
            P("grp"),
            P(("grp", "shard"), None),
            P("shard", None),
            P("shard", None),
            P(None, "shard"),
            P("shard", None),
            P("shard", None),
            P(None, "shard", None),
            P(None, "shard", None),
            P(None, "shard"),
            P("shard"),
            P("shard"),
            P(None, "shard"),
            P("shard"),
            P("shard"),
            P("shard"),
        ),
        out_specs=(
            P(("grp", "shard"), None),
            P(("grp", "shard"), None),
            P("shard", "grp"),
            P("shard", "grp"),
            P(None, "shard", "grp"),
            P(None, "shard", "grp"),
            P("shard", None),
            P(None, "shard"),
            P("shard", None),
            P(None, "shard"),
            P("shard"),
            P("shard"),
            P(None, "shard"),
            P("shard"),
            P("shard"),
            P("shard"),
        ),
        check_vma=False,
    )
```

```python
import functools
import jax
import jax.numpy as jnp
from jax import lax
from jax.experimental import pallas as pl
from jax.experimental.pallas import tpu as pltpu
from jax.sharding import PartitionSpec as P

R = 72
KW = 4
E = 2
CAP = 192
EPSILON = 1e-05
FTILE = 768
LOG2E = 1.4426950408889634

NS = 16
LANES = 128
STEP = 8
CHUNK = 64


def swap(value, bit):
    size = lax.axis_size("shard")
    return lax.ppermute(value, "shard", [(i, i ^ bit) for i in range(size)])


def swap_groups(value, bit):
    size = lax.axis_size("grp")
    return lax.ppermute(value, "grp", [(g, g ^ bit) for g in range(size)])


def tie(value, *others):
    for other in others:
        corner = other[(0,) * other.ndim].astype(jnp.float32)
        value = value + (0.0 * corner).astype(value.dtype)
    return value


def gather_pieces(value):
    far = swap(value, 2)
    return (value, swap(value, 1), far, swap(far, 1))


def scatter_near(held, given, *others):
    side = lax.axis_index("shard") // 2
    held = tie(held + swap(given, 1).astype(jnp.float32), *others)
    mine = lax.dynamic_index_in_dim(held, side, 0, False)
    return mine, lax.dynamic_index_in_dim(held, 1 - side, 0, False).astype(jnp.bfloat16)


def halve(value, axis, bit, *others):
    mine = (lax.axis_index("grp") // bit) % 2
    terms = value if isinstance(value, tuple) else (value,)
    size = terms[0].shape[axis] // 2

    def side(index):
        picked = [lax.dynamic_slice_in_dim(term, index * size, size, axis) for term in terms]
        total = picked[0].astype(jnp.float32)
        for term in picked[1:]:
            total = total + term.astype(jnp.float32)
        return tie(total, *others)

    return side(mine), side(1 - mine).astype(jnp.bfloat16)


def join(held, got, *others):
    return tie(held.astype(jnp.float32) + got.astype(jnp.float32), *others)


def share_pieces(pieces):
    groups, parts = (lax.axis_size("grp"), lax.axis_size("shard"))
    moves = [
        (g * parts + s, g * parts + (s ^ (2 + g % 2))) for g in range(groups) for s in range(parts)
    ]
    crossed = lax.ppermute(pieces[2], ("grp", "shard"), moves)
    shared = lax.ppermute(crossed, "grp", [(g, g ^ 1) for g in range(groups)])
    return [pieces[0], swap(pieces[1], 1), crossed, shared]


def exchange(value, bits):
    return [value] + [swap_groups(value, sum(bits[i] for i in range(len(bits)) if k >> i & 1)) for k in range(1, 2 ** len(bits))]


def balanced(terms, *others):
    terms = [term.astype(jnp.float32) for term in terms]
    while len(terms) > 1:
        terms = [terms[i] + terms[i + 1] for i in range(0, len(terms), 2)]
    return tie(terms[0], *others)


def total_rest(value, bits, kind=jnp.bfloat16):
    for bit in bits:
        value = balanced(exchange(value.astype(kind), [bit]))
    return value


def matmul(left, right):
    return jnp.dot(left, right, preferred_element_type=jnp.float32)


def pack(value, tiles):
    edge = tiles * LANES
    full = value[:, :edge].reshape(2, 8, tiles, LANES).transpose(2, 0, 1, 3)
    rest = jnp.concatenate([value[:8, edge:], value[8:, edge:]], axis=1)
    return jnp.concatenate([full.reshape(2 * tiles, 8, LANES), rest[None]], axis=0)


def unpack(value, tiles):
    full = value[: 2 * tiles].reshape(tiles, 2, 8, LANES).transpose(1, 2, 0, 3)
    rest = value[2 * tiles]
    rest = jnp.concatenate([rest[:, : LANES // 2], rest[:, LANES // 2 :]], axis=0)
    return jnp.concatenate([full.reshape(NS, tiles * LANES), rest], axis=1)


def fold_rows(parts):
    row = lax.broadcasted_iota(jnp.int32, (8, LANES), 0)
    top, pair, even = (row < 4, (row & 2) == 0, (row & 1) == 0)
    fours = [
        jnp.where(top, parts[i], parts[i + 4])
        + pltpu.roll(jnp.where(top, parts[i + 4], parts[i]), 4, 0)
        for i in range(4)
    ]
    twos = [
        jnp.where(
            pair,
            fours[i] + pltpu.roll(fours[i], 6, 0),
            fours[i + 2] + pltpu.roll(fours[i + 2], 2, 0),
        )
        for i in range(2)
    ]
    return jnp.where(
        even, twos[0] + pltpu.roll(twos[0], 7, 0), twos[1] + pltpu.roll(twos[1], 1, 0)
    )


def halves(pair_ref, at, left):
    low, high = (pair_ref[at, 0:8], pair_ref[at, 8:16])
    return (low, high, jnp.where(left, low, high))


def scan_forward_chunk(tiles, dt_ref, dx_ref, entry_ref, read_ref, rate_ref, out_ref, state_ref, end_ref, held):
    left = lax.broadcasted_iota(jnp.int32, (8, LANES), 1) < LANES // 2

    def group(g, states):
        at, base = (g, g * STEP)
        states = list(states)
        entry = [halves(entry_ref, base + t, left) for t in range(STEP)]
        read = [halves(read_ref, base + t, left) for t in range(STEP)]
        for tile in range(tiles + 1):
            columns = slice(tile * LANES, (tile + 1) * LANES)
            rows = [2 * tile] if tile == tiles else [2 * tile, 2 * tile + 1]
            which = [2] if tile == tiles else [0, 1]
            sums = []
            for t in range(STEP):
                step = dt_ref[at, t : t + 1, columns]
                fed = dx_ref[at, t : t + 1, columns]
                total = None
                for r, w in zip(rows, which):
                    state_ref[base + t, r] = states[r]
                    states[r] = jnp.exp2(step * rate_ref[r]) * states[r] + entry[t][w] * fed
                    term = read[t][w] * states[r]
                    total = term if total is None else total + term
                sums.append(total)
            out_ref[at, :, columns] = fold_rows(sums)
        return tuple(states)

    count = 2 * tiles + 1
    states = lax.fori_loop(0, dt_ref.shape[0], group, tuple(held[r] for r in range(count)))
    for r in range(count):
        held[r] = states[r]
        end_ref[r] = states[r]


def scan_backward_chunk(
    tiles, dt_ref, dx_ref, grad_ref, entry_ref, read_ref, rate_ref, state_ref,
    fed_out, step_out, entry_out, read_out, rate_out, flow, after,
):
    count = 2 * tiles + 1
    left = lax.broadcasted_iota(jnp.int32, (8, LANES), 1) < LANES // 2
    groups = dt_ref.shape[0]

    def group(g, carry):
        at = groups - 1 - g
        base = at * STEP
        flows, afters = (list(carry[0]), list(carry[1]))
        entry = [halves(entry_ref, base + t, left) for t in range(STEP)]
        read = [halves(read_ref, base + t, left) for t in range(STEP)]
        entry_sum = [[None, None] for _ in range(STEP)]
        read_sum = [[None, None] for _ in range(STEP)]
        for tile in range(tiles + 1):
            last = tile == tiles
            columns = slice(tile * LANES, (tile + 1) * LANES)
            rows = [2 * tile] if last else [2 * tile, 2 * tile + 1]
            which = [2] if last else [0, 1]
            fed_sums, step_sums = ([None] * STEP, [None] * STEP)
            rate_sum = [rate_out[r] for r in rows]
            for t in reversed(range(STEP)):
                step = dt_ref[at, t : t + 1, columns]
                fed = dx_ref[at, t : t + 1, columns]
                grad = grad_ref[at, t : t + 1, columns]
                for i, (r, w) in enumerate(zip(rows, which)):
                    before = state_ref[base + t, r]
                    arriving = flows[r] + read[t][w] * grad
                    entry_term = arriving * fed
                    read_term = afters[r] * grad
                    fed_term = entry[t][w] * arriving
                    leaving = jnp.exp2(step * rate_ref[r]) * arriving
                    product = leaving * before
                    step_term = product * rate_ref[r]
                    rate_sum[i] = rate_sum[i] + product * step
                    flows[r] = leaving
                    afters[r] = before
                    fed_sums[t] = fed_term if i == 0 else fed_sums[t] + fed_term
                    step_sums[t] = step_term if i == 0 else step_sums[t] + step_term
                    for total, term in ((entry_sum[t], entry_term), (read_sum[t], read_term)):
                        if last:
                            total[0] = total[0] + jnp.where(left, term, 0.0)
                            total[1] = total[1] + jnp.where(left, 0.0, term)
                        else:
                            total[i] = term if total[i] is None else total[i] + term
            fed_out[at, :, columns] = fold_rows(fed_sums)
            step_out[at, :, columns] = fold_rows(step_sums)
            for i, r in enumerate(rows):
                rate_out[r] = rate_sum[i]
        for t in range(STEP):
            for i in range(2):
                entry_out[base + STEP - 1 - t, 8 * i : 8 * i + 8] = entry_sum[t][i]
                read_out[base + STEP - 1 - t, 8 * i : 8 * i + 8] = read_sum[t][i]
        return (tuple(flows), tuple(afters))

    flows, afters = lax.fori_loop(
        0,
        groups,
        group,
        (tuple(flow[r] for r in range(count)), tuple(after[r] for r in range(count))),
    )
    for r in range(count):
        flow[r] = flows[r]
        after[r] = afters[r]


def split_low(value):
    high = value.astype(jnp.bfloat16)
    return high, (value - high.astype(jnp.float32)).astype(jnp.bfloat16)


def dot(left, right):
    return jnp.dot(left, right, preferred_element_type=jnp.float32)


def dot_t(left, right):
    return lax.dot_general(left, right, (((1,), (1,)), ((), ())), preferred_element_type=jnp.float32)


def t_dot(left, right):
    return lax.dot_general(left, right, (((0,), (0,)), ((), ())), preferred_element_type=jnp.float32)


def live_rows(me_ref, length_ref, rows):
    slot = me_ref[0] * rows + lax.broadcasted_iota(jnp.int32, (rows, 1), 0)
    return slot < length_ref[0]


def router_rows(gains_ref):
    row = lax.broadcasted_iota(jnp.int32, gains_ref.shape, 0)
    return jnp.where(row < E, gains_ref[...], 0.0).astype(jnp.bfloat16)


def cut_kernel(parts, inside, cols, goal_ref, in_ref, up_ref, *rest):
    number = len(rest) // 2
    in_outs, up_outs, sems = (rest[:number], rest[number : 2 * number], rest[-1])
    copies = []
    for k in range(number):
        columns = pl.ds(pl.multiple_of(goal_ref[k] * cols, LANES), cols)
        copies.append(pltpu.make_async_copy(up_ref.at[:, :, columns], up_outs[k], sems.at[k]))
        copies[-1].start()
    for d in range(parts):
        for k in range(number):

            @pl.when(goal_ref[k] == d)
            def write():
                in_outs[k][:, :inside] = in_ref[:, d * inside : (d + 1) * inside]
                at = (parts + d) * inside
                in_outs[k][:, inside:] = in_ref[:, at : at + inside]

    for copy in copies:
        copy.wait()


def cut_weights(goal, in_weight, up_weight, parts, inside):
    slab = in_weight.shape[0]
    cols = up_weight.shape[2] // parts
    number = 3
    in_shape = jax.ShapeDtypeStruct((slab, 2 * inside), in_weight.dtype)
    up_shape = jax.ShapeDtypeStruct((up_weight.shape[0], slab, cols), up_weight.dtype)
    vmem, anywhere = (pl.BlockSpec(memory_space=pltpu.VMEM), pl.BlockSpec(memory_space=pl.ANY))
    outs = pl.pallas_call(
        functools.partial(cut_kernel, parts, inside, cols),
        in_specs=[pl.BlockSpec(memory_space=pltpu.SMEM), vmem, anywhere],
        out_specs=[vmem] * number + [anywhere] * number,
        out_shape=[in_shape] * number + [up_shape] * number,
        scratch_shapes=[pltpu.SemaphoreType.DMA((number,))],
        compiler_params=pltpu.CompilerParams(vmem_limit_bytes=24 * 2**20),
        name="cut_weights",
    )(goal, in_weight, up_weight)
    return outs[:number], outs[number:]


def to_power(value):
    return value / (1.0 + jnp.exp(-value))


def project_kernel(parts, inside, me_ref, source_ref, length_ref, *rest):
    normed_refs, weight_refs, rest = (rest[:parts], rest[parts : 2 * parts], rest[2 * parts :])
    taps_ref, bias_ref, select_ref, inner_out, gate_out, summed_out, conv_out, low_out, selected_out = rest[:9]
    normed, weight, shifted, sems = rest[9:]
    block = pl.program_id(0)
    me = me_ref[0]
    rows, slab = (normed_refs[0].shape[0], weight_refs[0].shape[0])

    @pl.when(block == 0)
    def fetch():
        copies = []
        for k in range(parts):
            at = pl.ds(pl.multiple_of(source_ref[k] * slab, 16), slab)
            copies.append(pltpu.make_async_copy(weight_refs[k], weight.at[at], sems.at[k]))
            at = pl.ds(pl.multiple_of((me ^ k) * rows, 16), rows)
            copies.append(pltpu.make_async_copy(normed_refs[k], normed.at[at], sems.at[parts + k]))
        for copy in copies:
            copy.start()
        for copy in copies:
            copy.wait()
        shifted[0:8] = jnp.zeros((8, inside), jnp.float32)

    start = pl.multiple_of(block * rows, 16)
    projected = jnp.dot(normed[pl.ds(start, rows)], weight[...], preferred_element_type=jnp.float32)
    slot = block * rows + lax.broadcasted_iota(jnp.int32, (rows, 1), 0)
    inner = jnp.where(slot < length_ref[0], projected[:, :inside], 0.0)
    gate_out[...] = projected[:, inside:]
    inner_out[...] = inner
    shifted[8:] = inner
    summed = bias_ref[...]
    for k in range(KW):
        summed = summed + taps_ref[k : k + 1] * shifted[8 - (KW - 1) + k : 8 - (KW - 1) + k + rows]
    shifted[0:8] = shifted[rows : rows + 8]
    summed_out[...] = summed
    value = to_power(summed)
    conv_out[...] = value
    low = value.astype(jnp.bfloat16)
    low_out[...] = low
    selected_out[...] = jnp.dot(low, select_ref[...], preferred_element_type=jnp.float32)


def project(me, source, length, normed_pieces, weight_pieces, taps, bias, select_wide):
    parts = len(normed_pieces)
    rows, width = normed_pieces[0].shape
    slab, both = weight_pieces[0].shape
    inside, picked = select_wide.shape
    total = rows * parts
    smem, anywhere = (pl.BlockSpec(memory_space=pltpu.SMEM), pl.BlockSpec(memory_space=pl.ANY))
    vmem = pl.BlockSpec(memory_space=pltpu.VMEM)
    row = pl.BlockSpec((rows, inside), lambda i: (i, 0))
    wide = jax.ShapeDtypeStruct((total, inside), jnp.float32)
    return pl.pallas_call(
        functools.partial(project_kernel, parts, inside),
        grid=(parts,),
        in_specs=[smem] * 3 + [anywhere] * (2 * parts) + [vmem] * 3,
        out_specs=[row] * 5 + [pl.BlockSpec((rows, picked), lambda i: (i, 0))],
        out_shape=[wide] * 4
        + [
            jax.ShapeDtypeStruct((total, inside), jnp.bfloat16),
            jax.ShapeDtypeStruct((total, picked), jnp.float32),
        ],
        scratch_shapes=[
            pltpu.VMEM((total, width), jnp.bfloat16),
            pltpu.VMEM((slab * parts, both), jnp.bfloat16),
            pltpu.VMEM((rows + 8, inside), jnp.float32),
            pltpu.SemaphoreType.DMA((2 * parts,)),
        ],
        compiler_params=pltpu.CompilerParams(vmem_limit_bytes=40 * 2**20),
        cost_estimate=pl.CostEstimate(flops=4 * 10**9, bytes_accessed=2**20, transcendentals=0),
        name="project",
    )(me, source, length, *normed_pieces, *weight_pieces, taps, bias, select_wide)


def live_slots(start, length_ref, rows):
    return start + lax.broadcasted_iota(jnp.int32, (rows, 1), 0) < length_ref[0]


def store_wide(ref, value):
    groups, _, width = ref.shape
    inside = value.shape[1]
    ref[:, :, :inside] = value.reshape(groups, STEP, inside)
    ref[:, :, inside:] = value[:, 2 * inside - width :].reshape(groups, STEP, width - inside)


def load_narrow(ref, inside):
    groups, _, width = ref.shape
    edge = 2 * inside - width
    value = ref[...].reshape(groups * STEP, width)
    return jnp.concatenate([value[:, :edge], value[:, edge:inside] + value[:, inside:]], axis=1)


def store_spread(entry_ref, read_ref, selected):
    turned = selected.T
    for t in range(selected.shape[0]):
        entry_ref[t] = jnp.broadcast_to(turned[R : R + NS, t : t + 1], (NS, LANES))
        read_ref[t] = jnp.broadcast_to(turned[R + NS : R + 2 * NS, t : t + 1], (NS, LANES))


def step_sizes(selected, weight_ref, bias_ref, live):
    low = selected.astype(jnp.bfloat16)
    pre = dot(low, weight_ref[...]) + bias_ref[...]
    soft = jnp.maximum(pre, 0.0) + jnp.log1p(jnp.exp(-jnp.abs(pre)))
    return low, pre, jnp.where(live, soft, 0.0)


def mixer_kernel(
    tiles, share, me_ref, length_ref, selected_ref, conv_ref, gate_ref, weight_ref, bias_ref, skip_ref, rate_ref, project_ref,
    state_ref, end_ref, mixed_out, gated_out, held_out, given_out,
    dt_ref, dx_ref, entry_ref, read_ref, out_ref, held,
):
    chunk, inside = conv_ref.shape
    step = pl.program_id(0)

    @pl.when(step == 0)
    def start():
        held[...] = jnp.zeros_like(held)

    selected, conv = (selected_ref[...], conv_ref[...])
    live = live_slots(step * chunk, length_ref, chunk)
    _, _, size = step_sizes(selected, weight_ref, bias_ref, live)
    store_wide(dt_ref, size)
    store_wide(dx_ref, size * conv)
    store_spread(entry_ref, read_ref, selected)
    scan_forward_chunk(tiles, dt_ref, dx_ref, entry_ref, read_ref, rate_ref, out_ref, state_ref, end_ref, held)
    mixed = load_narrow(out_ref, inside) + skip_ref[...] * conv
    mixed_out[...] = mixed
    gated = (mixed * to_power(gate_ref[...])).astype(jnp.bfloat16)
    gated_out[...] = gated
    part = dot(gated, project_ref[...])
    block = step // share
    rows = pl.ds(pl.multiple_of((step % share) * chunk, chunk), chunk)

    @pl.when(block % 2 == me_ref[0] % 2)
    def keep():
        held_out[0, rows] = part

    @pl.when(block % 2 != me_ref[0] % 2)
    def give():
        given_out[0, rows] = part.astype(jnp.bfloat16)


def mixer(me, length, selected, conv_out, zgate, step_wide, bias, skip, rate, out_weight, span, tiles):
    total, inside = conv_out.shape
    width = out_weight.shape[1]
    count = 2 * tiles + 1
    chunk = CHUNK
    wide = (tiles + 1) * LANES
    share = span // chunk
    smem, vmem = (pl.BlockSpec(memory_space=pltpu.SMEM), pl.BlockSpec(memory_space=pltpu.VMEM))
    row = pl.BlockSpec((chunk, inside), lambda i: (i, 0))
    part = pl.BlockSpec((1, span, width), lambda i: (i // (2 * share), 0, 0))
    f32, bf16 = (jnp.float32, jnp.bfloat16)
    return pl.pallas_call(
        functools.partial(mixer_kernel, tiles, share),
        grid=(total // chunk,),
        in_specs=[smem, smem, pl.BlockSpec((chunk, LANES), lambda i: (i, 0)), row, row] + [vmem] * 5,
        out_specs=[pl.BlockSpec((chunk, count, 8, LANES), lambda i: (i, 0, 0, 0)), vmem, row, row, part, part],
        out_shape=[
            jax.ShapeDtypeStruct((total, count, 8, LANES), f32),
            jax.ShapeDtypeStruct((count, 8, LANES), f32),
            jax.ShapeDtypeStruct((total, inside), f32),
            jax.ShapeDtypeStruct((total, inside), bf16),
            jax.ShapeDtypeStruct((2, span, width), f32),
            jax.ShapeDtypeStruct((2, span, width), bf16),
        ],
        scratch_shapes=[pltpu.VMEM((chunk // STEP, STEP, wide), f32)] * 2
        + [pltpu.VMEM((chunk, NS, LANES), f32)] * 2
        + [pltpu.VMEM((chunk // STEP, STEP, wide), f32), pltpu.VMEM((count, 8, LANES), f32)],
        compiler_params=pltpu.CompilerParams(vmem_limit_bytes=40 * 2**20),
        cost_estimate=pl.CostEstimate(flops=4 * 10**9, bytes_accessed=2**20, transcendentals=0),
        name="mixer",
    )(me, length, selected, conv_out, zgate, step_wide, bias, skip, rate, out_weight)


def row_sums(value):
    high, low = split_low(value)
    ones = jnp.ones((8, LANES), jnp.bfloat16)
    return dot_t(ones, high) + dot_t(ones, low)


def mixer_back_kernel(tiles, length_ref, *rest):
    (
        selected_ref, conv_ref, grad_ref, state_ref, end_ref, weight_ref, bias_ref, skip_ref, rate_ref,
        conv_out, rank_out, step_out, bias_out, skip_out, rate_out,
        dt_ref, dx_ref, mix_ref, entry_ref, read_ref, fed_ref, rise_ref, entry_parts, read_parts, flow, after,
    ) = rest
    chunk, inside = conv_ref.shape
    index = pl.program_id(0)
    step = pl.num_programs(0) - 1 - index

    @pl.when(index == 0)
    def start():
        flow[...] = jnp.zeros_like(flow)
        after[...] = end_ref[...]
        rate_out[...] = jnp.zeros_like(rate_out)
        step_out[...] = jnp.zeros_like(step_out)
        bias_out[...] = jnp.zeros_like(bias_out)
        skip_out[...] = jnp.zeros_like(skip_out)

    conv, grad_mixed = (conv_ref[...], grad_ref[...])
    skip_out[...] += jnp.sum(grad_mixed * conv, axis=0, keepdims=True)
    selected = selected_ref[...]
    live = live_slots(step * chunk, length_ref, chunk)
    low, pre, size = step_sizes(selected, weight_ref, bias_ref, live)
    store_wide(dt_ref, size)
    store_wide(dx_ref, size * conv)
    store_wide(mix_ref, grad_mixed)
    store_spread(entry_ref, read_ref, selected)
    scan_backward_chunk(
        tiles, dt_ref, dx_ref, mix_ref, entry_ref, read_ref, rate_ref, state_ref,
        fed_ref, rise_ref, entry_parts, read_parts, rate_out, flow, after,
    )
    fed = load_narrow(fed_ref, inside)
    grad_size = load_narrow(rise_ref, inside) * (1.0 / LOG2E) + fed * conv
    grad_pre = jnp.where(live, grad_size / (1.0 + jnp.exp(-pre)), 0.0)
    bias_out[...] += jnp.sum(grad_pre, axis=0, keepdims=True)
    grad_low = grad_pre.astype(jnp.bfloat16)
    rank = dot_t(grad_low, weight_ref[...])
    sums = [row_sums(part[...].reshape(chunk * NS, LANES)) for part in (entry_parts, read_parts)]
    lane = lax.broadcasted_iota(jnp.int32, (STEP, LANES), 1)
    for g in range(chunk // STEP):
        total = rank[g * STEP : (g + 1) * STEP]
        for i, part in enumerate(sums):
            start = R + i * NS
            moved = pltpu.roll(part[:, g * LANES : (g + 1) * LANES], start + NS, 1)
            moved = pltpu.roll(moved, 0, 1, stride=NS, stride_axis=0)
            total = jnp.where((lane >= start) & (lane < start + NS), moved, total)
        rank_out[g * STEP : (g + 1) * STEP] = total
    step_out[...] += t_dot(low, grad_low)
    conv_out[...] = fed * size + skip_ref[...] * grad_mixed


def mixer_back(length, selected, conv_out, grad_mixed, states, end, step_wide, bias, skip, rate, tiles):
    total, inside = conv_out.shape
    count = 2 * tiles + 1
    chunk = CHUNK
    steps = total // chunk
    wide = (tiles + 1) * LANES
    smem, vmem = (pl.BlockSpec(memory_space=pltpu.SMEM), pl.BlockSpec(memory_space=pltpu.VMEM))
    row = pl.BlockSpec((chunk, inside), lambda i: (steps - 1 - i, 0))
    lane = pl.BlockSpec((chunk, LANES), lambda i: (steps - 1 - i, 0))
    f32 = jnp.float32
    one = jax.ShapeDtypeStruct((1, inside), f32)
    return pl.pallas_call(
        functools.partial(mixer_back_kernel, tiles),
        grid=(steps,),
        in_specs=[smem, lane, row, row]
        + [pl.BlockSpec((chunk, count, 8, LANES), lambda i: (steps - 1 - i, 0, 0, 0))]
        + [vmem] * 5,
        out_specs=[row, lane] + [vmem] * 4,
        out_shape=[
            jax.ShapeDtypeStruct((total, inside), f32),
            jax.ShapeDtypeStruct((total, LANES), f32),
            jax.ShapeDtypeStruct((LANES, inside), f32),
            one,
            one,
            jax.ShapeDtypeStruct((count, 8, LANES), f32),
        ],
        scratch_shapes=[pltpu.VMEM((chunk // STEP, STEP, wide), f32)] * 3
        + [pltpu.VMEM((chunk, NS, LANES), f32)] * 2
        + [pltpu.VMEM((chunk // STEP, STEP, wide), f32)] * 2
        + [pltpu.VMEM((chunk, NS, LANES), f32)] * 2
        + [pltpu.VMEM((count, 8, LANES), f32)] * 2,
        compiler_params=pltpu.CompilerParams(vmem_limit_bytes=48 * 2**20),
        cost_estimate=pl.CostEstimate(flops=4 * 10**9, bytes_accessed=2**20, transcendentals=0),
        name="mixer_back",
    )(length, selected, conv_out, grad_mixed, states, end, step_wide, bias, skip, rate)


def gate_back_kernel(parts, pair, me_ref, source_ref, *rest):
    normed_refs, grad_refs, rest = (rest[:parts], rest[parts : 2 * parts], rest[2 * parts :])
    (
        gate_ref, mixed_ref, gated_ref, project_ref,
        mix_out, gate_out, gate_held, gate_given, out_held, out_given,
        normed, grads, lows, product, sems,
    ) = rest
    block = pl.program_id(0)
    rows, width = normed_refs[0].shape
    slab = width // parts
    me, odd, second = (me_ref[0], source_ref[parts], source_ref[parts + 1])

    @pl.when(block == 0)
    def fetch():
        copies = []
        for k in range(parts):
            at = pl.ds(pl.multiple_of((me ^ k) * rows, 16), rows)
            copies.append(pltpu.make_async_copy(normed_refs[k], normed.at[at], sems.at[k]))
            copies.append(pltpu.make_async_copy(grad_refs[k], grads.at[at], sems.at[parts + k]))
        for copy in copies:
            copy.start()
        for copy in copies:
            copy.wait()

    at = pl.ds(pl.multiple_of(block * rows, rows), rows)
    grad = grads[at]
    grad_gated = dot_t(grad, project_ref[...])
    gate = gate_ref[...]
    curve = 1.0 / (1.0 + jnp.exp(-gate))
    mix_out[...] = grad_gated * (gate * curve)
    low = (grad_gated * mixed_ref[...] * (curve * (1.0 + gate * (1.0 - curve)))).astype(jnp.bfloat16)
    gate_out[...] = low
    lows[at] = low

    @pl.when(block == parts - 1)
    def finish():
        product[...] = t_dot(normed[...], lows[...])
        for h in range(parts // 2):
            at = pl.ds(pl.multiple_of((2 * h + odd) * slab, 8), slab)
            gate_held[h] = product[at]
            at = pl.ds(pl.multiple_of((2 * h + 1 - odd) * slab, 8), slab)
            gate_given[h] = product[at].astype(jnp.bfloat16)
        product[...] = t_dot(grads[...], gated_ref[...])
        for h in range(width // (2 * pair)):
            at = pl.ds(pl.multiple_of((2 * h + second) * pair, 8), pair)
            out_held[h] = product[at]
            at = pl.ds(pl.multiple_of((2 * h + 1 - second) * pair, 8), pair)
            out_given[h] = product[at].astype(jnp.bfloat16)


def gate_back(me, source, normed_pieces, grad_pieces, zgate, mixed, gated, out_weight, pair):
    parts = len(normed_pieces)
    rows, width = normed_pieces[0].shape
    total, inside = gated.shape
    slab = width // parts
    smem, anywhere = (pl.BlockSpec(memory_space=pltpu.SMEM), pl.BlockSpec(memory_space=pl.ANY))
    vmem = pl.BlockSpec(memory_space=pltpu.VMEM)
    row = pl.BlockSpec((rows, inside), lambda i: (i, 0))
    f32, bf16 = (jnp.float32, jnp.bfloat16)
    gate_shape = (parts // 2, slab, inside)
    out_shape = (width // (2 * pair), pair, inside)
    return pl.pallas_call(
        functools.partial(gate_back_kernel, parts, pair),
        grid=(parts,),
        in_specs=[smem] * 2 + [anywhere] * (2 * parts) + [row] * 2 + [vmem] * 2,
        out_specs=[row] * 2 + [vmem] * 4,
        out_shape=[
            jax.ShapeDtypeStruct((total, inside), f32),
            jax.ShapeDtypeStruct((total, inside), bf16),
            jax.ShapeDtypeStruct(gate_shape, f32),
            jax.ShapeDtypeStruct(gate_shape, bf16),
            jax.ShapeDtypeStruct(out_shape, f32),
            jax.ShapeDtypeStruct(out_shape, bf16),
        ],
        scratch_shapes=[
            pltpu.VMEM((total, width), bf16),
            pltpu.VMEM((total, width), bf16),
            pltpu.VMEM((total, inside), bf16),
            pltpu.VMEM((width, inside), f32),
            pltpu.SemaphoreType.DMA((2 * parts,)),
        ],
        compiler_params=pltpu.CompilerParams(vmem_limit_bytes=48 * 2**20),
        cost_estimate=pl.CostEstimate(flops=4 * 10**9, bytes_accessed=2**20, transcendentals=0),
        name="gate_back",
    )(me, source, *normed_pieces, *grad_pieces, zgate, mixed, gated, out_weight)


def conv_back_kernel(parts, me_ref, source_ref, length_ref, *rest):
    normed_refs, rest = (rest[:parts], rest[parts:])
    (
        selected_ref, conv_ref, summed_ref, inner_ref, low_ref, taps_ref, select_ref,
        inner_out, inner_held, inner_given, select_out, taps_out, bias_out,
        normed, shifted, lows, total, sems,
    ) = rest
    index = pl.program_id(0)
    block = parts - 1 - index
    rows, inside = inner_ref.shape
    slab = normed.shape[1] // parts
    me = me_ref[0]
    odd = source_ref[parts]

    def fetched(k):
        at = pl.ds(pl.multiple_of((me ^ k) * rows, 16), rows)
        return pltpu.make_async_copy(normed_refs[k], normed.at[at], sems.at[k])

    @pl.when(index == 0)
    def fetch():
        for k in range(parts):
            fetched(k).start()
        shifted[rows:] = jnp.zeros((8, inside), jnp.float32)
        select_out[...] = jnp.zeros_like(select_out)
        taps_out[...] = jnp.zeros_like(taps_out)
        bias_out[...] = jnp.zeros_like(bias_out)

    selected = selected_ref[...]
    summed = summed_ref[...]
    curve = 1.0 / (1.0 + jnp.exp(-summed))
    grad_summed = (conv_ref[...] + dot_t(selected, select_ref[...])) * (curve * (1.0 + summed * (1.0 - curve)))
    select_out[...] += t_dot(selected, low_ref[...])
    bias_out[...] += jnp.sum(grad_summed, axis=0, keepdims=True)
    shifted[:rows] = grad_summed
    inner = inner_ref[...]
    grad_inner = jnp.zeros((rows, inside), jnp.float32)
    for k in range(KW):
        moved = shifted[KW - 1 - k : KW - 1 - k + rows]
        grad_inner = grad_inner + taps_ref[k : k + 1] * moved
        taps_out[k : k + 1] += jnp.sum(inner * moved, axis=0, keepdims=True)
    shifted[rows:] = shifted[0:8]
    live = live_slots(block * rows, length_ref, rows)
    low = jnp.where(live, grad_inner, 0.0).astype(jnp.bfloat16)
    inner_out[...] = low

    lows[pl.ds(pl.multiple_of(block * rows, rows), rows)] = low

    @pl.when(block == 0)
    def finish():
        for k in range(parts):
            fetched(k).wait()
        total[...] = t_dot(normed[...], lows[...])
        for h in range(parts // 2):
            at = pl.ds(pl.multiple_of((2 * h + odd) * slab, 8), slab)
            inner_held[h] = total[at]
            at = pl.ds(pl.multiple_of((2 * h + 1 - odd) * slab, 8), slab)
            inner_given[h] = total[at].astype(jnp.bfloat16)


def conv_back(me, source, length, normed_pieces, grad_selected, conv_grad, summed, inner, conv_low, taps, select_wide):
    parts = len(normed_pieces)
    rows, width = normed_pieces[0].shape
    slab = width // parts
    total, inside = inner.shape
    smem, anywhere = (pl.BlockSpec(memory_space=pltpu.SMEM), pl.BlockSpec(memory_space=pl.ANY))
    vmem = pl.BlockSpec(memory_space=pltpu.VMEM)
    row = pl.BlockSpec((rows, inside), lambda i: (parts - 1 - i, 0))
    f32, bf16 = (jnp.float32, jnp.bfloat16)
    return pl.pallas_call(
        functools.partial(conv_back_kernel, parts),
        grid=(parts,),
        in_specs=[smem] * 3
        + [anywhere] * parts
        + [pl.BlockSpec((rows, LANES), lambda i: (parts - 1 - i, 0))]
        + [row] * 4
        + [vmem] * 2,
        out_specs=[row] + [vmem] * 5,
        out_shape=[
            jax.ShapeDtypeStruct((total, inside), bf16),
            jax.ShapeDtypeStruct((2, slab, inside), f32),
            jax.ShapeDtypeStruct((2, slab, inside), bf16),
            jax.ShapeDtypeStruct((LANES, inside), f32),
            jax.ShapeDtypeStruct((8, inside), f32),
            jax.ShapeDtypeStruct((1, inside), f32),
        ],
        scratch_shapes=[
            pltpu.VMEM((total, width), bf16),
            pltpu.VMEM((rows + 8, inside), f32),
            pltpu.VMEM((total, inside), bf16),
            pltpu.VMEM((width, inside), f32),
            pltpu.SemaphoreType.DMA((parts,)),
        ],
        compiler_params=pltpu.CompilerParams(vmem_limit_bytes=48 * 2**20),
        cost_estimate=pl.CostEstimate(flops=4 * 10**9, bytes_accessed=2**20, transcendentals=0),
        name="conv_back",
    )(me, source, length, *normed_pieces, grad_selected, conv_grad, summed, inner, conv_low, taps, select_wide)


def project_back_kernel(parts, me_ref, source_ref, *rest):
    normed_refs, weight_refs, rest = (rest[:parts], rest[parts : 2 * parts], rest[2 * parts :])
    inner_ref, gate_ref, held_out, given_out, gain_out, normed, weight, projected, sems = rest
    block = pl.program_id(0)
    rows, inside = inner_ref.shape
    slab = weight_refs[0].shape[0]
    me = me_ref[0]

    @pl.when(block == 0)
    def fetch():
        copies = []
        for k in range(parts):
            at = pl.ds(pl.multiple_of(source_ref[k] * slab, 16), slab)
            copies.append(pltpu.make_async_copy(weight_refs[k], weight.at[at], sems.at[k]))
            at = pl.ds(pl.multiple_of((me ^ k) * rows, 16), rows)
            copies.append(pltpu.make_async_copy(normed_refs[k], normed.at[at], sems.at[parts + k]))
        for copy in copies:
            copy.start()
        gain_out[...] = jnp.zeros_like(gain_out)
        for copy in copies:
            copy.wait()

    projected[:, :inside] = inner_ref[...]
    projected[:, inside:] = gate_ref[...]
    normed_rows = normed[pl.ds(pl.multiple_of(block * rows, rows), rows)]
    grad_normed = dot_t(projected[...], weight[...])
    gain_out[...] += jnp.sum(grad_normed * normed_rows.astype(jnp.float32), axis=0, keepdims=True)

    @pl.when(block % 2 == me % 2)
    def keep():
        held_out[0] = grad_normed

    @pl.when(block % 2 != me % 2)
    def give():
        given_out[0] = grad_normed.astype(jnp.bfloat16)


def project_back(me, source, normed_pieces, weight_pieces, inner_grad, gate_grad):
    parts = len(normed_pieces)
    rows, width = normed_pieces[0].shape
    slab, both = weight_pieces[0].shape
    total, inside = inner_grad.shape
    smem, anywhere = (pl.BlockSpec(memory_space=pltpu.SMEM), pl.BlockSpec(memory_space=pl.ANY))
    vmem = pl.BlockSpec(memory_space=pltpu.VMEM)
    row = pl.BlockSpec((rows, inside), lambda i: (i, 0))
    part = pl.BlockSpec((1, rows, width), lambda i: (i // 2, 0, 0))
    f32, bf16 = (jnp.float32, jnp.bfloat16)
    return pl.pallas_call(
        functools.partial(project_back_kernel, parts),
        grid=(parts,),
        in_specs=[smem] * 2 + [anywhere] * (2 * parts) + [row] * 2,
        out_specs=[part, part, vmem],
        out_shape=[
            jax.ShapeDtypeStruct((2, rows, width), f32),
            jax.ShapeDtypeStruct((2, rows, width), bf16),
            jax.ShapeDtypeStruct((1, width), f32),
        ],
        scratch_shapes=[
            pltpu.VMEM((total, width), bf16),
            pltpu.VMEM((slab * parts, both), bf16),
            pltpu.VMEM((rows, both), bf16),
            pltpu.SemaphoreType.DMA((2 * parts,)),
        ],
        compiler_params=pltpu.CompilerParams(vmem_limit_bytes=40 * 2**20),
        cost_estimate=pl.CostEstimate(flops=4 * 10**9, bytes_accessed=2**20, transcendentals=0),
        name="project_back",
    )(me, source, *normed_pieces, *weight_pieces, inner_grad, gate_grad)


def norm_kernel(parts, me_ref, tokens_ref, *rest):
    small_refs, normed_out, gains_out = (rest[:parts], rest[parts], rest[parts + 1])
    slab = small_refs[0].shape[1]
    for m in range(parts):

        @pl.when(me_ref[0] == m)
        def lay():
            for p in range(parts):
                gains_out[:, p * slab : (p + 1) * slab] = small_refs[p ^ m][...]

    tokens = tokens_ref[...]
    scale = lax.rsqrt(jnp.mean(tokens * tokens, axis=-1, keepdims=True) + EPSILON)
    normed_out[...] = (tokens * scale * gains_out[2:3]).astype(jnp.bfloat16)


def norm_rows(me, tokens, small_pieces):
    parts = len(small_pieces)
    smem, vmem = (pl.BlockSpec(memory_space=pltpu.SMEM), pl.BlockSpec(memory_space=pltpu.VMEM))
    return pl.pallas_call(
        functools.partial(norm_kernel, parts),
        in_specs=[smem] + [vmem] * (1 + parts),
        out_specs=[vmem] * 2,
        out_shape=[
            jax.ShapeDtypeStruct(tokens.shape, jnp.bfloat16),
            jax.ShapeDtypeStruct((small_pieces[0].shape[0], tokens.shape[1]), jnp.float32),
        ],
        compiler_params=pltpu.CompilerParams(vmem_limit_bytes=16 * 2**20),
        name="norm_rows",
    )(me, tokens, *small_pieces)


def route_kernel(
    me_ref, length_ref, tokens_ref, near_ref, got_ref, gains_ref, order_ref, routes_ref,
    first_out, normed_out, sent_out, probs_out,
):
    rows, width = tokens_ref.shape
    first = tokens_ref[...] + near_ref[...] + got_ref[...].astype(jnp.float32)
    first_out[...] = first
    scale = lax.rsqrt(jnp.mean(first * first, axis=-1, keepdims=True) + EPSILON)
    normed = (first * scale * gains_ref[3:4]).astype(jnp.bfloat16)
    normed_out[...] = normed
    logits = dot_t(normed, router_rows(gains_ref))
    gap = logits[:, 0:1] - logits[:, 1:2]
    prob_zero = 1.0 / (1.0 + jnp.exp(-gap))
    prob_one = 1.0 / (1.0 + jnp.exp(gap))
    lane = lax.broadcasted_iota(jnp.int32, (rows, LANES), 1)
    probs_out[...] = jnp.where(lane == 0, prob_zero, jnp.where(lane == 1, prob_one, 0.0))
    gate = jnp.where(routes_ref[...] == 0, prob_zero, prob_one)
    gate = jnp.where(live_rows(me_ref, length_ref, rows), gate, 0.0)
    high, low = split_low(gate)
    high, low = (high.astype(jnp.float32), low.astype(jnp.float32))
    gates = jnp.where(lane == 0, high, jnp.where(lane == 1, low, 0.0)).astype(jnp.bfloat16)
    sent_out[:, :width] = dot(order_ref[...], normed).astype(jnp.bfloat16)
    sent_out[:, width:] = dot(order_ref[...], gates).astype(jnp.bfloat16)


def route(me, length, tokens, near, got, gains, order, routes):
    rows, width = tokens.shape
    smem, vmem = (pl.BlockSpec(memory_space=pltpu.SMEM), pl.BlockSpec(memory_space=pltpu.VMEM))
    return pl.pallas_call(
        route_kernel,
        in_specs=[smem, smem] + [vmem] * 6,
        out_specs=[vmem] * 4,
        out_shape=[
            jax.ShapeDtypeStruct((rows, width), jnp.float32),
            jax.ShapeDtypeStruct((rows, width), jnp.bfloat16),
            jax.ShapeDtypeStruct((rows, width + LANES), jnp.bfloat16),
            jax.ShapeDtypeStruct((rows, LANES), jnp.float32),
        ],
        compiler_params=pltpu.CompilerParams(vmem_limit_bytes=32 * 2**20),
        name="route",
    )(me, length, tokens, near, got, gains, order, routes)


def expert_kernel(parts, cap, steps, me_ref, source_ref, counts_ref, *rest):
    sent_refs, cot_refs, up_refs = (rest[:parts], rest[parts : 2 * parts], rest[2 * parts : 3 * parts])
    (
        down_ref, grad_held, grad_given, out_held, out_given, packed,
    ) = rest[3 * parts : 3 * parts + 6]
    rows, cots, up, down, rows_t, cots_t, scale, dots, grad_sum, out_sum, product, sems = rest[3 * parts + 6 :]
    step = pl.program_id(0)
    expert, tile = (step // steps, step % steps)
    span, width = cots.shape[1:]
    slab = up_refs[0].shape[1]
    offset = span - cap
    count = parts * cap
    me = me_ref[0]

    def weights(e):
        base = 2 * parts + e * (parts + 1)
        copies = [pltpu.make_async_copy(down_ref.at[e], down.at[e], sems.at[base])]
        for k in range(parts):
            at = pl.ds(pl.multiple_of(source_ref[k] * slab, 16), slab)
            copies.append(pltpu.make_async_copy(up_refs[k].at[e], up.at[e, at], sems.at[base + 1 + k]))
        return copies

    @pl.when(step == 0)
    def fetch():
        copies = []
        for k in range(parts):
            copies.append(pltpu.make_async_copy(sent_refs[k], rows.at[me ^ k], sems.at[k]))
            copies.append(pltpu.make_async_copy(cot_refs[k], cots.at[me ^ k], sems.at[parts + k]))
        for copy in copies:
            copy.start()
        for e in range(2):
            for copy in weights(e):
                copy.start()
        grad_sum[...] = jnp.zeros_like(grad_sum)
        out_sum[...] = jnp.zeros_like(out_sum)
        dots[...] = jnp.zeros_like(dots)
        for copy in copies:
            copy.wait()

    at = pl.ds(pl.multiple_of(expert * offset, 16), cap)
    mine = rows[:, at, :width].reshape(count, width)
    cot = cots[:, at].reshape(count, width)

    @pl.when(tile == 0)
    def turn():
        rows_t[...] = mine.T
        cots_t[...] = cot.T
        slot = lax.broadcasted_iota(jnp.int32, (cap, LANES), 0)
        for b in range(parts):
            gates = rows[b, at, width:].astype(jnp.float32)
            gate = gates[:, 0:1] + gates[:, 1:2]
            first = slot < counts_ref[b]
            later = slot + offset >= counts_ref[b]
            live = jnp.where(expert == 0, first.astype(jnp.float32), later.astype(jnp.float32))
            scale[b * cap : (b + 1) * cap] = live * gate
        for e in range(2):

            @pl.when(expert == e)
            def arrive():
                for copy in weights(e):
                    copy.wait()

    columns = pl.ds(pl.multiple_of(tile * FTILE, FTILE), FTILE)
    up_tile = up[expert, :, columns]
    down_tile = down[expert, columns, :]
    weight = scale[...][:, 0:1]
    pre = dot(mine, up_tile)
    grad_hidden = dot_t(cot, down_tile)
    square = pre * pre
    bend = jnp.tanh(0.7978845608028654 * pre * (1.0 + 0.044715 * square))
    rise = 0.5 * (1.0 + bend)
    slope = rise + 0.5 * pre * (1.0 - bend * bend) * (0.7978845608028654 * (1.0 + 0.134145 * square))
    hidden = (weight * (pre * rise)).astype(jnp.bfloat16)
    grad_pre = (weight * slope * grad_hidden).astype(jnp.bfloat16)
    part = jnp.sum(hidden.astype(jnp.float32) * grad_hidden, axis=1, keepdims=True)
    dots[:, at] += jnp.broadcast_to(part, (count, LANES)).reshape(parts, cap, LANES)
    out_sum[:, at] += dot(hidden, down_tile).reshape(parts, cap, width)
    grad_sum[:, at] += dot_t(grad_pre, up_tile).reshape(parts, cap, width)
    product[...] = dot(rows_t[...], grad_pre)
    fours = packed.shape[0]
    inside = packed.shape[-1] // LANES
    share = width // (fours * parts)
    pieces = []
    for q in range(FTILE // LANES):
        piece = tile * (FTILE // LANES) + q
        pieces.append((piece // inside, pl.ds(pl.multiple_of(piece % inside * LANES, LANES), LANES)))
    up_rows = pl.ds(pl.multiple_of(expert * slab, 16), slab)
    for q, (block, lanes) in enumerate(pieces):
        for r in range(parts):
            taken = product[r * slab : (r + 1) * slab, q * LANES : (q + 1) * LANES]
            packed[block, r, up_rows, lanes] = taken.astype(jnp.bfloat16)
    product[...] = dot(cots_t[...], hidden)
    base = 2 * slab
    for q, (block, lanes) in enumerate(pieces):
        down_rows = pl.ds(pl.multiple_of(base + (expert * fours + block) * share, 16), share)
        for g in range(fours * parts):
            taken = product[g * share : (g + 1) * share, q * LANES : (q + 1) * LANES]
            packed[g // parts, g % parts, down_rows, lanes] = taken.astype(jnp.bfloat16)

    @pl.when(step == pl.num_programs(0) - 1)
    def finish():
        for b in range(parts):

            @pl.when(me % 2 == b % 2)
            def hold():
                grad_held[b // 2, :, :width] = grad_sum[b]
                grad_held[b // 2, :, width:] = dots[b]
                out_held[b // 2] = out_sum[b]

            @pl.when(me % 2 != b % 2)
            def give():
                grad_given[b // 2, :, :width] = grad_sum[b].astype(jnp.bfloat16)
                grad_given[b // 2, :, width:] = dots[b].astype(jnp.bfloat16)
                out_given[b // 2] = out_sum[b].astype(jnp.bfloat16)


def experts(me, source, counts, sent_pieces, cot_pieces, up_pieces, down_weight, fours):
    parts = len(sent_pieces)
    span, width = cot_pieces[0].shape
    number, hid = down_weight.shape[:2]
    steps = hid // FTILE
    slab = up_pieces[0].shape[1]
    smem, anywhere = (pl.BlockSpec(memory_space=pltpu.SMEM), pl.BlockSpec(memory_space=pl.ANY))
    vmem = pl.BlockSpec(memory_space=pltpu.VMEM)
    f32, bf16 = (jnp.float32, jnp.bfloat16)
    packed = (fours, parts, 2 * number * slab, hid // fours)
    count = parts * CAP
    return pl.pallas_call(
        functools.partial(expert_kernel, parts, CAP, steps),
        grid=(number * steps,),
        in_specs=[smem] * 3 + [anywhere] * (3 * parts + 1),
        out_specs=[vmem] * 5,
        out_shape=[
            jax.ShapeDtypeStruct((2, span, width + LANES), f32),
            jax.ShapeDtypeStruct((2, span, width + LANES), bf16),
            jax.ShapeDtypeStruct((2, span, width), f32),
            jax.ShapeDtypeStruct((2, span, width), bf16),
            jax.ShapeDtypeStruct(packed, bf16),
        ],
        scratch_shapes=[
            pltpu.VMEM((parts, span, width + LANES), bf16),
            pltpu.VMEM((parts, span, width), bf16),
            pltpu.VMEM((number, slab * parts, hid), bf16),
            pltpu.VMEM((number, hid, width), bf16),
            pltpu.VMEM((width, count), bf16),
            pltpu.VMEM((width, count), bf16),
            pltpu.VMEM((count, LANES), f32),
            pltpu.VMEM((parts, span, LANES), f32),
            pltpu.VMEM((parts, span, width), f32),
            pltpu.VMEM((parts, span, width), f32),
            pltpu.VMEM((width, FTILE), f32),
            pltpu.SemaphoreType.DMA((2 * parts + 2 * (parts + 1),)),
        ],
        compiler_params=pltpu.CompilerParams(vmem_limit_bytes=60 * 2**20),
        cost_estimate=pl.CostEstimate(flops=4 * 10**9, bytes_accessed=2**20, transcendentals=0),
        name="experts",
    )(me, source, counts, *sent_pieces, *cot_pieces, *up_pieces, down_weight)


def return_kernel(
    me_ref, length_ref, near_ref, got_ref, order_ref, normed_ref, probs_ref, routes_ref, first_ref, cot_ref, gains_ref,
    grad_out, low_out, gain_out, router_out,
):
    rows, width = first_ref.shape
    grad = near_ref[...] + got_ref[...].astype(jnp.float32)
    high, low = split_low(grad)
    grad = dot(order_ref[...], high) + dot(order_ref[...], low)
    lane = lax.broadcasted_iota(jnp.int32, (rows, LANES), 1)
    chosen = (lane == routes_ref[...]).astype(jnp.float32)
    grad_logits = (grad[:, width : width + 1] * (chosen - probs_ref[...])).astype(jnp.bfloat16)
    grad_normed = grad[:, :width] + dot(grad_logits[:, :NS], router_rows(gains_ref))
    router_out[...] = t_dot(grad_logits, normed_ref[...])[0:8]
    first = first_ref[...]
    scale = lax.rsqrt(jnp.mean(first * first, axis=-1, keepdims=True) + EPSILON)
    unit = first * scale
    gain_out[...] = jnp.sum(grad_normed * unit, axis=0, keepdims=True)
    pulled = grad_normed * gains_ref[3:4]
    pulled = scale * (pulled - unit * jnp.mean(pulled * unit, axis=-1, keepdims=True))
    total = jnp.where(live_rows(me_ref, length_ref, rows), cot_ref[...], 0.0) + pulled
    grad_out[...] = total
    low_out[...] = total.astype(jnp.bfloat16)


def return_rows(me, length, *operands):
    rows, width = operands[6].shape
    smem, vmem = (pl.BlockSpec(memory_space=pltpu.SMEM), pl.BlockSpec(memory_space=pltpu.VMEM))
    return pl.pallas_call(
        return_kernel,
        in_specs=[smem, smem] + [vmem] * 9,
        out_specs=[vmem] * 4,
        out_shape=[
            jax.ShapeDtypeStruct((rows, width), jnp.float32),
            jax.ShapeDtypeStruct((rows, width), jnp.bfloat16),
            jax.ShapeDtypeStruct((1, width), jnp.float32),
            jax.ShapeDtypeStruct((8, width), jnp.float32),
        ],
        compiler_params=pltpu.CompilerParams(vmem_limit_bytes=32 * 2**20),
        name="return_rows",
    )(me, length, *operands)


def finish_kernel(
    me_ref, length_ref, near_ref, got_ref, out_near_ref, out_got_ref, order_ref, first_ref, grad_ref, tokens_ref, gains_ref,
    result_out, grad_out,
):
    rows = tokens_ref.shape[0]
    grad = near_ref[...] + got_ref[...].astype(jnp.float32)
    tokens = tokens_ref[...]
    scale = lax.rsqrt(jnp.mean(tokens * tokens, axis=-1, keepdims=True) + EPSILON)
    unit = tokens * scale
    pulled = grad * gains_ref[2:3]
    grad_out[...] = grad_ref[...] + scale * (pulled - unit * jnp.mean(pulled * unit, axis=-1, keepdims=True))
    high, low = split_low(out_near_ref[...] + out_got_ref[...].astype(jnp.float32))
    added = dot(order_ref[...], high) + dot(order_ref[...], low)
    result_out[...] = jnp.where(live_rows(me_ref, length_ref, rows), first_ref[...] + added, 0.0)


def finish_rows(me, length, *operands):
    shape = operands[5].shape
    smem, vmem = (pl.BlockSpec(memory_space=pltpu.SMEM), pl.BlockSpec(memory_space=pltpu.VMEM))
    return pl.pallas_call(
        finish_kernel,
        in_specs=[smem, smem] + [vmem] * 9,
        out_specs=[vmem] * 2,
        out_shape=[jax.ShapeDtypeStruct(shape, jnp.float32)] * 2,
        compiler_params=pltpu.CompilerParams(vmem_limit_bytes=32 * 2**20),
        name="finish_rows",
    )(me, length, *operands)


def body(
    tokens,
    routes,
    lengths,
    cotangent,
    in_weight,
    select_weight,
    step_weight,
    out_weight,
    router_weight,
    up_weight,
    down_weight,
    conv_weight,
    conv_bias,
    step_bias,
    decay_log,
    skip_gain,
    mixer_gain,
    expert_gain,
):
    f32, bf16 = (jnp.float32, jnp.bfloat16)
    span, width = tokens.shape
    groups, parts = (lax.axis_size("grp"), lax.axis_size("shard"))
    me, group = (lax.axis_index("shard"), lax.axis_index("grp"))
    total = span * parts
    inside = conv_bias.shape[0]
    tiles = inside // LANES
    slab = in_weight.shape[0]
    hidden_cols = up_weight.shape[2] // parts
    share = width // groups
    bits = [2**i for i in range(groups.bit_length() - 1)]
    down_bit = 2 if share % 8 == 0 else bits[-1]
    pair = 2 * share if share % 8 == 0 else width // 2
    odd, second = (group % 2, (group // down_bit) % 2)
    me_one = jnp.full((1,), me, jnp.int32)
    source = [me, me ^ 1, me ^ (2 + odd), me ^ (3 - odd), odd, second]
    source = jnp.stack(source).astype(jnp.int32)

    first = (routes[:, 0] == 0).astype(jnp.int32)
    count_first = jnp.sum(first)
    small = jnp.concatenate(
        [
            router_weight.astype(f32).T,
            mixer_gain.astype(f32)[None],
            expert_gain.astype(f32)[None],
            jnp.full((1, slab), count_first, jnp.int32).astype(f32),
            jnp.zeros((11, slab), f32),
        ],
        axis=0,
    )
    small = [small] + [swap(small, k) for k in range(1, parts)]
    in_pieces, up_pieces = cut_weights(source[:3], in_weight, up_weight, parts, inside)
    in_pieces = share_pieces(in_pieces)
    normed, gains = norm_rows(me_one, tokens, small)
    normed_pieces = gather_pieces(normed)
    counts = gains[4].reshape(parts, slab)[:, 0].astype(jnp.int32)

    goal = jnp.where(first > 0, jnp.cumsum(first), count_first + jnp.cumsum(1 - first)) - 1
    slots = jnp.arange(span, dtype=jnp.int32)
    order = (slots[:, None] == goal[None, :]).astype(bf16)
    order_t = (goal[:, None] == slots[None, :]).astype(bf16)
    live = (me * span + slots < lengths[0])[:, None]
    cots = matmul(order, jnp.where(live, cotangent, 0.0).astype(bf16)).astype(bf16)
    cot_pieces = gather_pieces(cots)

    taps = conv_weight.astype(f32)
    spare = LANES - select_weight.shape[1]
    select_wide = jnp.pad(select_weight, ((0, 0), (0, spare)))
    inner, zgate, summed, conv_out, conv_low, selected = project(
        me_one,
        source,
        lengths,
        normed_pieces,
        in_pieces,
        taps,
        conv_bias.astype(f32)[None, :],
        select_wide,
    )
    selected = tie(selected + swap(selected, 1), cot_pieces[2])
    selected = selected + swap(selected, 2)
    up_pieces = share_pieces([up_pieces[0], up_pieces[1], tie(up_pieces[2], selected)])
    step_wide = jnp.pad(step_weight, ((0, LANES - R), (0, 0)))
    step_row = step_bias.astype(f32)[None, :]
    decay = -jnp.exp(decay_log.astype(f32))
    rate = pack(decay * LOG2E, tiles)
    skip = skip_gain.astype(f32)[None, :]
    states, end, mixed, gated, held, given = mixer(
        me_one, lengths, selected, conv_out, zgate, step_wide, step_row, skip, rate, out_weight, span, tiles
    )
    near, given = scatter_near(held, tie(given, up_pieces[2]))
    first_sum, normed_two, sent, probs = route(
        me_one, lengths, tokens, near, swap(given, 2), gains, order, routes
    )
    fours, eights = (groups // 4, groups // 8)
    fine = hidden_cols // fours % LANES == 0 and share % 16 == 0
    grad_held, grad_given, out_held, out_given, packed = experts(
        me_one, source, counts, gather_pieces(sent), cot_pieces, up_pieces, down_weight, fours if fine else 1
    )
    up_cols = hidden_cols // fours
    if not fine:
        up_rows = packed[0, :, : E * slab].reshape(parts, E * slab, fours, up_cols).transpose(2, 0, 1, 3)
        down_rows = packed[0, :, E * slab :].reshape(parts, E, fours, share, fours, up_cols)
        down_rows = down_rows.transpose(2, 0, 1, 4, 3, 5).reshape(fours, parts, E * fours * share, up_cols)
        down_rows = down_rows.swapaxes(0, 1).reshape(fours, parts, E * fours * share, up_cols)
        packed = jnp.concatenate([up_rows, down_rows], axis=2)
    packed = packed.reshape(groups, 2 * E * slab, up_cols)
    packed = lax.psum_scatter(packed, "grp", scatter_dimension=0, tiled=True)
    up_sum, down_sum = (packed[:, : E * slab], packed[:, E * slab :])
    near, given = scatter_near(grad_held, grad_given)
    grad_first, grad_first_low, expert_gain_grad, router_grad = return_rows(
        me_one,
        lengths,
        near,
        swap(given, 2),
        order_t,
        normed_two,
        probs,
        routes,
        first_sum,
        cotangent,
        gains,
    )
    grad_pieces = gather_pieces(grad_first_low)
    top = bits[-1]
    out_bits = [bit for bit in bits[:0:-1] if bit != down_bit]
    blocks = (groups // 4, 2, share, inside)
    grad_mixed, grad_zgate, gate_held, gate_given, out_grad_held, out_grad_given = gate_back(
        me_one, source, normed_pieces, grad_pieces, zgate, mixed, gated, out_weight, pair
    )
    gate_got, out_grad_got = (swap_groups(gate_given, 1), swap_groups(out_grad_given, down_bit))
    conv_part, grad_selected, step_grad, step_bias_grad, skip_grad, rate_grad = mixer_back(
        lengths, selected, conv_out, grad_mixed, states, end, step_wide, step_row, skip, rate, tiles
    )
    chip_selected = grad_selected + swap(grad_selected, 1)
    gate_held, gate_given = halve((gate_held, gate_got), 0, 2, chip_selected)
    gate_got = swap_groups(gate_given, 2)
    out_parts = (out_grad_held.reshape(blocks), out_grad_got.reshape(blocks))
    out_grad_held, out_grad_given = halve(out_parts, 1, 1, chip_selected)
    out_grad_got = swap_groups(out_grad_given, 1)

    def up_home(g, s):
        return (s * fours + g // 4) * parts + g % 4

    def in_home(g, s):
        half, k = (g // (groups // 2), (g // 4) % eights)
        return (half * (groups // 2) + s * eights + k) * parts + g % 4

    both_axes = ("grp", "shard")
    places = [(g, s) for g in range(groups) for s in range(parts)]
    up_sum = lax.ppermute(tie(up_sum, chip_selected), both_axes, [(g * parts + s, up_home(g, s)) for g, s in places])
    grad_selected = (chip_selected + swap(chip_selected, 2)).astype(bf16)
    inner_grad, inner_held, inner_given, select_grad, conv_grad, conv_bias_grad = conv_back(
        me_one,
        source,
        lengths,
        normed_pieces,
        grad_selected,
        conv_part,
        summed,
        inner,
        conv_low,
        taps,
        select_wide,
    )
    inner_got = swap_groups(inner_given, 1)
    held, given, mixer_part = project_back(
        me_one, source, normed_pieces, in_pieces, inner_grad, grad_zgate
    )
    inner_held, inner_given = halve((inner_held, inner_got), 0, 2, given)
    inner_got = swap_groups(inner_given, 2)
    gate_sum = join(gate_held, gate_got, inner_held)
    for bit in out_bits:
        out_grad_held, out_grad_given = halve((out_grad_held, out_grad_got), 0, bit, inner_held)
        out_grad_got = swap_groups(out_grad_given, bit)
    shared = jnp.concatenate([router_grad[0:E], expert_gain_grad, mixer_part / gains[2:3]], axis=0)
    shared = shared + swap(shared, 1)
    shared = tie(shared + swap(shared, 2), inner_held)
    shared = lax.dynamic_slice_in_dim(shared, me * slab, slab, 1)
    decay_grad = decay * unpack(rate_grad, tiles)
    picked = select_weight.shape[1]
    few = [
        select_grad[:picked],
        conv_grad[:KW],
        conv_bias_grad,
        step_grad[:R],
        decay_grad,
        step_bias_grad,
        skip_grad,
        shared.reshape(2, inside),
    ]
    starts = [0]
    for part in few:
        starts.append(starts[-1] + part.shape[0])
    few = jnp.concatenate(few, axis=0).astype(bf16)
    few_got = swap_groups(few, 1)
    near, given = scatter_near(held, given, inner_held)
    got = swap(given, 2)
    out_near, out_given = scatter_near(out_held, out_given, inner_held)
    out_got = swap(out_given, 2)
    few = join(few, few_got, given, out_given).astype(bf16)
    few_got = swap_groups(few, 2)

    inner_sum = join(inner_held, inner_got, few)
    for bit in bits[-2:1:-1]:
        inner_held, inner_given = halve(inner_sum, 2, bit)
        inner_sum = join(inner_held, swap_groups(inner_given, bit))
        gate_held, gate_given = halve(gate_sum, 2, bit)
        gate_sum = join(gate_held, swap_groups(gate_given, bit))
    upper = group >= top
    own = jnp.where(upper, gate_sum, inner_sum).reshape(slab, inside // eights).astype(bf16)
    other = jnp.where(upper, inner_sum, gate_sum).reshape(slab, inside // eights).astype(bf16)
    own = lax.ppermute(own, both_axes, [(g * parts + s, in_home(g, s)) for g, s in places])
    other = lax.ppermute(other, both_axes, [(g * parts + s, in_home(g ^ top, s)) for g, s in places])
    few = join(few, few_got, inner_sum).astype(bf16)
    few_got = swap_groups(few, bits[2])
    out_sum = join(out_grad_held, out_grad_got, inner_sum).reshape(share, inside)
    result, tokens_grad = finish_rows(
        tie(me_one, few),
        lengths,
        near,
        got,
        out_near,
        out_got,
        order_t,
        first_sum,
        grad_first,
        tokens,
        gains,
    )
    in_sum = join(own, other, result)
    few = total_rest(join(few, few_got, result), bits[3:])
    few = [few[a:b] for a, b in zip(starts[:-1], starts[1:])]
    select_grad, conv_grad, conv_bias_grad, step_grad, decay_grad, step_bias_grad, skip_grad, shared = few
    shared = shared.reshape(4, slab)
    up_sum = up_sum.astype(f32).reshape(E, slab, up_cols)
    down_sum = down_sum.astype(f32).reshape(E, fours, share, up_cols).transpose(0, 2, 1, 3)
    down_sum = down_sum.reshape(E, share, hidden_cols)
    return (
        result,
        tokens_grad,
        in_sum,
        out_sum.T,
        up_sum,
        down_sum.transpose(0, 2, 1),
        select_grad.T,
        step_grad,
        shared[0:E].T,
        conv_grad,
        conv_bias_grad[0],
        step_bias_grad[0],
        decay_grad,
        skip_grad[0],
        shared[3],
        shared[2],
    )


def solution(mesh):
    return jax.shard_map(
        body,
        mesh=mesh,
        in_specs=(
            P(("grp", "shard"), None),
            P(("grp", "shard"), None),
            P("grp"),
            P(("grp", "shard"), None),
            P("shard", None),
            P("shard", None),
            P(None, "shard"),
            P("shard", None),
            P("shard", None),
            P(None, "shard", None),
            P(None, "shard", None),
            P(None, "shard"),
            P("shard"),
            P("shard"),
            P(None, "shard"),
            P("shard"),
            P("shard"),
            P("shard"),
        ),
        out_specs=(
            P(("grp", "shard"), None),
            P(("grp", "shard"), None),
            P("shard", "grp"),
            P("shard", "grp"),
            P(None, "shard", "grp"),
            P(None, "shard", "grp"),
            P("shard", None),
            P(None, "shard"),
            P("shard", None),
            P(None, "shard"),
            P("shard"),
            P("shard"),
            P(None, "shard"),
            P("shard"),
            P("shard"),
            P("shard"),
        ),
        check_vma=False,
    )
```

```python
import functools
import jax
import jax.numpy as jnp
from jax import lax
from jax.experimental import pallas as pl
from jax.experimental.pallas import tpu as pltpu
from jax.sharding import PartitionSpec as P

R = 72
KW = 4
E = 2
CAP = 192
EPSILON = 1e-05
FTILE = 768
LOG2E = 1.4426950408889634

NS = 16
LANES = 128
STEP = 8
CHUNK = 128


def swap(value, bit):
    size = lax.axis_size("shard")
    return lax.ppermute(value, "shard", [(i, i ^ bit) for i in range(size)])


def swap_groups(value, bit):
    size = lax.axis_size("grp")
    return lax.ppermute(value, "grp", [(g, g ^ bit) for g in range(size)])


def tie(value, *others):
    for other in others:
        corner = other[(0,) * other.ndim].astype(jnp.float32)
        value = value + (0.0 * corner).astype(value.dtype)
    return value


def gather_pieces(value):
    far = swap(value, 2)
    return (value, swap(value, 1), far, swap(far, 1))


def scatter_near(held, given, *others):
    side = lax.axis_index("shard") // 2
    held = tie(held + swap(given, 1).astype(jnp.float32), *others)
    mine = lax.dynamic_index_in_dim(held, side, 0, False)
    return mine, lax.dynamic_index_in_dim(held, 1 - side, 0, False).astype(jnp.bfloat16)


def halve(value, axis, bit, *others):
    mine = (lax.axis_index("grp") // bit) % 2
    terms = value if isinstance(value, tuple) else (value,)
    size = terms[0].shape[axis] // 2

    def side(index):
        picked = [lax.dynamic_slice_in_dim(term, index * size, size, axis) for term in terms]
        total = picked[0].astype(jnp.float32)
        for term in picked[1:]:
            total = total + term.astype(jnp.float32)
        return tie(total, *others)

    return side(mine), side(1 - mine).astype(jnp.bfloat16)


def join(held, got, *others):
    return tie(held.astype(jnp.float32) + got.astype(jnp.float32), *others)


def share_pieces(pieces):
    groups, parts = (lax.axis_size("grp"), lax.axis_size("shard"))
    moves = [
        (g * parts + s, g * parts + (s ^ (2 + g % 2))) for g in range(groups) for s in range(parts)
    ]
    crossed = lax.ppermute(pieces[2], ("grp", "shard"), moves)
    shared = lax.ppermute(crossed, "grp", [(g, g ^ 1) for g in range(groups)])
    return [pieces[0], swap(pieces[1], 1), crossed, shared]


def exchange(value, bits):
    return [value] + [swap_groups(value, sum(bits[i] for i in range(len(bits)) if k >> i & 1)) for k in range(1, 2 ** len(bits))]


def balanced(terms, *others):
    terms = [term.astype(jnp.float32) for term in terms]
    while len(terms) > 1:
        terms = [terms[i] + terms[i + 1] for i in range(0, len(terms), 2)]
    return tie(terms[0], *others)


def total_rest(value, bits, kind=jnp.bfloat16):
    for bit in bits:
        value = balanced(exchange(value.astype(kind), [bit]))
    return value


def matmul(left, right):
    return jnp.dot(left, right, preferred_element_type=jnp.float32)


def pack(value, tiles):
    edge = tiles * LANES
    full = value[:, :edge].reshape(2, 8, tiles, LANES).transpose(2, 0, 1, 3)
    rest = jnp.concatenate([value[:8, edge:], value[8:, edge:]], axis=1)
    return jnp.concatenate([full.reshape(2 * tiles, 8, LANES), rest[None]], axis=0)


def unpack(value, tiles):
    full = value[: 2 * tiles].reshape(tiles, 2, 8, LANES).transpose(1, 2, 0, 3)
    rest = value[2 * tiles]
    rest = jnp.concatenate([rest[:, : LANES // 2], rest[:, LANES // 2 :]], axis=0)
    return jnp.concatenate([full.reshape(NS, tiles * LANES), rest], axis=1)


def fold_rows(parts):
    row = lax.broadcasted_iota(jnp.int32, (8, LANES), 0)
    top, pair, even = (row < 4, (row & 2) == 0, (row & 1) == 0)
    fours = [
        jnp.where(top, parts[i], parts[i + 4])
        + pltpu.roll(jnp.where(top, parts[i + 4], parts[i]), 4, 0)
        for i in range(4)
    ]
    twos = [
        jnp.where(
            pair,
            fours[i] + pltpu.roll(fours[i], 6, 0),
            fours[i + 2] + pltpu.roll(fours[i + 2], 2, 0),
        )
        for i in range(2)
    ]
    return jnp.where(
        even, twos[0] + pltpu.roll(twos[0], 7, 0), twos[1] + pltpu.roll(twos[1], 1, 0)
    )


def halves(pair_ref, at, left):
    low, high = (pair_ref[at, 0:8], pair_ref[at, 8:16])
    return (low, high, jnp.where(left, low, high))


def scan_forward_chunk(tiles, dt_ref, dx_ref, entry_ref, read_ref, rate_ref, out_ref, state_ref, end_ref, held):
    left = lax.broadcasted_iota(jnp.int32, (8, LANES), 1) < LANES // 2

    def group(g, states):
        at, base = (g, g * STEP)
        states = list(states)
        entry = [halves(entry_ref, base + t, left) for t in range(STEP)]
        read = [halves(read_ref, base + t, left) for t in range(STEP)]
        for tile in range(tiles + 1):
            columns = slice(tile * LANES, (tile + 1) * LANES)
            rows = [2 * tile] if tile == tiles else [2 * tile, 2 * tile + 1]
            which = [2] if tile == tiles else [0, 1]
            sums = []
            for t in range(STEP):
                step = dt_ref[at, t : t + 1, columns]
                fed = dx_ref[at, t : t + 1, columns]
                total = None
                for r, w in zip(rows, which):
                    state_ref[base + t, r] = states[r]
                    states[r] = jnp.exp2(step * rate_ref[r]) * states[r] + entry[t][w] * fed
                    term = read[t][w] * states[r]
                    total = term if total is None else total + term
                sums.append(total)
            out_ref[at, :, columns] = fold_rows(sums)
        return tuple(states)

    count = 2 * tiles + 1
    states = lax.fori_loop(0, dt_ref.shape[0], group, tuple(held[r] for r in range(count)))
    for r in range(count):
        held[r] = states[r]
        end_ref[r] = states[r]


def scan_backward_chunk(
    tiles, dt_ref, dx_ref, grad_ref, entry_ref, read_ref, rate_ref, state_ref,
    fed_out, step_out, entry_out, read_out, rate_out, flow, after,
):
    count = 2 * tiles + 1
    left = lax.broadcasted_iota(jnp.int32, (8, LANES), 1) < LANES // 2
    groups = dt_ref.shape[0]

    def group(g, carry):
        at = groups - 1 - g
        base = at * STEP
        flows, afters = (list(carry[0]), list(carry[1]))
        entry = [halves(entry_ref, base + t, left) for t in range(STEP)]
        read = [halves(read_ref, base + t, left) for t in range(STEP)]
        entry_sum = [[None, None] for _ in range(STEP)]
        read_sum = [[None, None] for _ in range(STEP)]
        for tile in range(tiles + 1):
            last = tile == tiles
            columns = slice(tile * LANES, (tile + 1) * LANES)
            rows = [2 * tile] if last else [2 * tile, 2 * tile + 1]
            which = [2] if last else [0, 1]
            fed_sums, step_sums = ([None] * STEP, [None] * STEP)
            rate_sum = [rate_out[r] for r in rows]
            for t in reversed(range(STEP)):
                step = dt_ref[at, t : t + 1, columns]
                fed = dx_ref[at, t : t + 1, columns]
                grad = grad_ref[at, t : t + 1, columns]
                for i, (r, w) in enumerate(zip(rows, which)):
                    before = state_ref[base + t, r]
                    arriving = flows[r] + read[t][w] * grad
                    entry_term = arriving * fed
                    read_term = afters[r] * grad
                    fed_term = entry[t][w] * arriving
                    leaving = jnp.exp2(step * rate_ref[r]) * arriving
                    product = leaving * before
                    step_term = product * rate_ref[r]
                    rate_sum[i] = rate_sum[i] + product * step
                    flows[r] = leaving
                    afters[r] = before
                    fed_sums[t] = fed_term if i == 0 else fed_sums[t] + fed_term
                    step_sums[t] = step_term if i == 0 else step_sums[t] + step_term
                    for total, term in ((entry_sum[t], entry_term), (read_sum[t], read_term)):
                        if last:
                            total[0] = total[0] + jnp.where(left, term, 0.0)
                            total[1] = total[1] + jnp.where(left, 0.0, term)
                        else:
                            total[i] = term if total[i] is None else total[i] + term
            fed_out[at, :, columns] = fold_rows(fed_sums)
            step_out[at, :, columns] = fold_rows(step_sums)
            for i, r in enumerate(rows):
                rate_out[r] = rate_sum[i]
        for t in range(STEP):
            for i in range(2):
                entry_out[base + STEP - 1 - t, 8 * i : 8 * i + 8] = entry_sum[t][i]
                read_out[base + STEP - 1 - t, 8 * i : 8 * i + 8] = read_sum[t][i]
        return (tuple(flows), tuple(afters))

    flows, afters = lax.fori_loop(
        0,
        groups,
        group,
        (tuple(flow[r] for r in range(count)), tuple(after[r] for r in range(count))),
    )
    for r in range(count):
        flow[r] = flows[r]
        after[r] = afters[r]


def split_low(value):
    high = value.astype(jnp.bfloat16)
    return high, (value - high.astype(jnp.float32)).astype(jnp.bfloat16)


def dot(left, right):
    return jnp.dot(left, right, preferred_element_type=jnp.float32)


def dot_t(left, right):
    return lax.dot_general(left, right, (((1,), (1,)), ((), ())), preferred_element_type=jnp.float32)


def t_dot(left, right):
    return lax.dot_general(left, right, (((0,), (0,)), ((), ())), preferred_element_type=jnp.float32)


def live_rows(me_ref, length_ref, rows):
    slot = me_ref[0] * rows + lax.broadcasted_iota(jnp.int32, (rows, 1), 0)
    return slot < length_ref[0]


def router_rows(gains_ref):
    row = lax.broadcasted_iota(jnp.int32, gains_ref.shape, 0)
    return jnp.where(row < E, gains_ref[...], 0.0).astype(jnp.bfloat16)


def cut_kernel(parts, inside, cols, goal_ref, in_ref, up_ref, *rest):
    number = len(rest) // 2
    in_outs, up_outs, sems = (rest[:number], rest[number : 2 * number], rest[-1])
    copies = []
    for k in range(number):
        columns = pl.ds(pl.multiple_of(goal_ref[k] * cols, LANES), cols)
        copies.append(pltpu.make_async_copy(up_ref.at[:, :, columns], up_outs[k], sems.at[k]))
        copies[-1].start()
    for d in range(parts):
        for k in range(number):

            @pl.when(goal_ref[k] == d)
            def write():
                in_outs[k][:, :inside] = in_ref[:, d * inside : (d + 1) * inside]
                at = (parts + d) * inside
                in_outs[k][:, inside:] = in_ref[:, at : at + inside]

    for copy in copies:
        copy.wait()


def cut_weights(goal, in_weight, up_weight, parts, inside):
    slab = in_weight.shape[0]
    cols = up_weight.shape[2] // parts
    number = 3
    in_shape = jax.ShapeDtypeStruct((slab, 2 * inside), in_weight.dtype)
    up_shape = jax.ShapeDtypeStruct((up_weight.shape[0], slab, cols), up_weight.dtype)
    vmem, anywhere = (pl.BlockSpec(memory_space=pltpu.VMEM), pl.BlockSpec(memory_space=pl.ANY))
    outs = pl.pallas_call(
        functools.partial(cut_kernel, parts, inside, cols),
        in_specs=[pl.BlockSpec(memory_space=pltpu.SMEM), vmem, anywhere],
        out_specs=[vmem] * number + [anywhere] * number,
        out_shape=[in_shape] * number + [up_shape] * number,
        scratch_shapes=[pltpu.SemaphoreType.DMA((number,))],
        compiler_params=pltpu.CompilerParams(vmem_limit_bytes=24 * 2**20),
        name="cut_weights",
    )(goal, in_weight, up_weight)
    return outs[:number], outs[number:]


def to_power(value):
    return value / (1.0 + jnp.exp(-value))


def project_kernel(parts, inside, me_ref, source_ref, length_ref, *rest):
    normed_refs, weight_refs, rest = (rest[:parts], rest[parts : 2 * parts], rest[2 * parts :])
    taps_ref, bias_ref, select_ref, inner_out, gate_out, summed_out, conv_out, low_out, selected_out = rest[:9]
    normed, weight, shifted, sems = rest[9:]
    block = pl.program_id(0)
    me = me_ref[0]
    rows, slab = (normed_refs[0].shape[0], weight_refs[0].shape[0])

    @pl.when(block == 0)
    def fetch():
        copies = []
        for k in range(parts):
            at = pl.ds(pl.multiple_of(source_ref[k] * slab, 16), slab)
            copies.append(pltpu.make_async_copy(weight_refs[k], weight.at[at], sems.at[k]))
            at = pl.ds(pl.multiple_of((me ^ k) * rows, 16), rows)
            copies.append(pltpu.make_async_copy(normed_refs[k], normed.at[at], sems.at[parts + k]))
        for copy in copies:
            copy.start()
        for copy in copies:
            copy.wait()
        shifted[0:8] = jnp.zeros((8, inside), jnp.float32)

    start = pl.multiple_of(block * rows, 16)
    projected = jnp.dot(normed[pl.ds(start, rows)], weight[...], preferred_element_type=jnp.float32)
    slot = block * rows + lax.broadcasted_iota(jnp.int32, (rows, 1), 0)
    inner = jnp.where(slot < length_ref[0], projected[:, :inside], 0.0)
    gate_out[...] = projected[:, inside:]
    inner_out[...] = inner
    shifted[8:] = inner
    summed = bias_ref[...]
    for k in range(KW):
        summed = summed + taps_ref[k : k + 1] * shifted[8 - (KW - 1) + k : 8 - (KW - 1) + k + rows]
    shifted[0:8] = shifted[rows : rows + 8]
    summed_out[...] = summed
    value = to_power(summed)
    conv_out[...] = value
    low = value.astype(jnp.bfloat16)
    low_out[...] = low
    selected_out[...] = jnp.dot(low, select_ref[...], preferred_element_type=jnp.float32)


def project(me, source, length, normed_pieces, weight_pieces, taps, bias, select_wide):
    parts = len(normed_pieces)
    rows, width = normed_pieces[0].shape
    slab, both = weight_pieces[0].shape
    inside, picked = select_wide.shape
    total = rows * parts
    smem, anywhere = (pl.BlockSpec(memory_space=pltpu.SMEM), pl.BlockSpec(memory_space=pl.ANY))
    vmem = pl.BlockSpec(memory_space=pltpu.VMEM)
    row = pl.BlockSpec((rows, inside), lambda i: (i, 0))
    wide = jax.ShapeDtypeStruct((total, inside), jnp.float32)
    return pl.pallas_call(
        functools.partial(project_kernel, parts, inside),
        grid=(parts,),
        in_specs=[smem] * 3 + [anywhere] * (2 * parts) + [vmem] * 3,
        out_specs=[row] * 5 + [pl.BlockSpec((rows, picked), lambda i: (i, 0))],
        out_shape=[wide] * 4
        + [
            jax.ShapeDtypeStruct((total, inside), jnp.bfloat16),
            jax.ShapeDtypeStruct((total, picked), jnp.float32),
        ],
        scratch_shapes=[
            pltpu.VMEM((total, width), jnp.bfloat16),
            pltpu.VMEM((slab * parts, both), jnp.bfloat16),
            pltpu.VMEM((rows + 8, inside), jnp.float32),
            pltpu.SemaphoreType.DMA((2 * parts,)),
        ],
        compiler_params=pltpu.CompilerParams(vmem_limit_bytes=40 * 2**20),
        cost_estimate=pl.CostEstimate(flops=4 * 10**9, bytes_accessed=2**20, transcendentals=0),
        name="project",
    )(me, source, length, *normed_pieces, *weight_pieces, taps, bias, select_wide)


def live_slots(start, length_ref, rows):
    return start + lax.broadcasted_iota(jnp.int32, (rows, 1), 0) < length_ref[0]


def store_wide(ref, value):
    groups, _, width = ref.shape
    inside = value.shape[1]
    ref[:, :, :inside] = value.reshape(groups, STEP, inside)
    ref[:, :, inside:] = value[:, 2 * inside - width :].reshape(groups, STEP, width - inside)


def load_narrow(ref, inside):
    groups, _, width = ref.shape
    edge = 2 * inside - width
    value = ref[...].reshape(groups * STEP, width)
    return jnp.concatenate([value[:, :edge], value[:, edge:inside] + value[:, inside:]], axis=1)


def store_spread(entry_ref, read_ref, selected):
    turned = selected.T
    for t in range(selected.shape[0]):
        entry_ref[t] = jnp.broadcast_to(turned[R : R + NS, t : t + 1], (NS, LANES))
        read_ref[t] = jnp.broadcast_to(turned[R + NS : R + 2 * NS, t : t + 1], (NS, LANES))


def step_sizes(selected, weight_ref, bias_ref, live):
    low = selected.astype(jnp.bfloat16)
    pre = dot(low, weight_ref[...]) + bias_ref[...]
    soft = jnp.maximum(pre, 0.0) + jnp.log1p(jnp.exp(-jnp.abs(pre)))
    return low, pre, jnp.where(live, soft, 0.0)


def mixer_kernel(
    tiles, share, me_ref, length_ref, selected_ref, conv_ref, gate_ref, weight_ref, bias_ref, skip_ref, rate_ref, project_ref,
    state_ref, end_ref, mixed_out, gated_out, held_out, given_out,
    dt_ref, dx_ref, entry_ref, read_ref, out_ref, held,
):
    chunk, inside = conv_ref.shape
    step = pl.program_id(0)

    @pl.when(step == 0)
    def start():
        held[...] = jnp.zeros_like(held)

    selected, conv = (selected_ref[...], conv_ref[...])
    live = live_slots(step * chunk, length_ref, chunk)
    _, _, size = step_sizes(selected, weight_ref, bias_ref, live)
    store_wide(dt_ref, size)
    store_wide(dx_ref, size * conv)
    store_spread(entry_ref, read_ref, selected)
    scan_forward_chunk(tiles, dt_ref, dx_ref, entry_ref, read_ref, rate_ref, out_ref, state_ref, end_ref, held)
    mixed = load_narrow(out_ref, inside) + skip_ref[...] * conv
    mixed_out[...] = mixed
    gated = (mixed * to_power(gate_ref[...])).astype(jnp.bfloat16)
    gated_out[...] = gated
    part = dot(gated, project_ref[...])
    block = step // share
    rows = pl.ds(pl.multiple_of((step % share) * chunk, chunk), chunk)

    @pl.when(block % 2 == me_ref[0] % 2)
    def keep():
        held_out[0, rows] = part

    @pl.when(block % 2 != me_ref[0] % 2)
    def give():
        given_out[0, rows] = part.astype(jnp.bfloat16)


def mixer(me, length, selected, conv_out, zgate, step_wide, bias, skip, rate, out_weight, span, tiles):
    total, inside = conv_out.shape
    width = out_weight.shape[1]
    count = 2 * tiles + 1
    chunk = CHUNK
    wide = (tiles + 1) * LANES
    share = span // chunk
    smem, vmem = (pl.BlockSpec(memory_space=pltpu.SMEM), pl.BlockSpec(memory_space=pltpu.VMEM))
    row = pl.BlockSpec((chunk, inside), lambda i: (i, 0))
    part = pl.BlockSpec((1, span, width), lambda i: (i // (2 * share), 0, 0))
    f32, bf16 = (jnp.float32, jnp.bfloat16)
    return pl.pallas_call(
        functools.partial(mixer_kernel, tiles, share),
        grid=(total // chunk,),
        in_specs=[smem, smem, pl.BlockSpec((chunk, LANES), lambda i: (i, 0)), row, row] + [vmem] * 5,
        out_specs=[pl.BlockSpec((chunk, count, 8, LANES), lambda i: (i, 0, 0, 0)), vmem, row, row, part, part],
        out_shape=[
            jax.ShapeDtypeStruct((total, count, 8, LANES), f32),
            jax.ShapeDtypeStruct((count, 8, LANES), f32),
            jax.ShapeDtypeStruct((total, inside), f32),
            jax.ShapeDtypeStruct((total, inside), bf16),
            jax.ShapeDtypeStruct((2, span, width), f32),
            jax.ShapeDtypeStruct((2, span, width), bf16),
        ],
        scratch_shapes=[pltpu.VMEM((chunk // STEP, STEP, wide), f32)] * 2
        + [pltpu.VMEM((chunk, NS, LANES), f32)] * 2
        + [pltpu.VMEM((chunk // STEP, STEP, wide), f32), pltpu.VMEM((count, 8, LANES), f32)],
        compiler_params=pltpu.CompilerParams(vmem_limit_bytes=40 * 2**20),
        cost_estimate=pl.CostEstimate(flops=4 * 10**9, bytes_accessed=2**20, transcendentals=0),
        name="mixer",
    )(me, length, selected, conv_out, zgate, step_wide, bias, skip, rate, out_weight)


def row_sums(value):
    high, low = split_low(value)
    ones = jnp.ones((8, LANES), jnp.bfloat16)
    return dot_t(ones, high) + dot_t(ones, low)


def mixer_back_kernel(tiles, length_ref, *rest):
    (
        selected_ref, conv_ref, grad_ref, state_ref, end_ref, weight_ref, bias_ref, skip_ref, rate_ref,
        conv_out, rank_out, step_out, bias_out, skip_out, rate_out,
        dt_ref, dx_ref, mix_ref, entry_ref, read_ref, fed_ref, rise_ref, entry_parts, read_parts, flow, after,
    ) = rest
    chunk, inside = conv_ref.shape
    index = pl.program_id(0)
    step = pl.num_programs(0) - 1 - index

    @pl.when(index == 0)
    def start():
        flow[...] = jnp.zeros_like(flow)
        after[...] = end_ref[...]
        rate_out[...] = jnp.zeros_like(rate_out)
        step_out[...] = jnp.zeros_like(step_out)
        bias_out[...] = jnp.zeros_like(bias_out)
        skip_out[...] = jnp.zeros_like(skip_out)

    conv, grad_mixed = (conv_ref[...], grad_ref[...])
    skip_out[...] += jnp.sum(grad_mixed * conv, axis=0, keepdims=True)
    selected = selected_ref[...]
    live = live_slots(step * chunk, length_ref, chunk)
    low, pre, size = step_sizes(selected, weight_ref, bias_ref, live)
    store_wide(dt_ref, size)
    store_wide(dx_ref, size * conv)
    store_wide(mix_ref, grad_mixed)
    store_spread(entry_ref, read_ref, selected)
    scan_backward_chunk(
        tiles, dt_ref, dx_ref, mix_ref, entry_ref, read_ref, rate_ref, state_ref,
        fed_ref, rise_ref, entry_parts, read_parts, rate_out, flow, after,
    )
    fed = load_narrow(fed_ref, inside)
    grad_size = load_narrow(rise_ref, inside) * (1.0 / LOG2E) + fed * conv
    grad_pre = jnp.where(live, grad_size / (1.0 + jnp.exp(-pre)), 0.0)
    bias_out[...] += jnp.sum(grad_pre, axis=0, keepdims=True)
    grad_low = grad_pre.astype(jnp.bfloat16)
    rank = dot_t(grad_low, weight_ref[...])
    sums = [row_sums(part[...].reshape(chunk * NS, LANES)) for part in (entry_parts, read_parts)]
    lane = lax.broadcasted_iota(jnp.int32, (STEP, LANES), 1)
    for g in range(chunk // STEP):
        total = rank[g * STEP : (g + 1) * STEP]
        for i, part in enumerate(sums):
            start = R + i * NS
            moved = pltpu.roll(part[:, g * LANES : (g + 1) * LANES], start + NS, 1)
            moved = pltpu.roll(moved, 0, 1, stride=NS, stride_axis=0)
            total = jnp.where((lane >= start) & (lane < start + NS), moved, total)
        rank_out[g * STEP : (g + 1) * STEP] = total
    step_out[...] += t_dot(low, grad_low)
    conv_out[...] = fed * size + skip_ref[...] * grad_mixed


def mixer_back(length, selected, conv_out, grad_mixed, states, end, step_wide, bias, skip, rate, tiles):
    total, inside = conv_out.shape
    count = 2 * tiles + 1
    chunk = CHUNK
    steps = total // chunk
    wide = (tiles + 1) * LANES
    smem, vmem = (pl.BlockSpec(memory_space=pltpu.SMEM), pl.BlockSpec(memory_space=pltpu.VMEM))
    row = pl.BlockSpec((chunk, inside), lambda i: (steps - 1 - i, 0))
    lane = pl.BlockSpec((chunk, LANES), lambda i: (steps - 1 - i, 0))
    f32 = jnp.float32
    one = jax.ShapeDtypeStruct((1, inside), f32)
    return pl.pallas_call(
        functools.partial(mixer_back_kernel, tiles),
        grid=(steps,),
        in_specs=[smem, lane, row, row]
        + [pl.BlockSpec((chunk, count, 8, LANES), lambda i: (steps - 1 - i, 0, 0, 0))]
        + [vmem] * 5,
        out_specs=[row, lane] + [vmem] * 4,
        out_shape=[
            jax.ShapeDtypeStruct((total, inside), f32),
            jax.ShapeDtypeStruct((total, LANES), f32),
            jax.ShapeDtypeStruct((LANES, inside), f32),
            one,
            one,
            jax.ShapeDtypeStruct((count, 8, LANES), f32),
        ],
        scratch_shapes=[pltpu.VMEM((chunk // STEP, STEP, wide), f32)] * 3
        + [pltpu.VMEM((chunk, NS, LANES), f32)] * 2
        + [pltpu.VMEM((chunk // STEP, STEP, wide), f32)] * 2
        + [pltpu.VMEM((chunk, NS, LANES), f32)] * 2
        + [pltpu.VMEM((count, 8, LANES), f32)] * 2,
        compiler_params=pltpu.CompilerParams(vmem_limit_bytes=48 * 2**20),
        cost_estimate=pl.CostEstimate(flops=4 * 10**9, bytes_accessed=2**20, transcendentals=0),
        name="mixer_back",
    )(length, selected, conv_out, grad_mixed, states, end, step_wide, bias, skip, rate)


def gate_back_kernel(parts, pair, me_ref, source_ref, *rest):
    normed_refs, grad_refs, rest = (rest[:parts], rest[parts : 2 * parts], rest[2 * parts :])
    (
        gate_ref, mixed_ref, gated_ref, project_ref,
        mix_out, gate_out, gate_held, gate_given, out_held, out_given,
        normed, grads, lows, product, sems,
    ) = rest
    block = pl.program_id(0)
    rows, width = normed_refs[0].shape
    slab = width // parts
    me, odd, second = (me_ref[0], source_ref[parts], source_ref[parts + 1])

    @pl.when(block == 0)
    def fetch():
        copies = []
        for k in range(parts):
            at = pl.ds(pl.multiple_of((me ^ k) * rows, 16), rows)
            copies.append(pltpu.make_async_copy(normed_refs[k], normed.at[at], sems.at[k]))
            copies.append(pltpu.make_async_copy(grad_refs[k], grads.at[at], sems.at[parts + k]))
        for copy in copies:
            copy.start()
        for copy in copies:
            copy.wait()

    at = pl.ds(pl.multiple_of(block * rows, rows), rows)
    grad = grads[at]
    grad_gated = dot_t(grad, project_ref[...])
    gate = gate_ref[...]
    curve = 1.0 / (1.0 + jnp.exp(-gate))
    mix_out[...] = grad_gated * (gate * curve)
    low = (grad_gated * mixed_ref[...] * (curve * (1.0 + gate * (1.0 - curve)))).astype(jnp.bfloat16)
    gate_out[...] = low
    lows[at] = low

    @pl.when(block == parts - 1)
    def finish():
        product[...] = t_dot(normed[...], lows[...])
        for h in range(parts // 2):
            at = pl.ds(pl.multiple_of((2 * h + odd) * slab, 8), slab)
            gate_held[h] = product[at]
            at = pl.ds(pl.multiple_of((2 * h + 1 - odd) * slab, 8), slab)
            gate_given[h] = product[at].astype(jnp.bfloat16)
        product[...] = t_dot(grads[...], gated_ref[...])
        for h in range(width // (2 * pair)):
            at = pl.ds(pl.multiple_of((2 * h + second) * pair, 8), pair)
            out_held[h] = product[at]
            at = pl.ds(pl.multiple_of((2 * h + 1 - second) * pair, 8), pair)
            out_given[h] = product[at].astype(jnp.bfloat16)


def gate_back(me, source, normed_pieces, grad_pieces, zgate, mixed, gated, out_weight, pair):
    parts = len(normed_pieces)
    rows, width = normed_pieces[0].shape
    total, inside = gated.shape
    slab = width // parts
    smem, anywhere = (pl.BlockSpec(memory_space=pltpu.SMEM), pl.BlockSpec(memory_space=pl.ANY))
    vmem = pl.BlockSpec(memory_space=pltpu.VMEM)
    row = pl.BlockSpec((rows, inside), lambda i: (i, 0))
    f32, bf16 = (jnp.float32, jnp.bfloat16)
    gate_shape = (parts // 2, slab, inside)
    out_shape = (width // (2 * pair), pair, inside)
    return pl.pallas_call(
        functools.partial(gate_back_kernel, parts, pair),
        grid=(parts,),
        in_specs=[smem] * 2 + [anywhere] * (2 * parts) + [row] * 2 + [vmem] * 2,
        out_specs=[row] * 2 + [vmem] * 4,
        out_shape=[
            jax.ShapeDtypeStruct((total, inside), f32),
            jax.ShapeDtypeStruct((total, inside), bf16),
            jax.ShapeDtypeStruct(gate_shape, f32),
            jax.ShapeDtypeStruct(gate_shape, bf16),
            jax.ShapeDtypeStruct(out_shape, f32),
            jax.ShapeDtypeStruct(out_shape, bf16),
        ],
        scratch_shapes=[
            pltpu.VMEM((total, width), bf16),
            pltpu.VMEM((total, width), bf16),
            pltpu.VMEM((total, inside), bf16),
            pltpu.VMEM((width, inside), f32),
            pltpu.SemaphoreType.DMA((2 * parts,)),
        ],
        compiler_params=pltpu.CompilerParams(vmem_limit_bytes=48 * 2**20),
        cost_estimate=pl.CostEstimate(flops=4 * 10**9, bytes_accessed=2**20, transcendentals=0),
        name="gate_back",
    )(me, source, *normed_pieces, *grad_pieces, zgate, mixed, gated, out_weight)


def conv_back_kernel(parts, me_ref, source_ref, length_ref, *rest):
    normed_refs, rest = (rest[:parts], rest[parts:])
    (
        selected_ref, conv_ref, summed_ref, inner_ref, low_ref, taps_ref, select_ref,
        inner_out, inner_held, inner_given, select_out, taps_out, bias_out,
        normed, shifted, lows, total, sems,
    ) = rest
    index = pl.program_id(0)
    block = parts - 1 - index
    rows, inside = inner_ref.shape
    slab = normed.shape[1] // parts
    me = me_ref[0]
    odd = source_ref[parts]

    def fetched(k):
        at = pl.ds(pl.multiple_of((me ^ k) * rows, 16), rows)
        return pltpu.make_async_copy(normed_refs[k], normed.at[at], sems.at[k])

    @pl.when(index == 0)
    def fetch():
        for k in range(parts):
            fetched(k).start()
        shifted[rows:] = jnp.zeros((8, inside), jnp.float32)
        select_out[...] = jnp.zeros_like(select_out)
        taps_out[...] = jnp.zeros_like(taps_out)
        bias_out[...] = jnp.zeros_like(bias_out)

    selected = selected_ref[...]
    summed = summed_ref[...]
    curve = 1.0 / (1.0 + jnp.exp(-summed))
    grad_summed = (conv_ref[...] + dot_t(selected, select_ref[...])) * (curve * (1.0 + summed * (1.0 - curve)))
    select_out[...] += t_dot(selected, low_ref[...])
    bias_out[...] += jnp.sum(grad_summed, axis=0, keepdims=True)
    shifted[:rows] = grad_summed
    inner = inner_ref[...]
    grad_inner = jnp.zeros((rows, inside), jnp.float32)
    for k in range(KW):
        moved = shifted[KW - 1 - k : KW - 1 - k + rows]
        grad_inner = grad_inner + taps_ref[k : k + 1] * moved
        taps_out[k : k + 1] += jnp.sum(inner * moved, axis=0, keepdims=True)
    shifted[rows:] = shifted[0:8]
    live = live_slots(block * rows, length_ref, rows)
    low = jnp.where(live, grad_inner, 0.0).astype(jnp.bfloat16)
    inner_out[...] = low

    lows[pl.ds(pl.multiple_of(block * rows, rows), rows)] = low

    @pl.when(block == 0)
    def finish():
        for k in range(parts):
            fetched(k).wait()
        total[...] = t_dot(normed[...], lows[...])
        for h in range(parts // 2):
            at = pl.ds(pl.multiple_of((2 * h + odd) * slab, 8), slab)
            inner_held[h] = total[at]
            at = pl.ds(pl.multiple_of((2 * h + 1 - odd) * slab, 8), slab)
            inner_given[h] = total[at].astype(jnp.bfloat16)


def conv_back(me, source, length, normed_pieces, grad_selected, conv_grad, summed, inner, conv_low, taps, select_wide):
    parts = len(normed_pieces)
    rows, width = normed_pieces[0].shape
    slab = width // parts
    total, inside = inner.shape
    smem, anywhere = (pl.BlockSpec(memory_space=pltpu.SMEM), pl.BlockSpec(memory_space=pl.ANY))
    vmem = pl.BlockSpec(memory_space=pltpu.VMEM)
    row = pl.BlockSpec((rows, inside), lambda i: (parts - 1 - i, 0))
    f32, bf16 = (jnp.float32, jnp.bfloat16)
    return pl.pallas_call(
        functools.partial(conv_back_kernel, parts),
        grid=(parts,),
        in_specs=[smem] * 3
        + [anywhere] * parts
        + [pl.BlockSpec((rows, LANES), lambda i: (parts - 1 - i, 0))]
        + [row] * 4
        + [vmem] * 2,
        out_specs=[row] + [vmem] * 5,
        out_shape=[
            jax.ShapeDtypeStruct((total, inside), bf16),
            jax.ShapeDtypeStruct((2, slab, inside), f32),
            jax.ShapeDtypeStruct((2, slab, inside), bf16),
            jax.ShapeDtypeStruct((LANES, inside), f32),
            jax.ShapeDtypeStruct((8, inside), f32),
            jax.ShapeDtypeStruct((1, inside), f32),
        ],
        scratch_shapes=[
            pltpu.VMEM((total, width), bf16),
            pltpu.VMEM((rows + 8, inside), f32),
            pltpu.VMEM((total, inside), bf16),
            pltpu.VMEM((width, inside), f32),
            pltpu.SemaphoreType.DMA((parts,)),
        ],
        compiler_params=pltpu.CompilerParams(vmem_limit_bytes=48 * 2**20),
        cost_estimate=pl.CostEstimate(flops=4 * 10**9, bytes_accessed=2**20, transcendentals=0),
        name="conv_back",
    )(me, source, length, *normed_pieces, grad_selected, conv_grad, summed, inner, conv_low, taps, select_wide)


def project_back_kernel(parts, me_ref, source_ref, *rest):
    normed_refs, weight_refs, rest = (rest[:parts], rest[parts : 2 * parts], rest[2 * parts :])
    inner_ref, gate_ref, held_out, given_out, gain_out, normed, weight, projected, sems = rest
    block = pl.program_id(0)
    rows, inside = inner_ref.shape
    slab = weight_refs[0].shape[0]
    me = me_ref[0]

    @pl.when(block == 0)
    def fetch():
        copies = []
        for k in range(parts):
            at = pl.ds(pl.multiple_of(source_ref[k] * slab, 16), slab)
            copies.append(pltpu.make_async_copy(weight_refs[k], weight.at[at], sems.at[k]))
            at = pl.ds(pl.multiple_of((me ^ k) * rows, 16), rows)
            copies.append(pltpu.make_async_copy(normed_refs[k], normed.at[at], sems.at[parts + k]))
        for copy in copies:
            copy.start()
        gain_out[...] = jnp.zeros_like(gain_out)
        for copy in copies:
            copy.wait()

    projected[:, :inside] = inner_ref[...]
    projected[:, inside:] = gate_ref[...]
    normed_rows = normed[pl.ds(pl.multiple_of(block * rows, rows), rows)]
    grad_normed = dot_t(projected[...], weight[...])
    gain_out[...] += jnp.sum(grad_normed * normed_rows.astype(jnp.float32), axis=0, keepdims=True)

    @pl.when(block % 2 == me % 2)
    def keep():
        held_out[0] = grad_normed

    @pl.when(block % 2 != me % 2)
    def give():
        given_out[0] = grad_normed.astype(jnp.bfloat16)


def project_back(me, source, normed_pieces, weight_pieces, inner_grad, gate_grad):
    parts = len(normed_pieces)
    rows, width = normed_pieces[0].shape
    slab, both = weight_pieces[0].shape
    total, inside = inner_grad.shape
    smem, anywhere = (pl.BlockSpec(memory_space=pltpu.SMEM), pl.BlockSpec(memory_space=pl.ANY))
    vmem = pl.BlockSpec(memory_space=pltpu.VMEM)
    row = pl.BlockSpec((rows, inside), lambda i: (i, 0))
    part = pl.BlockSpec((1, rows, width), lambda i: (i // 2, 0, 0))
    f32, bf16 = (jnp.float32, jnp.bfloat16)
    return pl.pallas_call(
        functools.partial(project_back_kernel, parts),
        grid=(parts,),
        in_specs=[smem] * 2 + [anywhere] * (2 * parts) + [row] * 2,
        out_specs=[part, part, vmem],
        out_shape=[
            jax.ShapeDtypeStruct((2, rows, width), f32),
            jax.ShapeDtypeStruct((2, rows, width), bf16),
            jax.ShapeDtypeStruct((1, width), f32),
        ],
        scratch_shapes=[
            pltpu.VMEM((total, width), bf16),
            pltpu.VMEM((slab * parts, both), bf16),
            pltpu.VMEM((rows, both), bf16),
            pltpu.SemaphoreType.DMA((2 * parts,)),
        ],
        compiler_params=pltpu.CompilerParams(vmem_limit_bytes=40 * 2**20),
        cost_estimate=pl.CostEstimate(flops=4 * 10**9, bytes_accessed=2**20, transcendentals=0),
        name="project_back",
    )(me, source, *normed_pieces, *weight_pieces, inner_grad, gate_grad)


def norm_kernel(parts, me_ref, tokens_ref, *rest):
    small_refs, normed_out, gains_out = (rest[:parts], rest[parts], rest[parts + 1])
    slab = small_refs[0].shape[1]
    for m in range(parts):

        @pl.when(me_ref[0] == m)
        def lay():
            for p in range(parts):
                gains_out[:, p * slab : (p + 1) * slab] = small_refs[p ^ m][...]

    tokens = tokens_ref[...]
    scale = lax.rsqrt(jnp.mean(tokens * tokens, axis=-1, keepdims=True) + EPSILON)
    normed_out[...] = (tokens * scale * gains_out[2:3]).astype(jnp.bfloat16)


def norm_rows(me, tokens, small_pieces):
    parts = len(small_pieces)
    smem, vmem = (pl.BlockSpec(memory_space=pltpu.SMEM), pl.BlockSpec(memory_space=pltpu.VMEM))
    return pl.pallas_call(
        functools.partial(norm_kernel, parts),
        in_specs=[smem] + [vmem] * (1 + parts),
        out_specs=[vmem] * 2,
        out_shape=[
            jax.ShapeDtypeStruct(tokens.shape, jnp.bfloat16),
            jax.ShapeDtypeStruct((small_pieces[0].shape[0], tokens.shape[1]), jnp.float32),
        ],
        compiler_params=pltpu.CompilerParams(vmem_limit_bytes=16 * 2**20),
        name="norm_rows",
    )(me, tokens, *small_pieces)


def route_kernel(
    me_ref, length_ref, tokens_ref, near_ref, got_ref, gains_ref, order_ref, routes_ref,
    first_out, normed_out, sent_out, probs_out,
):
    rows, width = tokens_ref.shape
    first = tokens_ref[...] + near_ref[...] + got_ref[...].astype(jnp.float32)
    first_out[...] = first
    scale = lax.rsqrt(jnp.mean(first * first, axis=-1, keepdims=True) + EPSILON)
    normed = (first * scale * gains_ref[3:4]).astype(jnp.bfloat16)
    normed_out[...] = normed
    logits = dot_t(normed, router_rows(gains_ref))
    gap = logits[:, 0:1] - logits[:, 1:2]
    prob_zero = 1.0 / (1.0 + jnp.exp(-gap))
    prob_one = 1.0 / (1.0 + jnp.exp(gap))
    lane = lax.broadcasted_iota(jnp.int32, (rows, LANES), 1)
    probs_out[...] = jnp.where(lane == 0, prob_zero, jnp.where(lane == 1, prob_one, 0.0))
    gate = jnp.where(routes_ref[...] == 0, prob_zero, prob_one)
    gate = jnp.where(live_rows(me_ref, length_ref, rows), gate, 0.0)
    high, low = split_low(gate)
    high, low = (high.astype(jnp.float32), low.astype(jnp.float32))
    gates = jnp.where(lane == 0, high, jnp.where(lane == 1, low, 0.0)).astype(jnp.bfloat16)
    sent_out[:, :width] = dot(order_ref[...], normed).astype(jnp.bfloat16)
    sent_out[:, width:] = dot(order_ref[...], gates).astype(jnp.bfloat16)


def route(me, length, tokens, near, got, gains, order, routes):
    rows, width = tokens.shape
    smem, vmem = (pl.BlockSpec(memory_space=pltpu.SMEM), pl.BlockSpec(memory_space=pltpu.VMEM))
    return pl.pallas_call(
        route_kernel,
        in_specs=[smem, smem] + [vmem] * 6,
        out_specs=[vmem] * 4,
        out_shape=[
            jax.ShapeDtypeStruct((rows, width), jnp.float32),
            jax.ShapeDtypeStruct((rows, width), jnp.bfloat16),
            jax.ShapeDtypeStruct((rows, width + LANES), jnp.bfloat16),
            jax.ShapeDtypeStruct((rows, LANES), jnp.float32),
        ],
        compiler_params=pltpu.CompilerParams(vmem_limit_bytes=32 * 2**20),
        name="route",
    )(me, length, tokens, near, got, gains, order, routes)


def expert_kernel(parts, cap, steps, me_ref, source_ref, counts_ref, *rest):
    sent_refs, cot_refs, up_refs = (rest[:parts], rest[parts : 2 * parts], rest[2 * parts : 3 * parts])
    (
        down_ref, grad_held, grad_given, out_held, out_given, packed,
    ) = rest[3 * parts : 3 * parts + 6]
    rows, cots, up, down, rows_t, cots_t, scale, dots, grad_sum, out_sum, product, sems = rest[3 * parts + 6 :]
    step = pl.program_id(0)
    expert, tile = (step // steps, step % steps)
    span, width = cots.shape[1:]
    slab = up_refs[0].shape[1]
    offset = span - cap
    count = parts * cap
    me = me_ref[0]

    def weights(e):
        base = 2 * parts + e * (parts + 1)
        copies = [pltpu.make_async_copy(down_ref.at[e], down.at[e], sems.at[base])]
        for k in range(parts):
            at = pl.ds(pl.multiple_of(source_ref[k] * slab, 16), slab)
            copies.append(pltpu.make_async_copy(up_refs[k].at[e], up.at[e, at], sems.at[base + 1 + k]))
        return copies

    @pl.when(step == 0)
    def fetch():
        copies = []
        for k in range(parts):
            copies.append(pltpu.make_async_copy(sent_refs[k], rows.at[me ^ k], sems.at[k]))
            copies.append(pltpu.make_async_copy(cot_refs[k], cots.at[me ^ k], sems.at[parts + k]))
        for copy in copies:
            copy.start()
        for e in range(2):
            for copy in weights(e):
                copy.start()
        grad_sum[...] = jnp.zeros_like(grad_sum)
        out_sum[...] = jnp.zeros_like(out_sum)
        dots[...] = jnp.zeros_like(dots)
        for copy in copies:
            copy.wait()

    at = pl.ds(pl.multiple_of(expert * offset, 16), cap)
    mine = rows[:, at, :width].reshape(count, width)
    cot = cots[:, at].reshape(count, width)

    @pl.when(tile == 0)
    def turn():
        rows_t[...] = mine.T
        cots_t[...] = cot.T
        slot = lax.broadcasted_iota(jnp.int32, (cap, LANES), 0)
        for b in range(parts):
            gates = rows[b, at, width:].astype(jnp.float32)
            gate = gates[:, 0:1] + gates[:, 1:2]
            first = slot < counts_ref[b]
            later = slot + offset >= counts_ref[b]
            live = jnp.where(expert == 0, first.astype(jnp.float32), later.astype(jnp.float32))
            scale[b * cap : (b + 1) * cap] = live * gate
        for e in range(2):

            @pl.when(expert == e)
            def arrive():
                for copy in weights(e):
                    copy.wait()

    columns = pl.ds(pl.multiple_of(tile * FTILE, FTILE), FTILE)
    up_tile = up[expert, :, columns]
    down_tile = down[expert, columns, :]
    weight = scale[...][:, 0:1]
    pre = dot(mine, up_tile)
    grad_hidden = dot_t(cot, down_tile)
    square = pre * pre
    bend = jnp.tanh(0.7978845608028654 * pre * (1.0 + 0.044715 * square))
    rise = 0.5 * (1.0 + bend)
    slope = rise + 0.5 * pre * (1.0 - bend * bend) * (0.7978845608028654 * (1.0 + 0.134145 * square))
    hidden = (weight * (pre * rise)).astype(jnp.bfloat16)
    grad_pre = (weight * slope * grad_hidden).astype(jnp.bfloat16)
    part = jnp.sum(hidden.astype(jnp.float32) * grad_hidden, axis=1, keepdims=True)
    dots[:, at] += jnp.broadcast_to(part, (count, LANES)).reshape(parts, cap, LANES)
    out_sum[:, at] += dot(hidden, down_tile).reshape(parts, cap, width)
    grad_sum[:, at] += dot_t(grad_pre, up_tile).reshape(parts, cap, width)
    product[...] = dot(rows_t[...], grad_pre)
    fours = packed.shape[0]
    inside = packed.shape[-1] // LANES
    share = width // (fours * parts)
    pieces = []
    for q in range(FTILE // LANES):
        piece = tile * (FTILE // LANES) + q
        pieces.append((piece // inside, pl.ds(pl.multiple_of(piece % inside * LANES, LANES), LANES)))
    up_rows = pl.ds(pl.multiple_of(expert * slab, 16), slab)
    for q, (block, lanes) in enumerate(pieces):
        for r in range(parts):
            taken = product[r * slab : (r + 1) * slab, q * LANES : (q + 1) * LANES]
            packed[block, r, up_rows, lanes] = taken.astype(jnp.bfloat16)
    product[...] = dot(cots_t[...], hidden)
    base = 2 * slab
    for q, (block, lanes) in enumerate(pieces):
        down_rows = pl.ds(pl.multiple_of(base + (expert * fours + block) * share, 16), share)
        for g in range(fours * parts):
            taken = product[g * share : (g + 1) * share, q * LANES : (q + 1) * LANES]
            packed[g // parts, g % parts, down_rows, lanes] = taken.astype(jnp.bfloat16)

    @pl.when(step == pl.num_programs(0) - 1)
    def finish():
        for b in range(parts):

            @pl.when(me % 2 == b % 2)
            def hold():
                grad_held[b // 2, :, :width] = grad_sum[b]
                grad_held[b // 2, :, width:] = dots[b]
                out_held[b // 2] = out_sum[b]

            @pl.when(me % 2 != b % 2)
            def give():
                grad_given[b // 2, :, :width] = grad_sum[b].astype(jnp.bfloat16)
                grad_given[b // 2, :, width:] = dots[b].astype(jnp.bfloat16)
                out_given[b // 2] = out_sum[b].astype(jnp.bfloat16)


def experts(me, source, counts, sent_pieces, cot_pieces, up_pieces, down_weight, fours):
    parts = len(sent_pieces)
    span, width = cot_pieces[0].shape
    number, hid = down_weight.shape[:2]
    steps = hid // FTILE
    slab = up_pieces[0].shape[1]
    smem, anywhere = (pl.BlockSpec(memory_space=pltpu.SMEM), pl.BlockSpec(memory_space=pl.ANY))
    vmem = pl.BlockSpec(memory_space=pltpu.VMEM)
    f32, bf16 = (jnp.float32, jnp.bfloat16)
    packed = (fours, parts, 2 * number * slab, hid // fours)
    count = parts * CAP
    return pl.pallas_call(
        functools.partial(expert_kernel, parts, CAP, steps),
        grid=(number * steps,),
        in_specs=[smem] * 3 + [anywhere] * (3 * parts + 1),
        out_specs=[vmem] * 5,
        out_shape=[
            jax.ShapeDtypeStruct((2, span, width + LANES), f32),
            jax.ShapeDtypeStruct((2, span, width + LANES), bf16),
            jax.ShapeDtypeStruct((2, span, width), f32),
            jax.ShapeDtypeStruct((2, span, width), bf16),
            jax.ShapeDtypeStruct(packed, bf16),
        ],
        scratch_shapes=[
            pltpu.VMEM((parts, span, width + LANES), bf16),
            pltpu.VMEM((parts, span, width), bf16),
            pltpu.VMEM((number, slab * parts, hid), bf16),
            pltpu.VMEM((number, hid, width), bf16),
            pltpu.VMEM((width, count), bf16),
            pltpu.VMEM((width, count), bf16),
            pltpu.VMEM((count, LANES), f32),
            pltpu.VMEM((parts, span, LANES), f32),
            pltpu.VMEM((parts, span, width), f32),
            pltpu.VMEM((parts, span, width), f32),
            pltpu.VMEM((width, FTILE), f32),
            pltpu.SemaphoreType.DMA((2 * parts + 2 * (parts + 1),)),
        ],
        compiler_params=pltpu.CompilerParams(vmem_limit_bytes=60 * 2**20),
        cost_estimate=pl.CostEstimate(flops=4 * 10**9, bytes_accessed=2**20, transcendentals=0),
        name="experts",
    )(me, source, counts, *sent_pieces, *cot_pieces, *up_pieces, down_weight)


def return_kernel(
    me_ref, length_ref, near_ref, got_ref, order_ref, normed_ref, probs_ref, routes_ref, first_ref, cot_ref, gains_ref,
    grad_out, low_out, gain_out, router_out,
):
    rows, width = first_ref.shape
    grad = near_ref[...] + got_ref[...].astype(jnp.float32)
    high, low = split_low(grad)
    grad = dot(order_ref[...], high) + dot(order_ref[...], low)
    lane = lax.broadcasted_iota(jnp.int32, (rows, LANES), 1)
    chosen = (lane == routes_ref[...]).astype(jnp.float32)
    grad_logits = (grad[:, width : width + 1] * (chosen - probs_ref[...])).astype(jnp.bfloat16)
    grad_normed = grad[:, :width] + dot(grad_logits[:, :NS], router_rows(gains_ref))
    router_out[...] = t_dot(grad_logits, normed_ref[...])[0:8]
    first = first_ref[...]
    scale = lax.rsqrt(jnp.mean(first * first, axis=-1, keepdims=True) + EPSILON)
    unit = first * scale
    gain_out[...] = jnp.sum(grad_normed * unit, axis=0, keepdims=True)
    pulled = grad_normed * gains_ref[3:4]
    pulled = scale * (pulled - unit * jnp.mean(pulled * unit, axis=-1, keepdims=True))
    total = jnp.where(live_rows(me_ref, length_ref, rows), cot_ref[...], 0.0) + pulled
    grad_out[...] = total
    low_out[...] = total.astype(jnp.bfloat16)


def return_rows(me, length, *operands):
    rows, width = operands[6].shape
    smem, vmem = (pl.BlockSpec(memory_space=pltpu.SMEM), pl.BlockSpec(memory_space=pltpu.VMEM))
    return pl.pallas_call(
        return_kernel,
        in_specs=[smem, smem] + [vmem] * 9,
        out_specs=[vmem] * 4,
        out_shape=[
            jax.ShapeDtypeStruct((rows, width), jnp.float32),
            jax.ShapeDtypeStruct((rows, width), jnp.bfloat16),
            jax.ShapeDtypeStruct((1, width), jnp.float32),
            jax.ShapeDtypeStruct((8, width), jnp.float32),
        ],
        compiler_params=pltpu.CompilerParams(vmem_limit_bytes=32 * 2**20),
        name="return_rows",
    )(me, length, *operands)


def finish_kernel(
    me_ref, length_ref, near_ref, got_ref, out_near_ref, out_got_ref, order_ref, first_ref, grad_ref, tokens_ref, gains_ref,
    result_out, grad_out,
):
    rows = tokens_ref.shape[0]
    grad = near_ref[...] + got_ref[...].astype(jnp.float32)
    tokens = tokens_ref[...]
    scale = lax.rsqrt(jnp.mean(tokens * tokens, axis=-1, keepdims=True) + EPSILON)
    unit = tokens * scale
    pulled = grad * gains_ref[2:3]
    grad_out[...] = grad_ref[...] + scale * (pulled - unit * jnp.mean(pulled * unit, axis=-1, keepdims=True))
    high, low = split_low(out_near_ref[...] + out_got_ref[...].astype(jnp.float32))
    added = dot(order_ref[...], high) + dot(order_ref[...], low)
    result_out[...] = jnp.where(live_rows(me_ref, length_ref, rows), first_ref[...] + added, 0.0)


def finish_rows(me, length, *operands):
    shape = operands[5].shape
    smem, vmem = (pl.BlockSpec(memory_space=pltpu.SMEM), pl.BlockSpec(memory_space=pltpu.VMEM))
    return pl.pallas_call(
        finish_kernel,
        in_specs=[smem, smem] + [vmem] * 9,
        out_specs=[vmem] * 2,
        out_shape=[jax.ShapeDtypeStruct(shape, jnp.float32)] * 2,
        compiler_params=pltpu.CompilerParams(vmem_limit_bytes=32 * 2**20),
        name="finish_rows",
    )(me, length, *operands)


def body(
    tokens,
    routes,
    lengths,
    cotangent,
    in_weight,
    select_weight,
    step_weight,
    out_weight,
    router_weight,
    up_weight,
    down_weight,
    conv_weight,
    conv_bias,
    step_bias,
    decay_log,
    skip_gain,
    mixer_gain,
    expert_gain,
):
    f32, bf16 = (jnp.float32, jnp.bfloat16)
    span, width = tokens.shape
    groups, parts = (lax.axis_size("grp"), lax.axis_size("shard"))
    me, group = (lax.axis_index("shard"), lax.axis_index("grp"))
    total = span * parts
    inside = conv_bias.shape[0]
    tiles = inside // LANES
    slab = in_weight.shape[0]
    hidden_cols = up_weight.shape[2] // parts
    share = width // groups
    bits = [2**i for i in range(groups.bit_length() - 1)]
    down_bit = 2 if share % 8 == 0 else bits[-1]
    pair = 2 * share if share % 8 == 0 else width // 2
    odd, second = (group % 2, (group // down_bit) % 2)
    me_one = jnp.full((1,), me, jnp.int32)
    source = [me, me ^ 1, me ^ (2 + odd), me ^ (3 - odd), odd, second]
    source = jnp.stack(source).astype(jnp.int32)

    first = (routes[:, 0] == 0).astype(jnp.int32)
    count_first = jnp.sum(first)
    small = jnp.concatenate(
        [
            router_weight.astype(f32).T,
            mixer_gain.astype(f32)[None],
            expert_gain.astype(f32)[None],
            jnp.full((1, slab), count_first, jnp.int32).astype(f32),
            jnp.zeros((11, slab), f32),
        ],
        axis=0,
    )
    small = [small] + [swap(small, k) for k in range(1, parts)]
    in_pieces, up_pieces = cut_weights(source[:3], in_weight, up_weight, parts, inside)
    in_pieces = share_pieces(in_pieces)
    normed, gains = norm_rows(me_one, tokens, small)
    normed_pieces = gather_pieces(normed)
    counts = gains[4].reshape(parts, slab)[:, 0].astype(jnp.int32)

    goal = jnp.where(first > 0, jnp.cumsum(first), count_first + jnp.cumsum(1 - first)) - 1
    slots = jnp.arange(span, dtype=jnp.int32)
    order = (slots[:, None] == goal[None, :]).astype(bf16)
    order_t = (goal[:, None] == slots[None, :]).astype(bf16)
    live = (me * span + slots < lengths[0])[:, None]
    cots = matmul(order, jnp.where(live, cotangent, 0.0).astype(bf16)).astype(bf16)
    cot_pieces = gather_pieces(cots)

    taps = conv_weight.astype(f32)
    spare = LANES - select_weight.shape[1]
    select_wide = jnp.pad(select_weight, ((0, 0), (0, spare)))
    inner, zgate, summed, conv_out, conv_low, selected = project(
        me_one,
        source,
        lengths,
        normed_pieces,
        in_pieces,
        taps,
        conv_bias.astype(f32)[None, :],
        select_wide,
    )
    selected = tie(selected + swap(selected, 1), cot_pieces[2])
    selected = selected + swap(selected, 2)
    up_pieces = share_pieces([up_pieces[0], up_pieces[1], tie(up_pieces[2], selected)])
    step_wide = jnp.pad(step_weight, ((0, LANES - R), (0, 0)))
    step_row = step_bias.astype(f32)[None, :]
    decay = -jnp.exp(decay_log.astype(f32))
    rate = pack(decay * LOG2E, tiles)
    skip = skip_gain.astype(f32)[None, :]
    states, end, mixed, gated, held, given = mixer(
        me_one, lengths, selected, conv_out, zgate, step_wide, step_row, skip, rate, out_weight, span, tiles
    )
    near, given = scatter_near(held, tie(given, up_pieces[2]))
    first_sum, normed_two, sent, probs = route(
        me_one, lengths, tokens, near, swap(given, 2), gains, order, routes
    )
    fours, eights = (groups // 4, groups // 8)
    fine = hidden_cols // fours % LANES == 0 and share % 16 == 0
    grad_held, grad_given, out_held, out_given, packed = experts(
        me_one, source, counts, gather_pieces(sent), cot_pieces, up_pieces, down_weight, fours if fine else 1
    )
    up_cols = hidden_cols // fours
    if not fine:
        up_rows = packed[0, :, : E * slab].reshape(parts, E * slab, fours, up_cols).transpose(2, 0, 1, 3)
        down_rows = packed[0, :, E * slab :].reshape(parts, E, fours, share, fours, up_cols)
        down_rows = down_rows.transpose(2, 0, 1, 4, 3, 5).reshape(fours, parts, E * fours * share, up_cols)
        down_rows = down_rows.swapaxes(0, 1).reshape(fours, parts, E * fours * share, up_cols)
        packed = jnp.concatenate([up_rows, down_rows], axis=2)
    packed = packed.reshape(groups, 2 * E * slab, up_cols)
    packed = lax.psum_scatter(packed, "grp", scatter_dimension=0, tiled=True)
    up_sum, down_sum = (packed[:, : E * slab], packed[:, E * slab :])
    near, given = scatter_near(grad_held, grad_given)
    grad_first, grad_first_low, expert_gain_grad, router_grad = return_rows(
        me_one,
        lengths,
        near,
        swap(given, 2),
        order_t,
        normed_two,
        probs,
        routes,
        first_sum,
        cotangent,
        gains,
    )
    grad_pieces = gather_pieces(grad_first_low)
    top = bits[-1]
    out_bits = [bit for bit in bits[:0:-1] if bit != down_bit]
    blocks = (groups // 4, 2, share, inside)
    grad_mixed, grad_zgate, gate_held, gate_given, out_grad_held, out_grad_given = gate_back(
        me_one, source, normed_pieces, grad_pieces, zgate, mixed, gated, out_weight, pair
    )
    gate_got, out_grad_got = (swap_groups(gate_given, 1), swap_groups(out_grad_given, down_bit))
    conv_part, grad_selected, step_grad, step_bias_grad, skip_grad, rate_grad = mixer_back(
        lengths, selected, conv_out, grad_mixed, states, end, step_wide, step_row, skip, rate, tiles
    )
    chip_selected = grad_selected + swap(grad_selected, 1)
    gate_held, gate_given = halve((gate_held, gate_got), 0, 2, chip_selected)
    gate_got = swap_groups(gate_given, 2)
    out_parts = (out_grad_held.reshape(blocks), out_grad_got.reshape(blocks))
    out_grad_held, out_grad_given = halve(out_parts, 1, 1, chip_selected)
    out_grad_got = swap_groups(out_grad_given, 1)

    def up_home(g, s):
        return (s * fours + g // 4) * parts + g % 4

    def in_home(g, s):
        half, k = (g // (groups // 2), (g // 4) % eights)
        return (half * (groups // 2) + s * eights + k) * parts + g % 4

    both_axes = ("grp", "shard")
    places = [(g, s) for g in range(groups) for s in range(parts)]
    up_sum = lax.ppermute(tie(up_sum, chip_selected), both_axes, [(g * parts + s, up_home(g, s)) for g, s in places])
    grad_selected = (chip_selected + swap(chip_selected, 2)).astype(bf16)
    inner_grad, inner_held, inner_given, select_grad, conv_grad, conv_bias_grad = conv_back(
        me_one,
        source,
        lengths,
        normed_pieces,
        grad_selected,
        conv_part,
        summed,
        inner,
        conv_low,
        taps,
        select_wide,
    )
    inner_got = swap_groups(inner_given, 1)
    held, given, mixer_part = project_back(
        me_one, source, normed_pieces, in_pieces, inner_grad, grad_zgate
    )
    inner_held, inner_given = halve((inner_held, inner_got), 0, 2, given)
    inner_got = swap_groups(inner_given, 2)
    gate_sum = join(gate_held, gate_got, inner_held)
    for bit in out_bits:
        out_grad_held, out_grad_given = halve((out_grad_held, out_grad_got), 0, bit, inner_held)
        out_grad_got = swap_groups(out_grad_given, bit)
    shared = jnp.concatenate([router_grad[0:E], expert_gain_grad, mixer_part / gains[2:3]], axis=0)
    shared = shared + swap(shared, 1)
    shared = tie(shared + swap(shared, 2), inner_held)
    shared = lax.dynamic_slice_in_dim(shared, me * slab, slab, 1)
    decay_grad = decay * unpack(rate_grad, tiles)
    picked = select_weight.shape[1]
    few = [
        select_grad[:picked],
        conv_grad[:KW],
        conv_bias_grad,
        step_grad[:R],
        decay_grad,
        step_bias_grad,
        skip_grad,
        shared.reshape(2, inside),
    ]
    starts = [0]
    for part in few:
        starts.append(starts[-1] + part.shape[0])
    few = jnp.concatenate(few, axis=0).astype(bf16)
    few_got = swap_groups(few, 1)
    near, given = scatter_near(held, given, inner_held)
    got = swap(given, 2)
    out_near, out_given = scatter_near(out_held, out_given, inner_held)
    out_got = swap(out_given, 2)
    few = join(few, few_got, given, out_given).astype(bf16)
    few_got = swap_groups(few, 2)

    inner_sum = join(inner_held, inner_got, few)
    for bit in bits[-2:1:-1]:
        inner_held, inner_given = halve(inner_sum, 2, bit)
        inner_sum = join(inner_held, swap_groups(inner_given, bit))
        gate_held, gate_given = halve(gate_sum, 2, bit)
        gate_sum = join(gate_held, swap_groups(gate_given, bit))
    upper = group >= top
    own = jnp.where(upper, gate_sum, inner_sum).reshape(slab, inside // eights).astype(bf16)
    other = jnp.where(upper, inner_sum, gate_sum).reshape(slab, inside // eights).astype(bf16)
    own = lax.ppermute(own, both_axes, [(g * parts + s, in_home(g, s)) for g, s in places])
    other = lax.ppermute(other, both_axes, [(g * parts + s, in_home(g ^ top, s)) for g, s in places])
    few = join(few, few_got, inner_sum).astype(bf16)
    few_got = swap_groups(few, bits[2])
    out_sum = join(out_grad_held, out_grad_got, inner_sum).reshape(share, inside)
    result, tokens_grad = finish_rows(
        tie(me_one, few),
        lengths,
        near,
        got,
        out_near,
        out_got,
        order_t,
        first_sum,
        grad_first,
        tokens,
        gains,
    )
    in_sum = join(own, other, result)
    few = total_rest(join(few, few_got, result, up_sum), bits[3:])
    few = [few[a:b] for a, b in zip(starts[:-1], starts[1:])]
    select_grad, conv_grad, conv_bias_grad, step_grad, decay_grad, step_bias_grad, skip_grad, shared = few
    shared = shared.reshape(4, slab)
    up_sum = up_sum.astype(f32).reshape(E, slab, up_cols)
    down_sum = down_sum.astype(f32).reshape(E, fours, share, up_cols).transpose(0, 2, 1, 3)
    down_sum = down_sum.reshape(E, share, hidden_cols)
    return (
        result,
        tokens_grad,
        in_sum,
        out_sum.T,
        up_sum,
        down_sum.transpose(0, 2, 1),
        select_grad.T,
        step_grad,
        shared[0:E].T,
        conv_grad,
        conv_bias_grad[0],
        step_bias_grad[0],
        decay_grad,
        skip_grad[0],
        shared[3],
        shared[2],
    )


def solution(mesh):
    return jax.shard_map(
        body,
        mesh=mesh,
        in_specs=(
            P(("grp", "shard"), None),
            P(("grp", "shard"), None),
            P("grp"),
            P(("grp", "shard"), None),
            P("shard", None),
            P("shard", None),
            P(None, "shard"),
            P("shard", None),
            P("shard", None),
            P(None, "shard", None),
            P(None, "shard", None),
            P(None, "shard"),
            P("shard"),
            P("shard"),
            P(None, "shard"),
            P("shard"),
            P("shard"),
            P("shard"),
        ),
        out_specs=(
            P(("grp", "shard"), None),
            P(("grp", "shard"), None),
            P("shard", "grp"),
            P("shard", "grp"),
            P(None, "shard", "grp"),
            P(None, "shard", "grp"),
            P("shard", None),
            P(None, "shard"),
            P("shard", None),
            P(None, "shard"),
            P("shard"),
            P("shard"),
            P(None, "shard"),
            P("shard"),
            P("shard"),
            P("shard"),
        ),
        check_vma=False,
    )
```

```python
import functools
import jax
import jax.numpy as jnp
from jax import lax
from jax.experimental import pallas as pl
from jax.experimental.pallas import tpu as pltpu
from jax.sharding import PartitionSpec as P

R = 72
KW = 4
E = 2
CAP = 192
EPSILON = 1e-05
FTILE = 768
LOG2E = 1.4426950408889634

NS = 16
LANES = 128
STEP = 8
CHUNK = 128


def swap(value, bit):
    size = lax.axis_size("shard")
    return lax.ppermute(value, "shard", [(i, i ^ bit) for i in range(size)])


def swap_groups(value, bit):
    size = lax.axis_size("grp")
    return lax.ppermute(value, "grp", [(g, g ^ bit) for g in range(size)])


def tie(value, *others):
    for other in others:
        corner = other[(0,) * other.ndim].astype(jnp.float32)
        value = value + (0.0 * corner).astype(value.dtype)
    return value


def gather_pieces(value):
    far = swap(value, 2)
    return (value, swap(value, 1), far, swap(far, 1))


def scatter_near(held, given, *others):
    side = lax.axis_index("shard") // 2
    held = tie(held + swap(given, 1).astype(jnp.float32), *others)
    mine = lax.dynamic_index_in_dim(held, side, 0, False)
    return mine, lax.dynamic_index_in_dim(held, 1 - side, 0, False).astype(jnp.bfloat16)


def halve(value, axis, bit, *others):
    mine = (lax.axis_index("grp") // bit) % 2
    terms = value if isinstance(value, tuple) else (value,)
    size = terms[0].shape[axis] // 2

    def side(index):
        picked = [lax.dynamic_slice_in_dim(term, index * size, size, axis) for term in terms]
        total = picked[0].astype(jnp.float32)
        for term in picked[1:]:
            total = total + term.astype(jnp.float32)
        return tie(total, *others)

    return side(mine), side(1 - mine).astype(jnp.bfloat16)


def join(held, got, *others):
    return tie(held.astype(jnp.float32) + got.astype(jnp.float32), *others)


def share_pieces(pieces):
    groups, parts = (lax.axis_size("grp"), lax.axis_size("shard"))
    moves = [
        (g * parts + s, g * parts + (s ^ (2 + g % 2))) for g in range(groups) for s in range(parts)
    ]
    crossed = lax.ppermute(pieces[2], ("grp", "shard"), moves)
    shared = lax.ppermute(crossed, "grp", [(g, g ^ 1) for g in range(groups)])
    return [pieces[0], swap(pieces[1], 1), crossed, shared]


def exchange(value, bits):
    return [value] + [swap_groups(value, sum(bits[i] for i in range(len(bits)) if k >> i & 1)) for k in range(1, 2 ** len(bits))]


def balanced(terms, *others):
    terms = [term.astype(jnp.float32) for term in terms]
    while len(terms) > 1:
        terms = [terms[i] + terms[i + 1] for i in range(0, len(terms), 2)]
    return tie(terms[0], *others)


def total_rest(value, bits, kind=jnp.bfloat16):
    for bit in bits:
        value = balanced(exchange(value.astype(kind), [bit]))
    return value


def matmul(left, right):
    return jnp.dot(left, right, preferred_element_type=jnp.float32)


def pack(value, tiles):
    edge = tiles * LANES
    full = value[:, :edge].reshape(2, 8, tiles, LANES).transpose(2, 0, 1, 3)
    rest = jnp.concatenate([value[:8, edge:], value[8:, edge:]], axis=1)
    return jnp.concatenate([full.reshape(2 * tiles, 8, LANES), rest[None]], axis=0)


def unpack(value, tiles):
    full = value[: 2 * tiles].reshape(tiles, 2, 8, LANES).transpose(1, 2, 0, 3)
    rest = value[2 * tiles]
    rest = jnp.concatenate([rest[:, : LANES // 2], rest[:, LANES // 2 :]], axis=0)
    return jnp.concatenate([full.reshape(NS, tiles * LANES), rest], axis=1)


def fold_rows(parts):
    row = lax.broadcasted_iota(jnp.int32, (8, LANES), 0)
    top, pair, even = (row < 4, (row & 2) == 0, (row & 1) == 0)
    fours = [
        jnp.where(top, parts[i], parts[i + 4])
        + pltpu.roll(jnp.where(top, parts[i + 4], parts[i]), 4, 0)
        for i in range(4)
    ]
    twos = [
        jnp.where(
            pair,
            fours[i] + pltpu.roll(fours[i], 6, 0),
            fours[i + 2] + pltpu.roll(fours[i + 2], 2, 0),
        )
        for i in range(2)
    ]
    return jnp.where(
        even, twos[0] + pltpu.roll(twos[0], 7, 0), twos[1] + pltpu.roll(twos[1], 1, 0)
    )


def halves(pair_ref, at, left):
    low, high = (pair_ref[at, 0:8], pair_ref[at, 8:16])
    return (low, high, jnp.where(left, low, high))


def scan_forward_chunk(tiles, dt_ref, dx_ref, entry_ref, read_ref, rate_ref, out_ref, state_ref, end_ref, held):
    left = lax.broadcasted_iota(jnp.int32, (8, LANES), 1) < LANES // 2

    def group(g, states):
        at, base = (g, g * STEP)
        states = list(states)
        entry = [halves(entry_ref, base + t, left) for t in range(STEP)]
        read = [halves(read_ref, base + t, left) for t in range(STEP)]
        for tile in range(tiles + 1):
            columns = slice(tile * LANES, (tile + 1) * LANES)
            rows = [2 * tile] if tile == tiles else [2 * tile, 2 * tile + 1]
            which = [2] if tile == tiles else [0, 1]
            sums = []
            for t in range(STEP):
                step = dt_ref[at, t : t + 1, columns]
                fed = dx_ref[at, t : t + 1, columns]
                total = None
                for r, w in zip(rows, which):
                    state_ref[base + t, r] = states[r]
                    states[r] = jnp.exp2(step * rate_ref[r]) * states[r] + entry[t][w] * fed
                    term = read[t][w] * states[r]
                    total = term if total is None else total + term
                sums.append(total)
            out_ref[at, :, columns] = fold_rows(sums)
        return tuple(states)

    count = 2 * tiles + 1
    states = lax.fori_loop(0, dt_ref.shape[0], group, tuple(held[r] for r in range(count)))
    for r in range(count):
        held[r] = states[r]
        end_ref[r] = states[r]


def scan_backward_chunk(
    tiles, dt_ref, dx_ref, grad_ref, entry_ref, read_ref, rate_ref, state_ref,
    fed_out, step_out, entry_out, read_out, rate_out, flow, after,
):
    count = 2 * tiles + 1
    left = lax.broadcasted_iota(jnp.int32, (8, LANES), 1) < LANES // 2
    groups = dt_ref.shape[0]

    def group(g, carry):
        at = groups - 1 - g
        base = at * STEP
        flows, afters = (list(carry[0]), list(carry[1]))
        entry = [halves(entry_ref, base + t, left) for t in range(STEP)]
        read = [halves(read_ref, base + t, left) for t in range(STEP)]
        entry_sum = [[None, None] for _ in range(STEP)]
        read_sum = [[None, None] for _ in range(STEP)]
        for tile in range(tiles + 1):
            last = tile == tiles
            columns = slice(tile * LANES, (tile + 1) * LANES)
            rows = [2 * tile] if last else [2 * tile, 2 * tile + 1]
            which = [2] if last else [0, 1]
            fed_sums, step_sums = ([None] * STEP, [None] * STEP)
            rate_sum = [rate_out[r] for r in rows]
            for t in reversed(range(STEP)):
                step = dt_ref[at, t : t + 1, columns]
                fed = dx_ref[at, t : t + 1, columns]
                grad = grad_ref[at, t : t + 1, columns]
                for i, (r, w) in enumerate(zip(rows, which)):
                    before = state_ref[base + t, r]
                    arriving = flows[r] + read[t][w] * grad
                    entry_term = arriving * fed
                    read_term = afters[r] * grad
                    fed_term = entry[t][w] * arriving
                    leaving = jnp.exp2(step * rate_ref[r]) * arriving
                    product = leaving * before
                    step_term = product * rate_ref[r]
                    rate_sum[i] = rate_sum[i] + product * step
                    flows[r] = leaving
                    afters[r] = before
                    fed_sums[t] = fed_term if i == 0 else fed_sums[t] + fed_term
                    step_sums[t] = step_term if i == 0 else step_sums[t] + step_term
                    for total, term in ((entry_sum[t], entry_term), (read_sum[t], read_term)):
                        if last:
                            total[0] = total[0] + jnp.where(left, term, 0.0)
                            total[1] = total[1] + jnp.where(left, 0.0, term)
                        else:
                            total[i] = term if total[i] is None else total[i] + term
            fed_out[at, :, columns] = fold_rows(fed_sums)
            step_out[at, :, columns] = fold_rows(step_sums)
            for i, r in enumerate(rows):
                rate_out[r] = rate_sum[i]
        for t in range(STEP):
            for i in range(2):
                entry_out[base + STEP - 1 - t, 8 * i : 8 * i + 8] = entry_sum[t][i]
                read_out[base + STEP - 1 - t, 8 * i : 8 * i + 8] = read_sum[t][i]
        return (tuple(flows), tuple(afters))

    flows, afters = lax.fori_loop(
        0,
        groups,
        group,
        (tuple(flow[r] for r in range(count)), tuple(after[r] for r in range(count))),
    )
    for r in range(count):
        flow[r] = flows[r]
        after[r] = afters[r]


def split_low(value):
    high = value.astype(jnp.bfloat16)
    return high, (value - high.astype(jnp.float32)).astype(jnp.bfloat16)


def dot(left, right):
    return jnp.dot(left, right, preferred_element_type=jnp.float32)


def dot_t(left, right):
    return lax.dot_general(left, right, (((1,), (1,)), ((), ())), preferred_element_type=jnp.float32)


def t_dot(left, right):
    return lax.dot_general(left, right, (((0,), (0,)), ((), ())), preferred_element_type=jnp.float32)


def live_rows(me_ref, length_ref, rows):
    slot = me_ref[0] * rows + lax.broadcasted_iota(jnp.int32, (rows, 1), 0)
    return slot < length_ref[0]


def router_rows(gains_ref):
    row = lax.broadcasted_iota(jnp.int32, gains_ref.shape, 0)
    return jnp.where(row < E, gains_ref[...], 0.0).astype(jnp.bfloat16)


def cut_kernel(parts, inside, cols, goal_ref, in_ref, up_ref, *rest):
    number = len(rest) // 2
    in_outs, up_outs, sems = (rest[:number], rest[number : 2 * number], rest[-1])
    copies = []
    for k in range(number):
        columns = pl.ds(pl.multiple_of(goal_ref[k] * cols, LANES), cols)
        copies.append(pltpu.make_async_copy(up_ref.at[:, :, columns], up_outs[k], sems.at[k]))
        copies[-1].start()
    for d in range(parts):
        for k in range(number):

            @pl.when(goal_ref[k] == d)
            def write():
                in_outs[k][:, :inside] = in_ref[:, d * inside : (d + 1) * inside]
                at = (parts + d) * inside
                in_outs[k][:, inside:] = in_ref[:, at : at + inside]

    for copy in copies:
        copy.wait()


def cut_weights(goal, in_weight, up_weight, parts, inside):
    slab = in_weight.shape[0]
    cols = up_weight.shape[2] // parts
    number = 3
    in_shape = jax.ShapeDtypeStruct((slab, 2 * inside), in_weight.dtype)
    up_shape = jax.ShapeDtypeStruct((up_weight.shape[0], slab, cols), up_weight.dtype)
    vmem, anywhere = (pl.BlockSpec(memory_space=pltpu.VMEM), pl.BlockSpec(memory_space=pl.ANY))
    outs = pl.pallas_call(
        functools.partial(cut_kernel, parts, inside, cols),
        in_specs=[pl.BlockSpec(memory_space=pltpu.SMEM), vmem, anywhere],
        out_specs=[vmem] * number + [anywhere] * number,
        out_shape=[in_shape] * number + [up_shape] * number,
        scratch_shapes=[pltpu.SemaphoreType.DMA((number,))],
        compiler_params=pltpu.CompilerParams(vmem_limit_bytes=24 * 2**20),
        name="cut_weights",
    )(goal, in_weight, up_weight)
    return outs[:number], outs[number:]


def to_power(value):
    return value / (1.0 + jnp.exp(-value))


def project_kernel(parts, inside, me_ref, source_ref, length_ref, *rest):
    normed_refs, weight_refs, rest = (rest[:parts], rest[parts : 2 * parts], rest[2 * parts :])
    taps_ref, bias_ref, select_ref, inner_out, gate_out, summed_out, conv_out, low_out, selected_out = rest[:9]
    normed, weight, shifted, sems = rest[9:]
    block = pl.program_id(0)
    me = me_ref[0]
    rows, slab = (normed_refs[0].shape[0], weight_refs[0].shape[0])

    @pl.when(block == 0)
    def fetch():
        copies = []
        for k in range(parts):
            at = pl.ds(pl.multiple_of(source_ref[k] * slab, 16), slab)
            copies.append(pltpu.make_async_copy(weight_refs[k], weight.at[at], sems.at[k]))
            at = pl.ds(pl.multiple_of((me ^ k) * rows, 16), rows)
            copies.append(pltpu.make_async_copy(normed_refs[k], normed.at[at], sems.at[parts + k]))
        for copy in copies:
            copy.start()
        for copy in copies:
            copy.wait()
        shifted[0:8] = jnp.zeros((8, inside), jnp.float32)

    start = pl.multiple_of(block * rows, 16)
    projected = jnp.dot(normed[pl.ds(start, rows)], weight[...], preferred_element_type=jnp.float32)
    slot = block * rows + lax.broadcasted_iota(jnp.int32, (rows, 1), 0)
    inner = jnp.where(slot < length_ref[0], projected[:, :inside], 0.0)
    gate_out[...] = projected[:, inside:]
    inner_out[...] = inner
    shifted[8:] = inner
    summed = bias_ref[...]
    for k in range(KW):
        summed = summed + taps_ref[k : k + 1] * shifted[8 - (KW - 1) + k : 8 - (KW - 1) + k + rows]
    shifted[0:8] = shifted[rows : rows + 8]
    summed_out[...] = summed
    value = to_power(summed)
    conv_out[...] = value
    low = value.astype(jnp.bfloat16)
    low_out[...] = low
    selected_out[...] = jnp.dot(low, select_ref[...], preferred_element_type=jnp.float32)


def project(me, source, length, normed_pieces, weight_pieces, taps, bias, select_wide):
    parts = len(normed_pieces)
    rows, width = normed_pieces[0].shape
    slab, both = weight_pieces[0].shape
    inside, picked = select_wide.shape
    total = rows * parts
    smem, anywhere = (pl.BlockSpec(memory_space=pltpu.SMEM), pl.BlockSpec(memory_space=pl.ANY))
    vmem = pl.BlockSpec(memory_space=pltpu.VMEM)
    row = pl.BlockSpec((rows, inside), lambda i: (i, 0))
    wide = jax.ShapeDtypeStruct((total, inside), jnp.float32)
    return pl.pallas_call(
        functools.partial(project_kernel, parts, inside),
        grid=(parts,),
        in_specs=[smem] * 3 + [anywhere] * (2 * parts) + [vmem] * 3,
        out_specs=[row] * 5 + [pl.BlockSpec((rows, picked), lambda i: (i, 0))],
        out_shape=[wide] * 4
        + [
            jax.ShapeDtypeStruct((total, inside), jnp.bfloat16),
            jax.ShapeDtypeStruct((total, picked), jnp.float32),
        ],
        scratch_shapes=[
            pltpu.VMEM((total, width), jnp.bfloat16),
            pltpu.VMEM((slab * parts, both), jnp.bfloat16),
            pltpu.VMEM((rows + 8, inside), jnp.float32),
            pltpu.SemaphoreType.DMA((2 * parts,)),
        ],
        compiler_params=pltpu.CompilerParams(vmem_limit_bytes=40 * 2**20),
        cost_estimate=pl.CostEstimate(flops=4 * 10**9, bytes_accessed=2**20, transcendentals=0),
        name="project",
    )(me, source, length, *normed_pieces, *weight_pieces, taps, bias, select_wide)


def live_slots(start, length_ref, rows):
    return start + lax.broadcasted_iota(jnp.int32, (rows, 1), 0) < length_ref[0]


def store_wide(ref, value):
    groups, _, width = ref.shape
    inside = value.shape[1]
    ref[:, :, :inside] = value.reshape(groups, STEP, inside)
    ref[:, :, inside:] = value[:, 2 * inside - width :].reshape(groups, STEP, width - inside)


def load_narrow(ref, inside):
    groups, _, width = ref.shape
    edge = 2 * inside - width
    value = ref[...].reshape(groups * STEP, width)
    return jnp.concatenate([value[:, :edge], value[:, edge:inside] + value[:, inside:]], axis=1)


def store_spread(entry_ref, read_ref, selected):
    turned = selected.T
    for t in range(selected.shape[0]):
        entry_ref[t] = jnp.broadcast_to(turned[R : R + NS, t : t + 1], (NS, LANES))
        read_ref[t] = jnp.broadcast_to(turned[R + NS : R + 2 * NS, t : t + 1], (NS, LANES))


def step_sizes(selected, weight_ref, bias_ref, live):
    low = selected.astype(jnp.bfloat16)
    pre = dot(low, weight_ref[...]) + bias_ref[...]
    soft = jnp.maximum(pre, 0.0) + jnp.log1p(jnp.exp(-jnp.abs(pre)))
    return low, pre, jnp.where(live, soft, 0.0)


def mixer_kernel(
    tiles, share, me_ref, length_ref, selected_ref, conv_ref, gate_ref, weight_ref, bias_ref, skip_ref, rate_ref, project_ref,
    state_ref, end_ref, mixed_out, gated_out, held_out, given_out,
    dt_ref, dx_ref, entry_ref, read_ref, out_ref, held,
):
    chunk, inside = conv_ref.shape
    step = pl.program_id(0)

    @pl.when(step == 0)
    def start():
        held[...] = jnp.zeros_like(held)

    selected, conv = (selected_ref[...], conv_ref[...])
    live = live_slots(step * chunk, length_ref, chunk)
    _, _, size = step_sizes(selected, weight_ref, bias_ref, live)
    store_wide(dt_ref, size)
    store_wide(dx_ref, size * conv)
    store_spread(entry_ref, read_ref, selected)
    scan_forward_chunk(tiles, dt_ref, dx_ref, entry_ref, read_ref, rate_ref, out_ref, state_ref, end_ref, held)
    mixed = load_narrow(out_ref, inside) + skip_ref[...] * conv
    mixed_out[...] = mixed
    gated = (mixed * to_power(gate_ref[...])).astype(jnp.bfloat16)
    gated_out[...] = gated
    part = dot(gated, project_ref[...])
    block = step // share
    rows = pl.ds(pl.multiple_of((step % share) * chunk, chunk), chunk)

    @pl.when(block % 2 == me_ref[0] % 2)
    def keep():
        held_out[0, rows] = part

    @pl.when(block % 2 != me_ref[0] % 2)
    def give():
        given_out[0, rows] = part.astype(jnp.bfloat16)


def mixer(me, length, selected, conv_out, zgate, step_wide, bias, skip, rate, out_weight, span, tiles):
    total, inside = conv_out.shape
    width = out_weight.shape[1]
    count = 2 * tiles + 1
    chunk = CHUNK
    wide = (tiles + 1) * LANES
    share = span // chunk
    smem, vmem = (pl.BlockSpec(memory_space=pltpu.SMEM), pl.BlockSpec(memory_space=pltpu.VMEM))
    row = pl.BlockSpec((chunk, inside), lambda i: (i, 0))
    part = pl.BlockSpec((1, span, width), lambda i: (i // (2 * share), 0, 0))
    f32, bf16 = (jnp.float32, jnp.bfloat16)
    return pl.pallas_call(
        functools.partial(mixer_kernel, tiles, share),
        grid=(total // chunk,),
        in_specs=[smem, smem, pl.BlockSpec((chunk, LANES), lambda i: (i, 0)), row, row] + [vmem] * 5,
        out_specs=[pl.BlockSpec((chunk, count, 8, LANES), lambda i: (i, 0, 0, 0)), vmem, row, row, part, part],
        out_shape=[
            jax.ShapeDtypeStruct((total, count, 8, LANES), f32),
            jax.ShapeDtypeStruct((count, 8, LANES), f32),
            jax.ShapeDtypeStruct((total, inside), f32),
            jax.ShapeDtypeStruct((total, inside), bf16),
            jax.ShapeDtypeStruct((2, span, width), f32),
            jax.ShapeDtypeStruct((2, span, width), bf16),
        ],
        scratch_shapes=[pltpu.VMEM((chunk // STEP, STEP, wide), f32)] * 2
        + [pltpu.VMEM((chunk, NS, LANES), f32)] * 2
        + [pltpu.VMEM((chunk // STEP, STEP, wide), f32), pltpu.VMEM((count, 8, LANES), f32)],
        compiler_params=pltpu.CompilerParams(vmem_limit_bytes=40 * 2**20),
        cost_estimate=pl.CostEstimate(flops=4 * 10**9, bytes_accessed=2**20, transcendentals=0),
        name="mixer",
    )(me, length, selected, conv_out, zgate, step_wide, bias, skip, rate, out_weight)


def row_sums(value):
    high, low = split_low(value)
    ones = jnp.ones((8, LANES), jnp.bfloat16)
    return dot_t(ones, high) + dot_t(ones, low)


def mixer_back_kernel(tiles, length_ref, *rest):
    (
        selected_ref, conv_ref, grad_ref, state_ref, end_ref, weight_ref, bias_ref, skip_ref, rate_ref,
        conv_out, rank_out, step_out, bias_out, skip_out, rate_out,
        dt_ref, dx_ref, mix_ref, entry_ref, read_ref, fed_ref, rise_ref, entry_parts, read_parts, flow, after,
    ) = rest
    chunk, inside = conv_ref.shape
    index = pl.program_id(0)
    step = pl.num_programs(0) - 1 - index

    @pl.when(index == 0)
    def start():
        flow[...] = jnp.zeros_like(flow)
        after[...] = end_ref[...]
        rate_out[...] = jnp.zeros_like(rate_out)
        step_out[...] = jnp.zeros_like(step_out)
        bias_out[...] = jnp.zeros_like(bias_out)
        skip_out[...] = jnp.zeros_like(skip_out)

    conv, grad_mixed = (conv_ref[...], grad_ref[...])
    skip_out[...] += jnp.sum(grad_mixed * conv, axis=0, keepdims=True)
    selected = selected_ref[...]
    live = live_slots(step * chunk, length_ref, chunk)
    low, pre, size = step_sizes(selected, weight_ref, bias_ref, live)
    store_wide(dt_ref, size)
    store_wide(dx_ref, size * conv)
    store_wide(mix_ref, grad_mixed)
    store_spread(entry_ref, read_ref, selected)
    scan_backward_chunk(
        tiles, dt_ref, dx_ref, mix_ref, entry_ref, read_ref, rate_ref, state_ref,
        fed_ref, rise_ref, entry_parts, read_parts, rate_out, flow, after,
    )
    fed = load_narrow(fed_ref, inside)
    grad_size = load_narrow(rise_ref, inside) * (1.0 / LOG2E) + fed * conv
    grad_pre = jnp.where(live, grad_size / (1.0 + jnp.exp(-pre)), 0.0)
    bias_out[...] += jnp.sum(grad_pre, axis=0, keepdims=True)
    grad_low = grad_pre.astype(jnp.bfloat16)
    rank = dot_t(grad_low, weight_ref[...])
    sums = [row_sums(part[...].reshape(chunk * NS, LANES)) for part in (entry_parts, read_parts)]
    lane = lax.broadcasted_iota(jnp.int32, (STEP, LANES), 1)
    for g in range(chunk // STEP):
        total = rank[g * STEP : (g + 1) * STEP]
        for i, part in enumerate(sums):
            start = R + i * NS
            moved = pltpu.roll(part[:, g * LANES : (g + 1) * LANES], start + NS, 1)
            moved = pltpu.roll(moved, 0, 1, stride=NS, stride_axis=0)
            total = jnp.where((lane >= start) & (lane < start + NS), moved, total)
        rank_out[g * STEP : (g + 1) * STEP] = total
    step_out[...] += t_dot(low, grad_low)
    conv_out[...] = fed * size + skip_ref[...] * grad_mixed


def mixer_back(length, selected, conv_out, grad_mixed, states, end, step_wide, bias, skip, rate, tiles):
    total, inside = conv_out.shape
    count = 2 * tiles + 1
    chunk = CHUNK
    steps = total // chunk
    wide = (tiles + 1) * LANES
    smem, vmem = (pl.BlockSpec(memory_space=pltpu.SMEM), pl.BlockSpec(memory_space=pltpu.VMEM))
    row = pl.BlockSpec((chunk, inside), lambda i: (steps - 1 - i, 0))
    lane = pl.BlockSpec((chunk, LANES), lambda i: (steps - 1 - i, 0))
    f32 = jnp.float32
    one = jax.ShapeDtypeStruct((1, inside), f32)
    return pl.pallas_call(
        functools.partial(mixer_back_kernel, tiles),
        grid=(steps,),
        in_specs=[smem, lane, row, row]
        + [pl.BlockSpec((chunk, count, 8, LANES), lambda i: (steps - 1 - i, 0, 0, 0))]
        + [vmem] * 5,
        out_specs=[row, lane] + [vmem] * 4,
        out_shape=[
            jax.ShapeDtypeStruct((total, inside), f32),
            jax.ShapeDtypeStruct((total, LANES), f32),
            jax.ShapeDtypeStruct((LANES, inside), f32),
            one,
            one,
            jax.ShapeDtypeStruct((count, 8, LANES), f32),
        ],
        scratch_shapes=[pltpu.VMEM((chunk // STEP, STEP, wide), f32)] * 3
        + [pltpu.VMEM((chunk, NS, LANES), f32)] * 2
        + [pltpu.VMEM((chunk // STEP, STEP, wide), f32)] * 2
        + [pltpu.VMEM((chunk, NS, LANES), f32)] * 2
        + [pltpu.VMEM((count, 8, LANES), f32)] * 2,
        compiler_params=pltpu.CompilerParams(vmem_limit_bytes=48 * 2**20),
        cost_estimate=pl.CostEstimate(flops=4 * 10**9, bytes_accessed=2**20, transcendentals=0),
        name="mixer_back",
    )(length, selected, conv_out, grad_mixed, states, end, step_wide, bias, skip, rate)


def gate_back_kernel(parts, pair, me_ref, source_ref, *rest):
    normed_refs, grad_refs, rest = (rest[:parts], rest[parts : 2 * parts], rest[2 * parts :])
    (
        gate_ref, mixed_ref, gated_ref, project_ref,
        mix_out, gate_out, gate_held, gate_given, out_held, out_given,
        normed, grads, lows, product, sems,
    ) = rest
    block = pl.program_id(0)
    rows, width = normed_refs[0].shape
    slab = width // parts
    me, odd, second = (me_ref[0], source_ref[parts], source_ref[parts + 1])

    def fetched(refs, target, base, k):
        at = pl.ds(pl.multiple_of((me ^ k) * rows, 16), rows)
        return pltpu.make_async_copy(refs[k], target.at[at], sems.at[base + k])

    @pl.when(block == 0)
    def fetch():
        for k in range(parts):
            fetched(grad_refs, grads, parts, k).start()
        for k in range(parts):
            fetched(normed_refs, normed, 0, k).start()
        for k in range(parts):
            fetched(grad_refs, grads, parts, k).wait()

    at = pl.ds(pl.multiple_of(block * rows, rows), rows)
    grad = grads[at]
    grad_gated = dot_t(grad, project_ref[...])
    gate = gate_ref[...]
    curve = 1.0 / (1.0 + jnp.exp(-gate))
    mix_out[...] = grad_gated * (gate * curve)
    low = (grad_gated * mixed_ref[...] * (curve * (1.0 + gate * (1.0 - curve)))).astype(jnp.bfloat16)
    gate_out[...] = low
    lows[at] = low

    @pl.when(block == parts - 1)
    def finish():
        for k in range(parts):
            fetched(normed_refs, normed, 0, k).wait()
        product[...] = t_dot(normed[...], lows[...])
        for h in range(parts // 2):
            at = pl.ds(pl.multiple_of((2 * h + odd) * slab, 8), slab)
            gate_held[h] = product[at]
            at = pl.ds(pl.multiple_of((2 * h + 1 - odd) * slab, 8), slab)
            gate_given[h] = product[at].astype(jnp.bfloat16)
        product[...] = t_dot(grads[...], gated_ref[...])
        for h in range(width // (2 * pair)):
            at = pl.ds(pl.multiple_of((2 * h + second) * pair, 8), pair)
            out_held[h] = product[at]
            at = pl.ds(pl.multiple_of((2 * h + 1 - second) * pair, 8), pair)
            out_given[h] = product[at].astype(jnp.bfloat16)


def gate_back(me, source, normed_pieces, grad_pieces, zgate, mixed, gated, out_weight, pair):
    parts = len(normed_pieces)
    rows, width = normed_pieces[0].shape
    total, inside = gated.shape
    slab = width // parts
    smem, anywhere = (pl.BlockSpec(memory_space=pltpu.SMEM), pl.BlockSpec(memory_space=pl.ANY))
    vmem = pl.BlockSpec(memory_space=pltpu.VMEM)
    row = pl.BlockSpec((rows, inside), lambda i: (i, 0))
    f32, bf16 = (jnp.float32, jnp.bfloat16)
    gate_shape = (parts // 2, slab, inside)
    out_shape = (width // (2 * pair), pair, inside)
    return pl.pallas_call(
        functools.partial(gate_back_kernel, parts, pair),
        grid=(parts,),
        in_specs=[smem] * 2 + [anywhere] * (2 * parts) + [row] * 2 + [vmem] * 2,
        out_specs=[row] * 2 + [vmem] * 4,
        out_shape=[
            jax.ShapeDtypeStruct((total, inside), f32),
            jax.ShapeDtypeStruct((total, inside), bf16),
            jax.ShapeDtypeStruct(gate_shape, f32),
            jax.ShapeDtypeStruct(gate_shape, bf16),
            jax.ShapeDtypeStruct(out_shape, f32),
            jax.ShapeDtypeStruct(out_shape, bf16),
        ],
        scratch_shapes=[
            pltpu.VMEM((total, width), bf16),
            pltpu.VMEM((total, width), bf16),
            pltpu.VMEM((total, inside), bf16),
            pltpu.VMEM((width, inside), f32),
            pltpu.SemaphoreType.DMA((2 * parts,)),
        ],
        compiler_params=pltpu.CompilerParams(vmem_limit_bytes=48 * 2**20),
        cost_estimate=pl.CostEstimate(flops=4 * 10**9, bytes_accessed=2**20, transcendentals=0),
        name="gate_back",
    )(me, source, *normed_pieces, *grad_pieces, zgate, mixed, gated, out_weight)


def conv_back_kernel(parts, me_ref, source_ref, length_ref, *rest):
    normed_refs, rest = (rest[:parts], rest[parts:])
    (
        selected_ref, conv_ref, summed_ref, inner_ref, low_ref, taps_ref, select_ref,
        inner_out, inner_held, inner_given, select_out, taps_out, bias_out,
        normed, shifted, lows, total, sems,
    ) = rest
    index = pl.program_id(0)
    block = parts - 1 - index
    rows, inside = inner_ref.shape
    slab = normed.shape[1] // parts
    me = me_ref[0]
    odd = source_ref[parts]

    def fetched(k):
        at = pl.ds(pl.multiple_of((me ^ k) * rows, 16), rows)
        return pltpu.make_async_copy(normed_refs[k], normed.at[at], sems.at[k])

    @pl.when(index == 0)
    def fetch():
        for k in range(parts):
            fetched(k).start()
        shifted[rows:] = jnp.zeros((8, inside), jnp.float32)
        select_out[...] = jnp.zeros_like(select_out)
        taps_out[...] = jnp.zeros_like(taps_out)
        bias_out[...] = jnp.zeros_like(bias_out)

    selected = selected_ref[...]
    summed = summed_ref[...]
    curve = 1.0 / (1.0 + jnp.exp(-summed))
    grad_summed = (conv_ref[...] + dot_t(selected, select_ref[...])) * (curve * (1.0 + summed * (1.0 - curve)))
    select_out[...] += t_dot(selected, low_ref[...])
    bias_out[...] += jnp.sum(grad_summed, axis=0, keepdims=True)
    shifted[:rows] = grad_summed
    inner = inner_ref[...]
    grad_inner = jnp.zeros((rows, inside), jnp.float32)
    for k in range(KW):
        moved = shifted[KW - 1 - k : KW - 1 - k + rows]
        grad_inner = grad_inner + taps_ref[k : k + 1] * moved
        taps_out[k : k + 1] += jnp.sum(inner * moved, axis=0, keepdims=True)
    shifted[rows:] = shifted[0:8]
    live = live_slots(block * rows, length_ref, rows)
    low = jnp.where(live, grad_inner, 0.0).astype(jnp.bfloat16)
    inner_out[...] = low

    lows[pl.ds(pl.multiple_of(block * rows, rows), rows)] = low

    @pl.when(block == 0)
    def finish():
        for k in range(parts):
            fetched(k).wait()
        total[...] = t_dot(normed[...], lows[...])
        for h in range(parts // 2):
            at = pl.ds(pl.multiple_of((2 * h + odd) * slab, 8), slab)
            inner_held[h] = total[at]
            at = pl.ds(pl.multiple_of((2 * h + 1 - odd) * slab, 8), slab)
            inner_given[h] = total[at].astype(jnp.bfloat16)


def conv_back(me, source, length, normed_pieces, grad_selected, conv_grad, summed, inner, conv_low, taps, select_wide):
    parts = len(normed_pieces)
    rows, width = normed_pieces[0].shape
    slab = width // parts
    total, inside = inner.shape
    smem, anywhere = (pl.BlockSpec(memory_space=pltpu.SMEM), pl.BlockSpec(memory_space=pl.ANY))
    vmem = pl.BlockSpec(memory_space=pltpu.VMEM)
    row = pl.BlockSpec((rows, inside), lambda i: (parts - 1 - i, 0))
    f32, bf16 = (jnp.float32, jnp.bfloat16)
    return pl.pallas_call(
        functools.partial(conv_back_kernel, parts),
        grid=(parts,),
        in_specs=[smem] * 3
        + [anywhere] * parts
        + [pl.BlockSpec((rows, LANES), lambda i: (parts - 1 - i, 0))]
        + [row] * 4
        + [vmem] * 2,
        out_specs=[row] + [vmem] * 5,
        out_shape=[
            jax.ShapeDtypeStruct((total, inside), bf16),
            jax.ShapeDtypeStruct((2, slab, inside), f32),
            jax.ShapeDtypeStruct((2, slab, inside), bf16),
            jax.ShapeDtypeStruct((LANES, inside), f32),
            jax.ShapeDtypeStruct((8, inside), f32),
            jax.ShapeDtypeStruct((1, inside), f32),
        ],
        scratch_shapes=[
            pltpu.VMEM((total, width), bf16),
            pltpu.VMEM((rows + 8, inside), f32),
            pltpu.VMEM((total, inside), bf16),
            pltpu.VMEM((width, inside), f32),
            pltpu.SemaphoreType.DMA((parts,)),
        ],
        compiler_params=pltpu.CompilerParams(vmem_limit_bytes=48 * 2**20),
        cost_estimate=pl.CostEstimate(flops=4 * 10**9, bytes_accessed=2**20, transcendentals=0),
        name="conv_back",
    )(me, source, length, *normed_pieces, grad_selected, conv_grad, summed, inner, conv_low, taps, select_wide)


def project_back_kernel(parts, me_ref, source_ref, *rest):
    normed_refs, weight_refs, rest = (rest[:parts], rest[parts : 2 * parts], rest[2 * parts :])
    inner_ref, gate_ref, held_out, given_out, gain_out, normed, weight, projected, sems = rest
    block = pl.program_id(0)
    rows, inside = inner_ref.shape
    slab = weight_refs[0].shape[0]
    me = me_ref[0]

    @pl.when(block == 0)
    def fetch():
        copies = []
        for k in range(parts):
            at = pl.ds(pl.multiple_of(source_ref[k] * slab, 16), slab)
            copies.append(pltpu.make_async_copy(weight_refs[k], weight.at[at], sems.at[k]))
            at = pl.ds(pl.multiple_of((me ^ k) * rows, 16), rows)
            copies.append(pltpu.make_async_copy(normed_refs[k], normed.at[at], sems.at[parts + k]))
        for copy in copies:
            copy.start()
        gain_out[...] = jnp.zeros_like(gain_out)
        for copy in copies:
            copy.wait()

    projected[:, :inside] = inner_ref[...]
    projected[:, inside:] = gate_ref[...]
    normed_rows = normed[pl.ds(pl.multiple_of(block * rows, rows), rows)]
    grad_normed = dot_t(projected[...], weight[...])
    gain_out[...] += jnp.sum(grad_normed * normed_rows.astype(jnp.float32), axis=0, keepdims=True)

    @pl.when(block % 2 == me % 2)
    def keep():
        held_out[0] = grad_normed

    @pl.when(block % 2 != me % 2)
    def give():
        given_out[0] = grad_normed.astype(jnp.bfloat16)


def project_back(me, source, normed_pieces, weight_pieces, inner_grad, gate_grad):
    parts = len(normed_pieces)
    rows, width = normed_pieces[0].shape
    slab, both = weight_pieces[0].shape
    total, inside = inner_grad.shape
    smem, anywhere = (pl.BlockSpec(memory_space=pltpu.SMEM), pl.BlockSpec(memory_space=pl.ANY))
    vmem = pl.BlockSpec(memory_space=pltpu.VMEM)
    row = pl.BlockSpec((rows, inside), lambda i: (i, 0))
    part = pl.BlockSpec((1, rows, width), lambda i: (i // 2, 0, 0))
    f32, bf16 = (jnp.float32, jnp.bfloat16)
    return pl.pallas_call(
        functools.partial(project_back_kernel, parts),
        grid=(parts,),
        in_specs=[smem] * 2 + [anywhere] * (2 * parts) + [row] * 2,
        out_specs=[part, part, vmem],
        out_shape=[
            jax.ShapeDtypeStruct((2, rows, width), f32),
            jax.ShapeDtypeStruct((2, rows, width), bf16),
            jax.ShapeDtypeStruct((1, width), f32),
        ],
        scratch_shapes=[
            pltpu.VMEM((total, width), bf16),
            pltpu.VMEM((slab * parts, both), bf16),
            pltpu.VMEM((rows, both), bf16),
            pltpu.SemaphoreType.DMA((2 * parts,)),
        ],
        compiler_params=pltpu.CompilerParams(vmem_limit_bytes=40 * 2**20),
        cost_estimate=pl.CostEstimate(flops=4 * 10**9, bytes_accessed=2**20, transcendentals=0),
        name="project_back",
    )(me, source, *normed_pieces, *weight_pieces, inner_grad, gate_grad)


def norm_kernel(parts, me_ref, tokens_ref, *rest):
    small_refs, normed_out, gains_out = (rest[:parts], rest[parts], rest[parts + 1])
    slab = small_refs[0].shape[1]
    for m in range(parts):

        @pl.when(me_ref[0] == m)
        def lay():
            for p in range(parts):
                gains_out[:, p * slab : (p + 1) * slab] = small_refs[p ^ m][...]

    tokens = tokens_ref[...]
    scale = lax.rsqrt(jnp.mean(tokens * tokens, axis=-1, keepdims=True) + EPSILON)
    normed_out[...] = (tokens * scale * gains_out[2:3]).astype(jnp.bfloat16)


def norm_rows(me, tokens, small_pieces):
    parts = len(small_pieces)
    smem, vmem = (pl.BlockSpec(memory_space=pltpu.SMEM), pl.BlockSpec(memory_space=pltpu.VMEM))
    return pl.pallas_call(
        functools.partial(norm_kernel, parts),
        in_specs=[smem] + [vmem] * (1 + parts),
        out_specs=[vmem] * 2,
        out_shape=[
            jax.ShapeDtypeStruct(tokens.shape, jnp.bfloat16),
            jax.ShapeDtypeStruct((small_pieces[0].shape[0], tokens.shape[1]), jnp.float32),
        ],
        compiler_params=pltpu.CompilerParams(vmem_limit_bytes=16 * 2**20),
        name="norm_rows",
    )(me, tokens, *small_pieces)


def route_kernel(
    me_ref, length_ref, tokens_ref, near_ref, got_ref, gains_ref, order_ref, routes_ref,
    first_out, normed_out, sent_out, probs_out,
):
    rows, width = tokens_ref.shape
    first = tokens_ref[...] + near_ref[...] + got_ref[...].astype(jnp.float32)
    first_out[...] = first
    scale = lax.rsqrt(jnp.mean(first * first, axis=-1, keepdims=True) + EPSILON)
    normed = (first * scale * gains_ref[3:4]).astype(jnp.bfloat16)
    normed_out[...] = normed
    logits = dot_t(normed, router_rows(gains_ref))
    gap = logits[:, 0:1] - logits[:, 1:2]
    prob_zero = 1.0 / (1.0 + jnp.exp(-gap))
    prob_one = 1.0 / (1.0 + jnp.exp(gap))
    lane = lax.broadcasted_iota(jnp.int32, (rows, LANES), 1)
    probs_out[...] = jnp.where(lane == 0, prob_zero, jnp.where(lane == 1, prob_one, 0.0))
    gate = jnp.where(routes_ref[...] == 0, prob_zero, prob_one)
    gate = jnp.where(live_rows(me_ref, length_ref, rows), gate, 0.0)
    high, low = split_low(gate)
    high, low = (high.astype(jnp.float32), low.astype(jnp.float32))
    gates = jnp.where(lane == 0, high, jnp.where(lane == 1, low, 0.0)).astype(jnp.bfloat16)
    sent_out[:, :width] = dot(order_ref[...], normed).astype(jnp.bfloat16)
    sent_out[:, width:] = dot(order_ref[...], gates).astype(jnp.bfloat16)


def route(me, length, tokens, near, got, gains, order, routes):
    rows, width = tokens.shape
    smem, vmem = (pl.BlockSpec(memory_space=pltpu.SMEM), pl.BlockSpec(memory_space=pltpu.VMEM))
    return pl.pallas_call(
        route_kernel,
        in_specs=[smem, smem] + [vmem] * 6,
        out_specs=[vmem] * 4,
        out_shape=[
            jax.ShapeDtypeStruct((rows, width), jnp.float32),
            jax.ShapeDtypeStruct((rows, width), jnp.bfloat16),
            jax.ShapeDtypeStruct((rows, width + LANES), jnp.bfloat16),
            jax.ShapeDtypeStruct((rows, LANES), jnp.float32),
        ],
        compiler_params=pltpu.CompilerParams(vmem_limit_bytes=32 * 2**20),
        name="route",
    )(me, length, tokens, near, got, gains, order, routes)


def expert_kernel(parts, cap, steps, me_ref, source_ref, counts_ref, *rest):
    sent_refs, cot_refs, up_refs = (rest[:parts], rest[parts : 2 * parts], rest[2 * parts : 3 * parts])
    (
        down_ref, grad_held, grad_given, out_held, out_given, packed,
    ) = rest[3 * parts : 3 * parts + 6]
    rows, cots, up, down, rows_t, cots_t, scale, dots, grad_sum, out_sum, product, sems = rest[3 * parts + 6 :]
    step = pl.program_id(0)
    expert, tile = (step // steps, step % steps)
    span, width = cots.shape[1:]
    slab = up_refs[0].shape[1]
    offset = span - cap
    count = parts * cap
    me = me_ref[0]

    def weights(e):
        base = 2 * parts + e * (parts + 1)
        copies = [pltpu.make_async_copy(down_ref.at[e], down.at[e], sems.at[base])]
        for k in range(parts):
            at = pl.ds(pl.multiple_of(source_ref[k] * slab, 16), slab)
            copies.append(pltpu.make_async_copy(up_refs[k].at[e], up.at[e, at], sems.at[base + 1 + k]))
        return copies

    @pl.when(step == 0)
    def fetch():
        copies = []
        for k in range(parts):
            copies.append(pltpu.make_async_copy(sent_refs[k], rows.at[me ^ k], sems.at[k]))
            copies.append(pltpu.make_async_copy(cot_refs[k], cots.at[me ^ k], sems.at[parts + k]))
        for copy in copies:
            copy.start()
        for e in range(2):
            for copy in weights(e):
                copy.start()
        grad_sum[...] = jnp.zeros_like(grad_sum)
        out_sum[...] = jnp.zeros_like(out_sum)
        dots[...] = jnp.zeros_like(dots)
        for copy in copies:
            copy.wait()

    at = pl.ds(pl.multiple_of(expert * offset, 16), cap)
    mine = rows[:, at, :width].reshape(count, width)
    cot = cots[:, at].reshape(count, width)

    @pl.when(tile == 0)
    def turn():
        rows_t[...] = mine.T
        cots_t[...] = cot.T
        slot = lax.broadcasted_iota(jnp.int32, (cap, LANES), 0)
        for b in range(parts):
            gates = rows[b, at, width:].astype(jnp.float32)
            gate = gates[:, 0:1] + gates[:, 1:2]
            first = slot < counts_ref[b]
            later = slot + offset >= counts_ref[b]
            live = jnp.where(expert == 0, first.astype(jnp.float32), later.astype(jnp.float32))
            scale[b * cap : (b + 1) * cap] = live * gate
        for e in range(2):

            @pl.when(expert == e)
            def arrive():
                for copy in weights(e):
                    copy.wait()

    columns = pl.ds(pl.multiple_of(tile * FTILE, FTILE), FTILE)
    up_tile = up[expert, :, columns]
    down_tile = down[expert, columns, :]
    weight = scale[...][:, 0:1]
    pre = dot(mine, up_tile)
    grad_hidden = dot_t(cot, down_tile)
    square = pre * pre
    bend = jnp.tanh(0.7978845608028654 * pre * (1.0 + 0.044715 * square))
    rise = 0.5 * (1.0 + bend)
    slope = rise + 0.5 * pre * (1.0 - bend * bend) * (0.7978845608028654 * (1.0 + 0.134145 * square))
    hidden = (weight * (pre * rise)).astype(jnp.bfloat16)
    grad_pre = (weight * slope * grad_hidden).astype(jnp.bfloat16)
    part = jnp.sum(hidden.astype(jnp.float32) * grad_hidden, axis=1, keepdims=True)
    dots[:, at] += jnp.broadcast_to(part, (count, LANES)).reshape(parts, cap, LANES)
    out_sum[:, at] += dot(hidden, down_tile).reshape(parts, cap, width)
    grad_sum[:, at] += dot_t(grad_pre, up_tile).reshape(parts, cap, width)
    product[...] = dot(rows_t[...], grad_pre)
    fours = packed.shape[0]
    inside = packed.shape[-1] // LANES
    share = width // (fours * parts)
    pieces = []
    for q in range(FTILE // LANES):
        piece = tile * (FTILE // LANES) + q
        pieces.append((piece // inside, pl.ds(pl.multiple_of(piece % inside * LANES, LANES), LANES)))
    up_rows = pl.ds(pl.multiple_of(expert * slab, 16), slab)
    for q, (block, lanes) in enumerate(pieces):
        for r in range(parts):
            taken = product[r * slab : (r + 1) * slab, q * LANES : (q + 1) * LANES]
            packed[block, r, up_rows, lanes] = taken.astype(jnp.bfloat16)
    product[...] = dot(cots_t[...], hidden)
    base = 2 * slab
    for q, (block, lanes) in enumerate(pieces):
        down_rows = pl.ds(pl.multiple_of(base + (expert * fours + block) * share, 16), share)
        for g in range(fours * parts):
            taken = product[g * share : (g + 1) * share, q * LANES : (q + 1) * LANES]
            packed[g // parts, g % parts, down_rows, lanes] = taken.astype(jnp.bfloat16)

    @pl.when(step == pl.num_programs(0) - 1)
    def finish():
        for b in range(parts):

            @pl.when(me % 2 == b % 2)
            def hold():
                grad_held[b // 2, :, :width] = grad_sum[b]
                grad_held[b // 2, :, width:] = dots[b]
                out_held[b // 2] = out_sum[b]

            @pl.when(me % 2 != b % 2)
            def give():
                grad_given[b // 2, :, :width] = grad_sum[b].astype(jnp.bfloat16)
                grad_given[b // 2, :, width:] = dots[b].astype(jnp.bfloat16)
                out_given[b // 2] = out_sum[b].astype(jnp.bfloat16)


def experts(me, source, counts, sent_pieces, cot_pieces, up_pieces, down_weight, fours):
    parts = len(sent_pieces)
    span, width = cot_pieces[0].shape
    number, hid = down_weight.shape[:2]
    steps = hid // FTILE
    slab = up_pieces[0].shape[1]
    smem, anywhere = (pl.BlockSpec(memory_space=pltpu.SMEM), pl.BlockSpec(memory_space=pl.ANY))
    vmem = pl.BlockSpec(memory_space=pltpu.VMEM)
    f32, bf16 = (jnp.float32, jnp.bfloat16)
    packed = (fours, parts, 2 * number * slab, hid // fours)
    count = parts * CAP
    return pl.pallas_call(
        functools.partial(expert_kernel, parts, CAP, steps),
        grid=(number * steps,),
        in_specs=[smem] * 3 + [anywhere] * (3 * parts + 1),
        out_specs=[vmem] * 5,
        out_shape=[
            jax.ShapeDtypeStruct((2, span, width + LANES), f32),
            jax.ShapeDtypeStruct((2, span, width + LANES), bf16),
            jax.ShapeDtypeStruct((2, span, width), f32),
            jax.ShapeDtypeStruct((2, span, width), bf16),
            jax.ShapeDtypeStruct(packed, bf16),
        ],
        scratch_shapes=[
            pltpu.VMEM((parts, span, width + LANES), bf16),
            pltpu.VMEM((parts, span, width), bf16),
            pltpu.VMEM((number, slab * parts, hid), bf16),
            pltpu.VMEM((number, hid, width), bf16),
            pltpu.VMEM((width, count), bf16),
            pltpu.VMEM((width, count), bf16),
            pltpu.VMEM((count, LANES), f32),
            pltpu.VMEM((parts, span, LANES), f32),
            pltpu.VMEM((parts, span, width), f32),
            pltpu.VMEM((parts, span, width), f32),
            pltpu.VMEM((width, FTILE), f32),
            pltpu.SemaphoreType.DMA((2 * parts + 2 * (parts + 1),)),
        ],
        compiler_params=pltpu.CompilerParams(vmem_limit_bytes=60 * 2**20),
        cost_estimate=pl.CostEstimate(flops=4 * 10**9, bytes_accessed=2**20, transcendentals=0),
        name="experts",
    )(me, source, counts, *sent_pieces, *cot_pieces, *up_pieces, down_weight)


def return_kernel(
    me_ref, length_ref, near_ref, got_ref, order_ref, normed_ref, probs_ref, routes_ref, first_ref, cot_ref, gains_ref,
    grad_out, low_out, gain_out, router_out,
):
    rows, width = first_ref.shape
    grad = near_ref[...] + got_ref[...].astype(jnp.float32)
    high, low = split_low(grad)
    grad = dot(order_ref[...], high) + dot(order_ref[...], low)
    lane = lax.broadcasted_iota(jnp.int32, (rows, LANES), 1)
    chosen = (lane == routes_ref[...]).astype(jnp.float32)
    grad_logits = (grad[:, width : width + 1] * (chosen - probs_ref[...])).astype(jnp.bfloat16)
    grad_normed = grad[:, :width] + dot(grad_logits[:, :NS], router_rows(gains_ref))
    router_out[...] = t_dot(grad_logits, normed_ref[...])[0:8]
    first = first_ref[...]
    scale = lax.rsqrt(jnp.mean(first * first, axis=-1, keepdims=True) + EPSILON)
    unit = first * scale
    gain_out[...] = jnp.sum(grad_normed * unit, axis=0, keepdims=True)
    pulled = grad_normed * gains_ref[3:4]
    pulled = scale * (pulled - unit * jnp.mean(pulled * unit, axis=-1, keepdims=True))
    total = jnp.where(live_rows(me_ref, length_ref, rows), cot_ref[...], 0.0) + pulled
    grad_out[...] = total
    low_out[...] = total.astype(jnp.bfloat16)


def return_rows(me, length, *operands):
    rows, width = operands[6].shape
    smem, vmem = (pl.BlockSpec(memory_space=pltpu.SMEM), pl.BlockSpec(memory_space=pltpu.VMEM))
    return pl.pallas_call(
        return_kernel,
        in_specs=[smem, smem] + [vmem] * 9,
        out_specs=[vmem] * 4,
        out_shape=[
            jax.ShapeDtypeStruct((rows, width), jnp.float32),
            jax.ShapeDtypeStruct((rows, width), jnp.bfloat16),
            jax.ShapeDtypeStruct((1, width), jnp.float32),
            jax.ShapeDtypeStruct((8, width), jnp.float32),
        ],
        compiler_params=pltpu.CompilerParams(vmem_limit_bytes=32 * 2**20),
        name="return_rows",
    )(me, length, *operands)


def finish_kernel(
    me_ref, length_ref, near_ref, got_ref, out_near_ref, out_got_ref, order_ref, first_ref, grad_ref, tokens_ref, gains_ref,
    result_out, grad_out,
):
    rows = tokens_ref.shape[0]
    grad = near_ref[...] + got_ref[...].astype(jnp.float32)
    tokens = tokens_ref[...]
    scale = lax.rsqrt(jnp.mean(tokens * tokens, axis=-1, keepdims=True) + EPSILON)
    unit = tokens * scale
    pulled = grad * gains_ref[2:3]
    grad_out[...] = grad_ref[...] + scale * (pulled - unit * jnp.mean(pulled * unit, axis=-1, keepdims=True))
    high, low = split_low(out_near_ref[...] + out_got_ref[...].astype(jnp.float32))
    added = dot(order_ref[...], high) + dot(order_ref[...], low)
    result_out[...] = jnp.where(live_rows(me_ref, length_ref, rows), first_ref[...] + added, 0.0)


def finish_rows(me, length, *operands):
    shape = operands[5].shape
    smem, vmem = (pl.BlockSpec(memory_space=pltpu.SMEM), pl.BlockSpec(memory_space=pltpu.VMEM))
    return pl.pallas_call(
        finish_kernel,
        in_specs=[smem, smem] + [vmem] * 9,
        out_specs=[vmem] * 2,
        out_shape=[jax.ShapeDtypeStruct(shape, jnp.float32)] * 2,
        compiler_params=pltpu.CompilerParams(vmem_limit_bytes=32 * 2**20),
        name="finish_rows",
    )(me, length, *operands)


def body(
    tokens,
    routes,
    lengths,
    cotangent,
    in_weight,
    select_weight,
    step_weight,
    out_weight,
    router_weight,
    up_weight,
    down_weight,
    conv_weight,
    conv_bias,
    step_bias,
    decay_log,
    skip_gain,
    mixer_gain,
    expert_gain,
):
    f32, bf16 = (jnp.float32, jnp.bfloat16)
    span, width = tokens.shape
    groups, parts = (lax.axis_size("grp"), lax.axis_size("shard"))
    me, group = (lax.axis_index("shard"), lax.axis_index("grp"))
    total = span * parts
    inside = conv_bias.shape[0]
    tiles = inside // LANES
    slab = in_weight.shape[0]
    hidden_cols = up_weight.shape[2] // parts
    share = width // groups
    bits = [2**i for i in range(groups.bit_length() - 1)]
    down_bit = 2 if share % 8 == 0 else bits[-1]
    pair = 2 * share if share % 8 == 0 else width // 2
    odd, second = (group % 2, (group // down_bit) % 2)
    me_one = jnp.full((1,), me, jnp.int32)
    source = [me, me ^ 1, me ^ (2 + odd), me ^ (3 - odd), odd, second]
    source = jnp.stack(source).astype(jnp.int32)

    first = (routes[:, 0] == 0).astype(jnp.int32)
    count_first = jnp.sum(first)
    small = jnp.concatenate(
        [
            router_weight.astype(f32).T,
            mixer_gain.astype(f32)[None],
            expert_gain.astype(f32)[None],
            jnp.full((1, slab), count_first, jnp.int32).astype(f32),
            jnp.zeros((11, slab), f32),
        ],
        axis=0,
    )
    small = [small] + [swap(small, k) for k in range(1, parts)]
    in_pieces, up_pieces = cut_weights(source[:3], in_weight, up_weight, parts, inside)
    in_pieces = share_pieces(in_pieces)
    normed, gains = norm_rows(me_one, tokens, small)
    normed_pieces = gather_pieces(normed)
    counts = gains[4].reshape(parts, slab)[:, 0].astype(jnp.int32)

    goal = jnp.where(first > 0, jnp.cumsum(first), count_first + jnp.cumsum(1 - first)) - 1
    slots = jnp.arange(span, dtype=jnp.int32)
    order = (slots[:, None] == goal[None, :]).astype(bf16)
    order_t = (goal[:, None] == slots[None, :]).astype(bf16)
    live = (me * span + slots < lengths[0])[:, None]
    cots = matmul(order, jnp.where(live, cotangent, 0.0).astype(bf16)).astype(bf16)
    cot_pieces = gather_pieces(cots)

    taps = conv_weight.astype(f32)
    spare = LANES - select_weight.shape[1]
    select_wide = jnp.pad(select_weight, ((0, 0), (0, spare)))
    inner, zgate, summed, conv_out, conv_low, selected = project(
        me_one,
        source,
        lengths,
        normed_pieces,
        in_pieces,
        taps,
        conv_bias.astype(f32)[None, :],
        select_wide,
    )
    selected = tie(selected + swap(selected, 1), cot_pieces[2])
    selected = selected + swap(selected, 2)
    up_pieces = share_pieces([up_pieces[0], up_pieces[1], tie(up_pieces[2], selected)])
    step_wide = jnp.pad(step_weight, ((0, LANES - R), (0, 0)))
    step_row = step_bias.astype(f32)[None, :]
    decay = -jnp.exp(decay_log.astype(f32))
    rate = pack(decay * LOG2E, tiles)
    skip = skip_gain.astype(f32)[None, :]
    states, end, mixed, gated, held, given = mixer(
        me_one, lengths, selected, conv_out, zgate, step_wide, step_row, skip, rate, out_weight, span, tiles
    )
    near, given = scatter_near(held, tie(given, up_pieces[2]))
    first_sum, normed_two, sent, probs = route(
        me_one, lengths, tokens, near, swap(given, 2), gains, order, routes
    )
    fours, eights = (groups // 4, groups // 8)
    fine = hidden_cols // fours % LANES == 0 and share % 16 == 0
    grad_held, grad_given, out_held, out_given, packed = experts(
        me_one, source, counts, gather_pieces(sent), cot_pieces, up_pieces, down_weight, fours if fine else 1
    )
    up_cols = hidden_cols // fours
    if not fine:
        up_rows = packed[0, :, : E * slab].reshape(parts, E * slab, fours, up_cols).transpose(2, 0, 1, 3)
        down_rows = packed[0, :, E * slab :].reshape(parts, E, fours, share, fours, up_cols)
        down_rows = down_rows.transpose(2, 0, 1, 4, 3, 5).reshape(fours, parts, E * fours * share, up_cols)
        down_rows = down_rows.swapaxes(0, 1).reshape(fours, parts, E * fours * share, up_cols)
        packed = jnp.concatenate([up_rows, down_rows], axis=2)
    packed = packed.reshape(groups, 2 * E * slab, up_cols)
    packed = lax.psum_scatter(packed, "grp", scatter_dimension=0, tiled=True)
    up_sum, down_sum = (packed[:, : E * slab], packed[:, E * slab :])
    near, given = scatter_near(grad_held, grad_given)
    grad_first, grad_first_low, expert_gain_grad, router_grad = return_rows(
        me_one,
        lengths,
        near,
        swap(given, 2),
        order_t,
        normed_two,
        probs,
        routes,
        first_sum,
        cotangent,
        gains,
    )
    grad_pieces = gather_pieces(grad_first_low)
    top = bits[-1]
    out_bits = [bit for bit in bits[:0:-1] if bit != down_bit]
    blocks = (groups // 4, 2, share, inside)
    grad_mixed, grad_zgate, gate_held, gate_given, out_grad_held, out_grad_given = gate_back(
        me_one, source, normed_pieces, grad_pieces, zgate, mixed, gated, out_weight, pair
    )
    gate_got, out_grad_got = (swap_groups(gate_given, 1), swap_groups(out_grad_given, down_bit))
    conv_part, grad_selected, step_grad, step_bias_grad, skip_grad, rate_grad = mixer_back(
        lengths, selected, conv_out, grad_mixed, states, end, step_wide, step_row, skip, rate, tiles
    )
    chip_selected = grad_selected + swap(grad_selected, 1)
    gate_held, gate_given = halve((gate_held, gate_got), 0, 2, chip_selected)
    gate_got = swap_groups(gate_given, 2)
    out_parts = (out_grad_held.reshape(blocks), out_grad_got.reshape(blocks))
    out_grad_held, out_grad_given = halve(out_parts, 1, 1, chip_selected)
    out_grad_got = swap_groups(out_grad_given, 1)

    def up_home(g, s):
        return (s * fours + g // 4) * parts + g % 4

    def in_home(g, s):
        half, k = (g // (groups // 2), (g // 4) % eights)
        return (half * (groups // 2) + s * eights + k) * parts + g % 4

    both_axes = ("grp", "shard")
    places = [(g, s) for g in range(groups) for s in range(parts)]
    up_sum = lax.ppermute(tie(up_sum, chip_selected), both_axes, [(g * parts + s, up_home(g, s)) for g, s in places])
    grad_selected = (chip_selected + swap(chip_selected, 2)).astype(bf16)
    inner_grad, inner_held, inner_given, select_grad, conv_grad, conv_bias_grad = conv_back(
        me_one,
        source,
        lengths,
        normed_pieces,
        grad_selected,
        conv_part,
        summed,
        inner,
        conv_low,
        taps,
        select_wide,
    )
    inner_got = swap_groups(inner_given, 1)
    held, given, mixer_part = project_back(
        me_one, source, normed_pieces, in_pieces, inner_grad, grad_zgate
    )
    inner_held, inner_given = halve((inner_held, inner_got), 0, 2, given)
    inner_got = swap_groups(inner_given, 2)
    gate_sum = join(gate_held, gate_got, inner_held)
    for bit in out_bits:
        out_grad_held, out_grad_given = halve((out_grad_held, out_grad_got), 0, bit, inner_held)
        out_grad_got = swap_groups(out_grad_given, bit)
    shared = jnp.concatenate([router_grad[0:E], expert_gain_grad, mixer_part / gains[2:3]], axis=0)
    shared = shared + swap(shared, 1)
    shared = tie(shared + swap(shared, 2), inner_held)
    shared = lax.dynamic_slice_in_dim(shared, me * slab, slab, 1)
    decay_grad = decay * unpack(rate_grad, tiles)
    picked = select_weight.shape[1]
    few = [
        select_grad[:picked],
        conv_grad[:KW],
        conv_bias_grad,
        step_grad[:R],
        decay_grad,
        step_bias_grad,
        skip_grad,
        shared.reshape(2, inside),
    ]
    starts = [0]
    for part in few:
        starts.append(starts[-1] + part.shape[0])
    few = jnp.concatenate(few, axis=0).astype(bf16)
    few_got = swap_groups(few, 1)
    near, given = scatter_near(held, given, inner_held)
    got = swap(given, 2)
    out_near, out_given = scatter_near(out_held, out_given, inner_held)
    out_got = swap(out_given, 2)
    few = join(few, few_got, given, out_given).astype(bf16)
    few_got = swap_groups(few, 2)

    inner_sum = join(inner_held, inner_got, few)
    for bit in bits[-2:1:-1]:
        inner_held, inner_given = halve(inner_sum, 2, bit)
        inner_sum = join(inner_held, swap_groups(inner_given, bit))
        gate_held, gate_given = halve(gate_sum, 2, bit)
        gate_sum = join(gate_held, swap_groups(gate_given, bit))
    upper = group >= top
    own = jnp.where(upper, gate_sum, inner_sum).reshape(slab, inside // eights).astype(bf16)
    other = jnp.where(upper, inner_sum, gate_sum).reshape(slab, inside // eights).astype(bf16)
    own = lax.ppermute(own, both_axes, [(g * parts + s, in_home(g, s)) for g, s in places])
    other = lax.ppermute(other, both_axes, [(g * parts + s, in_home(g ^ top, s)) for g, s in places])
    few = join(few, few_got, inner_sum).astype(bf16)
    few_got = swap_groups(few, bits[2])
    out_sum = join(out_grad_held, out_grad_got, inner_sum).reshape(share, inside)
    result, tokens_grad = finish_rows(
        tie(me_one, few),
        lengths,
        near,
        got,
        out_near,
        out_got,
        order_t,
        first_sum,
        grad_first,
        tokens,
        gains,
    )
    in_sum = join(own, other, result)
    few = total_rest(join(few, few_got, result, up_sum), bits[3:])
    few = [few[a:b] for a, b in zip(starts[:-1], starts[1:])]
    select_grad, conv_grad, conv_bias_grad, step_grad, decay_grad, step_bias_grad, skip_grad, shared = few
    shared = shared.reshape(4, slab)
    up_sum = up_sum.astype(f32).reshape(E, slab, up_cols)
    down_sum = down_sum.astype(f32).reshape(E, fours, share, up_cols).transpose(0, 2, 1, 3)
    down_sum = down_sum.reshape(E, share, hidden_cols)
    return (
        result,
        tokens_grad,
        in_sum,
        out_sum.T,
        up_sum,
        down_sum.transpose(0, 2, 1),
        select_grad.T,
        step_grad,
        shared[0:E].T,
        conv_grad,
        conv_bias_grad[0],
        step_bias_grad[0],
        decay_grad,
        skip_grad[0],
        shared[3],
        shared[2],
    )


def solution(mesh):
    return jax.shard_map(
        body,
        mesh=mesh,
        in_specs=(
            P(("grp", "shard"), None),
            P(("grp", "shard"), None),
            P("grp"),
            P(("grp", "shard"), None),
            P("shard", None),
            P("shard", None),
            P(None, "shard"),
            P("shard", None),
            P("shard", None),
            P(None, "shard", None),
            P(None, "shard", None),
            P(None, "shard"),
            P("shard"),
            P("shard"),
            P(None, "shard"),
            P("shard"),
            P("shard"),
            P("shard"),
        ),
        out_specs=(
            P(("grp", "shard"), None),
            P(("grp", "shard"), None),
            P("shard", "grp"),
            P("shard", "grp"),
            P(None, "shard", "grp"),
            P(None, "shard", "grp"),
            P("shard", None),
            P(None, "shard"),
            P("shard", None),
            P(None, "shard"),
            P("shard"),
            P("shard"),
            P(None, "shard"),
            P("shard"),
            P("shard"),
            P("shard"),
        ),
        check_vma=False,
    )
```
